32 devices in a mesh: dp: 16 (over z, y, x), rep: 2 (over core).
Axes of the slice: x: 2, y: 2, z: 4, core: 2. Of those that a mesh axis runs over, the one named last changes fastest.
Arguments:
- noise_owner: int32 [16, 1024, 8], P('dp', 'rep'), may hold values from 0 to 31, all different within a row; in each aligned block of 512 rows (0 to 511, 512 to 1023, ..., all dimensions but the last counted through in order) at most 256 rows name the same one
- noise_offset: int32 [16, 1024, 8], P('dp', 'rep'), may hold values from 0 to 1571
- option_scores: float32 [16, 1024, 8], P('dp', 'rep'), may hold values from -4 to 4
- seq_lengths: int32 [16], replicated, may hold values from 1 to 1024, as said below
- time_index: int32 [16], replicated, may hold values from 0 to 999
- loss_pick: int32 [16, 2, 64], replicated, may hold values from 0 to 511
- loss_target: int32 [16, 2, 64], replicated, may hold values from 0 to 50303
- vocab_table: float32 [50304, 768], P(('dp', 'rep'))
- table_mom: float32 [50304, 768], P(('dp', 'rep')), may hold values from -4.7683716e-06 to 4.7683716e-06
- table_sq: float32 [50304, 768], P(('dp', 'rep')), may hold values from 8.596075e-15 to 3.43843e-14
- attn_proj: float32 [768, 2304], P(('dp', 'rep')), may hold values from -0.21875 to 0.21875
- proj_mom: float32 [768, 2304], P(('dp', 'rep')), may hold values from -2.3841858e-06 to 2.3841858e-06
- proj_sq: float32 [768, 2304], P(('dp', 'rep')), may hold values from 2.1490187e-15 to 8.596075e-15
- out_proj: float32 [768, 768], P(('dp', 'rep')), may hold values from -0.875 to 0.875
- outp_mom: float32 [768, 768], P(('dp', 'rep')), may hold values from -2.3841858e-06 to 2.3841858e-06
- outp_sq: float32 [768, 768], P(('dp', 'rep')), may hold values from 2.1490187e-15 to 8.596075e-15
- up_proj: float32 [768, 3072], P(('dp', 'rep')), may hold values from -0.21875 to 0.21875
- up_mom: float32 [768, 3072], P(('dp', 'rep')), may hold values from -2.3841858e-06 to 2.3841858e-06
- up_sq: float32 [768, 3072], P(('dp', 'rep')), may hold values from 2.1490187e-15 to 8.596075e-15
- down_proj: float32 [3072, 768], P(('dp', 'rep')), may hold values from -0.109375 to 0.109375
- down_mom: float32 [3072, 768], P(('dp', 'rep')), may hold values from -2.3841858e-06 to 2.3841858e-06
- down_sq: float32 [3072, 768], P(('dp', 'rep')), may hold values from 2.1490187e-15 to 8.596075e-15
- time_proj: float32 [256, 128], P(('dp', 'rep')), may hold values from -0.5 to 0.5
- time_mom: float32 [256, 128], P(('dp', 'rep')), may hold values from -2.3841858e-06 to 2.3841858e-06
- time_sq: float32 [256, 128], P(('dp', 'rep')), may hold values from 2.1490187e-15 to 8.596075e-15
- mod_proj: float32 [128, 4608], P(('dp', 'rep')), may hold values from -0.5 to 0.5
- mod_mom: float32 [128, 4608], P(('dp', 'rep')), may hold values from -2.3841858e-06 to 2.3841858e-06
- mod_sq: float32 [128, 4608], P(('dp', 'rep')), may hold values from 2.1490187e-15 to 8.596075e-15
- final_proj: float32 [128, 1536], P(('dp', 'rep')), may hold values from -0.5 to 0.5
- final_mom: float32 [128, 1536], P(('dp', 'rep')), may hold values from -2.3841858e-06 to 2.3841858e-06
- final_sq: float32 [128, 1536], P(('dp', 'rep')), may hold values from 2.1490187e-15 to 8.596075e-15
- norm_gains: float32 [3, 768], P(None, ('dp', 'rep')), may hold values from 0.5 to 1.5
- gains_mom: float32 [3, 768], P(None, ('dp', 'rep')), may hold values from -1.9073486e-05 to 1.9073486e-05
- gains_sq: float32 [3, 768], P(None, ('dp', 'rep')), may hold values from 1.375372e-13 to 5.501488e-13
Outputs:
- loss_sum: float32 [], replicated
- coefficient_aggregate: float32 [], replicated
- grad_norm: float32 [], replicated
- fresh_table: float32 [50304, 768], P(('dp', 'rep'))
- table_mom_new: float32 [50304, 768], P(('dp', 'rep'))
- table_sq_new: float32 [50304, 768], P(('dp', 'rep'))
- attn_new: float32 [768, 2304], P(('dp', 'rep'))
- attn_mom_new: float32 [768, 2304], P(('dp', 'rep'))
- attn_sq_new: float32 [768, 2304], P(('dp', 'rep'))
- outp_new: float32 [768, 768], P(('dp', 'rep'))
- outp_mom_new: float32 [768, 768], P(('dp', 'rep'))
- outp_sq_new: float32 [768, 768], P(('dp', 'rep'))
- expand_matrix_revised: float32 [768, 3072], P(('dp', 'rep'))
- up_mom_new: float32 [768, 3072], P(('dp', 'rep'))
- up_second_moment: float32 [768, 3072], P(('dp', 'rep'))
- down_new: float32 [3072, 768], P(('dp', 'rep'))
- down_mom_new: float32 [3072, 768], P(('dp', 'rep'))
- down_sq_new: float32 [3072, 768], P(('dp', 'rep'))
- time_new: float32 [256, 128], P(('dp', 'rep'))
- time_mom_new: float32 [256, 128], P(('dp', 'rep'))
- time_sq_new: float32 [256, 128], P(('dp', 'rep'))
- mod_new: float32 [128, 4608], P(('dp', 'rep'))
- mod_mom_new: float32 [128, 4608], P(('dp', 'rep'))
- mod_sq_new: float32 [128, 4608], P(('dp', 'rep'))
- final_new: float32 [128, 1536], P(('dp', 'rep'))
- final_mom_new: float32 [128, 1536], P(('dp', 'rep'))
- final_sq_new: float32 [128, 1536], P(('dp', 'rep'))
- gains_new: float32 [3, 768], P(None, ('dp', 'rep'))
- gains_mom_new: float32 [3, 768], P(None, ('dp', 'rep'))
- gains_sq_new: float32 [3, 768], P(None, ('dp', 'rep'))
The draws below stay inside these ranges and needn't reach their ends.
Inputs may be any that keep to these rules, and one draw needn't show every extreme that they name: `noise_owner`: each position names 8 different blocks. In each aligned block of 512 positions (one half of one sequence), at most 256 positions name one value, a bound that some block reaches. `seq_lengths`: one sequence in every draw has length 1024.
All inputs are finite; a program needn't handle non-finite values.
Results may differ from the reference program's by a relative error of at most 0.006.
The reference program's roundings to bfloat16 on the way count: a program that leaves them out, or rounds other values in their place, can miss the bound.
Values may be sent and summed in bfloat16 or wider, within the bound.
No kernel may reach another device: no remote copies, remote signals or barrier semaphores. Data moves between devices by JAX's collectives and lax.ppermute only.
A program may use at most 320 MiB of HBM per device.

```python
import math
import jax
import jax.numpy as jnp
import numpy as np
from jax import lax

D = 768
H = 12
HD = 64
FF = 3072
V = 50304
COND = 128
FREQ = 256
L = 1024
CAND = 8
TSTEPS = 1000
STEP = 5
SEQS = 16
PICKS = 64
MOST = 256
VS = 1572
NPARAM = 46532864
N_REP = 2
DEVICES = 32


def draw_seq_lengths(key, part):
    key = jax.random.fold_in(key, 11)
    jitter_key, lengthy_key = jax.random.split(key)
    index = jnp.arange(SEQS, dtype=jnp.int32)
    base = L // 3 + (L - L // 3) * index // SEQS
    jitter = jax.random.randint(jitter_key, (SEQS,), -(L // 8), L // 8 + 1)
    length = jnp.clip(base + jitter, 1, L)
    longest = jax.random.randint(lengthy_key, (), 0, SEQS)
    return jnp.where(index == longest, L, length).astype(jnp.int32)


def draw_vocab_table(key, part):
    key = jax.random.fold_in(key, 5)
    rows = jnp.arange(V, dtype=jnp.float32)[:, None] / V
    base = jax.random.normal(key, (V, D), jnp.float32)
    scale = 1.0 + 2.0 * rows
    return base * scale / math.sqrt(D)


def place_ends(array, stream_key, least, high):
    index_at = [jax.random.randint(jax.random.fold_in(stream_key, axis), (), 0, length) for axis, length in enumerate(array.shape)]
    main_axis = array.shape.index(max(array.shape))
    next_to = index_at[:main_axis] + [(index_at[main_axis] + 1) % array.shape[main_axis]] + index_at[main_axis + 1:]
    return array.at[tuple(index_at)].set(least).at[tuple(next_to)].set(high)


def block_levels(rng, shape, shards, least, top_value):
    def one(axis_at, blocks):
        steps = jax.random.uniform(jax.random.fold_in(jax.random.fold_in(rng, 6), axis_at), (blocks,), jnp.float32, least / len(shards), top_value / len(shards))
        return jnp.repeat(jnp.exp(steps), shape[axis_at] // blocks).reshape((-1,) + (1,) * (len(shape) - axis_at - 1))

    loudness = one(*shards[0])
    for cut in shards[1:]:
        loudness = loudness * one(*cut)
    return loudness


def assign_block(own_key, own, number, rows, number_of, top, bound, lean):
    order = jax.random.permutation(own_key, number_of)
    heavy_load, usual = load_shares(number_of, rows * top, bound, lean, True), load_shares(number_of, rows * top, bound, lean, False)
    places = jnp.arange(number_of)

    def named(tallies, rotation):
        used = int((tallies > 0).sum())
        fixed = max(1, used // 4)
        moved = fixed + (places - fixed + rotation * (used - fixed)) % max(1, number_of - fixed)
        return jnp.zeros((number_of,), jnp.int32).at[order[jnp.where(places < fixed, places, moved)]].set(jnp.asarray(tallies, jnp.int32))

    tallies = jnp.where(number % 4 == 0, named(heavy_load, number // 4), named(usual, number - number // 4 - 1))
    mixed = jax.random.permutation(jax.random.fold_in(own, 3), number_of)
    giver, sink = mixed[0:number_of // 2 * 2:2], mixed[1:number_of // 2 * 2:2]
    slack = jnp.minimum(tallies[giver] - 1, bound - tallies[sink]) // 2
    slack = jnp.where((giver == order[0]) | (sink == order[0]) | (tallies[sink] == 0), 0, jnp.maximum(slack, 0))
    moved = jax.random.randint(jax.random.fold_in(own, 4), (number_of // 2,), 0, 1 << 20) % (slack + 1)
    tallies = tallies.at[giver].add(-moved).at[sink].add(moved)
    labels = jnp.searchsorted(jnp.cumsum(tallies), jnp.arange(rows * top), side="right").astype(jnp.int32)
    grid = labels.reshape(top, rows).T
    grid = grid[jax.random.permutation(jax.random.fold_in(own, 1), rows)]
    rotation = jax.random.randint(jax.random.fold_in(own, 2), (rows, 1), 0, top)
    return jnp.take_along_axis(grid, (jnp.arange(top)[None, :] + rotation) % top, axis=1)


def load_shares(count, total, most, lean, full):
    loads = [(1 << 20) // math.isqrt(grade ** lean) + 1 for grade in range(1, count + 1)]
    largest = most if full else min(most, max(-(-total // count), total * loads[0] // sum(loads)))
    least = 1 if total - largest >= count - 1 else 0
    holding, surplus = [largest] + [least] * (count - 1), total - largest - least * (count - 1)
    while surplus > 0:
        movable = [i for i in range(1, count) if holding[i] < largest] or [i for i in range(1, count) if holding[i] < most]
        pool, left = sum([loads[i] for i in movable]), surplus
        for i in movable:
            extra = min(most - holding[i], max(1, left * loads[i] // pool), surplus)
            holding[i] = holding[i] + extra
            surplus = surplus - extra
    return np.array(holding)


def normal_values(own_key, extent, deviation, bound, shards=(), held_as=jnp.bfloat16):
    entries = deviation * jax.random.normal(own_key, extent, jnp.float32)
    if shards:
        entries = entries * block_levels(own_key, extent, shards, -0.22, 0.18)
    return jnp.clip(entries, -bound, bound).astype(held_as)


def setup_inputs(seed: int = 0) -> dict:
    keys = jax.random.split(jax.random.key(seed), 35)
    noise_owner_keys = jax.random.split(jax.random.fold_in(keys[0], 1), SEQS * L // (L // N_REP))
    noise_owner_turns = jax.random.permutation(jax.random.fold_in(keys[0], 3), SEQS * L // (L // N_REP))
    noise_owner = jax.vmap(lambda own, number: assign_block(jax.random.fold_in(keys[0], 2), own, number, L // N_REP, DEVICES, CAND, MOST, 1))(noise_owner_keys, noise_owner_turns).reshape((SEQS, L, CAND))
    noise_offset = place_ends(jax.random.randint(keys[1], (SEQS, L, CAND), 0, VS), jax.random.fold_in(keys[1], 1), 0, VS - 1).astype(jnp.int32)
    option_scores = normal_values(keys[2], (SEQS, L, CAND), 1.0, 4.0, ((0, 16), (1, 2)), jnp.float32)
    seq_lengths = draw_seq_lengths(jax.random.fold_in(keys[34], 71), 0)
    time_index = place_ends(jax.random.randint(keys[4], (SEQS,), 0, TSTEPS), jax.random.fold_in(keys[4], 1), 0, TSTEPS - 1).astype(jnp.int32)
    loss_pick = place_ends(jax.random.randint(keys[5], (SEQS, N_REP, PICKS), 0, L // N_REP), jax.random.fold_in(keys[5], 1), 0, (L // N_REP) - 1).astype(jnp.int32)
    loss_target = place_ends(jax.random.randint(keys[6], (SEQS, N_REP, PICKS), 0, V), jax.random.fold_in(keys[6], 1), 0, V - 1).astype(jnp.int32)
    vocab_table = draw_vocab_table(jax.random.fold_in(keys[34], 71), 0)
    table_mom = normal_values(keys[8], (V, D), (0.0022 / NPARAM ** 0.5), 4.76837158203125e-06, ((0, 32),), jnp.float32)
    table_sq = jnp.clip(jnp.exp(math.log(3.4384299606778773e-14) - 1.3862944 * jax.random.uniform(keys[9], (V, D), jnp.float32) ** block_levels(keys[9], (V, D), ((0, 32),), -0.2, 0.2)), 8.596074901694693e-15, 3.4384299606778773e-14)
    attn_proj = normal_values(keys[10], (D, 3 * D), D ** -0.5, 0.21875, ((0, 32),), jnp.float32)
    proj_mom = normal_values(keys[11], (D, 3 * D), (0.0011 / NPARAM ** 0.5), 2.384185791015625e-06, ((0, 32),), jnp.float32)
    proj_sq = jnp.clip(jnp.exp(math.log(8.596074901694693e-15) - 1.3862944 * jax.random.uniform(keys[12], (D, 3 * D), jnp.float32) ** block_levels(keys[12], (D, 3 * D), ((0, 32),), -0.2, 0.2)), 2.1490187254236733e-15, 8.596074901694693e-15)
    out_proj = normal_values(keys[13], (D, D), (D // 16) ** -0.5, 0.875, ((0, 32),), jnp.float32)
    outp_mom = normal_values(keys[14], (D, D), (0.0011 / NPARAM ** 0.5), 2.384185791015625e-06, ((0, 32),), jnp.float32)
    outp_sq = jnp.clip(jnp.exp(math.log(8.596074901694693e-15) - 1.3862944 * jax.random.uniform(keys[15], (D, D), jnp.float32) ** block_levels(keys[15], (D, D), ((0, 32),), -0.2, 0.2)), 2.1490187254236733e-15, 8.596074901694693e-15)
    up_proj = normal_values(keys[16], (D, FF), D ** -0.5, 0.21875, ((0, 32),), jnp.float32)
    up_mom = normal_values(keys[17], (D, FF), (0.0011 / NPARAM ** 0.5), 2.384185791015625e-06, ((0, 32),), jnp.float32)
    up_sq = jnp.clip(jnp.exp(math.log(8.596074901694693e-15) - 1.3862944 * jax.random.uniform(keys[18], (D, FF), jnp.float32) ** block_levels(keys[18], (D, FF), ((0, 32),), -0.2, 0.2)), 2.1490187254236733e-15, 8.596074901694693e-15)
    down_proj = normal_values(keys[19], (FF, D), FF ** -0.5, 0.109375, ((0, 32),), jnp.float32)
    down_mom = normal_values(keys[20], (FF, D), (0.0011 / NPARAM ** 0.5), 2.384185791015625e-06, ((0, 32),), jnp.float32)
    down_sq = jnp.clip(jnp.exp(math.log(8.596074901694693e-15) - 1.3862944 * jax.random.uniform(keys[21], (FF, D), jnp.float32) ** block_levels(keys[21], (FF, D), ((0, 32),), -0.2, 0.2)), 2.1490187254236733e-15, 8.596074901694693e-15)
    time_proj = normal_values(keys[22], (FREQ, COND), (FREQ // 2) ** -0.5, 0.5, ((0, 32),), jnp.float32)
    time_mom = normal_values(keys[23], (FREQ, COND), (0.0011 / NPARAM ** 0.5), 2.384185791015625e-06, ((0, 32),), jnp.float32)
    time_sq = jnp.clip(jnp.exp(math.log(8.596074901694693e-15) - 1.3862944 * jax.random.uniform(keys[24], (FREQ, COND), jnp.float32) ** block_levels(keys[24], (FREQ, COND), ((0, 32),), -0.2, 0.2)), 2.1490187254236733e-15, 8.596074901694693e-15)
    mod_proj = normal_values(keys[25], (COND, 6 * D), COND ** -0.5, 0.5, ((0, 32),), jnp.float32)
    mod_mom = normal_values(keys[26], (COND, 6 * D), (0.0011 / NPARAM ** 0.5), 2.384185791015625e-06, ((0, 32),), jnp.float32)
    mod_sq = jnp.clip(jnp.exp(math.log(8.596074901694693e-15) - 1.3862944 * jax.random.uniform(keys[27], (COND, 6 * D), jnp.float32) ** block_levels(keys[27], (COND, 6 * D), ((0, 32),), -0.2, 0.2)), 2.1490187254236733e-15, 8.596074901694693e-15)
    final_proj = normal_values(keys[28], (COND, 2 * D), COND ** -0.5, 0.5, ((0, 32),), jnp.float32)
    final_mom = normal_values(keys[29], (COND, 2 * D), (0.0011 / NPARAM ** 0.5), 2.384185791015625e-06, ((0, 32),), jnp.float32)
    final_sq = jnp.clip(jnp.exp(math.log(8.596074901694693e-15) - 1.3862944 * jax.random.uniform(keys[30], (COND, 2 * D), jnp.float32) ** block_levels(keys[30], (COND, 2 * D), ((0, 32),), -0.2, 0.2)), 2.1490187254236733e-15, 8.596074901694693e-15)
    norm_gains = jnp.clip(1.0 + 0.1 * jax.random.normal(keys[31], (3, D), jnp.float32), 0.5, 1.5)
    gains_mom = normal_values(keys[32], (3, D), (0.0089 / NPARAM ** 0.5), 1.9073486328125e-05, ((1, 32),), jnp.float32)
    gains_sq = jnp.clip(jnp.exp(math.log(5.501487937084604e-13) - 1.3862944 * jax.random.uniform(keys[33], (3, D), jnp.float32) ** block_levels(keys[33], (3, D), ((1, 32),), -0.2, 0.2)), 1.375371984271151e-13, 5.501487937084604e-13)
    return dict(noise_owner=noise_owner, noise_offset=noise_offset, option_scores=option_scores, seq_lengths=seq_lengths, time_index=time_index, loss_pick=loss_pick, loss_target=loss_target, vocab_table=vocab_table, table_mom=table_mom, table_sq=table_sq, attn_proj=attn_proj, proj_mom=proj_mom, proj_sq=proj_sq, out_proj=out_proj, outp_mom=outp_mom, outp_sq=outp_sq, up_proj=up_proj, up_mom=up_mom, up_sq=up_sq, down_proj=down_proj, down_mom=down_mom, down_sq=down_sq, time_proj=time_proj, time_mom=time_mom, time_sq=time_sq, mod_proj=mod_proj, mod_mom=mod_mom, mod_sq=mod_sq, final_proj=final_proj, final_mom=final_mom, final_sq=final_sq, norm_gains=norm_gains, gains_mom=gains_mom, gains_sq=gains_sq)


@jax.custom_vjp
def low(v):
    return lax.optimization_barrier(v.astype(jnp.bfloat16)).astype(jnp.float32)

@jax.custom_vjp
def low_back(v):
    return v

def low_keep(v):
    return (low(v), None)

def low_pass(kept, grad):
    return (grad,)

def back_keep(v):
    return (v, None)

def back_low(kept, grad):
    return (low(grad),)
low.defvjp(low_keep, low_pass)
low_back.defvjp(back_keep, back_low)
annealed_softness = 0.5

def matmul(a, b):
    return jnp.dot(a, b, precision=lax.Precision.HIGHEST, preferred_element_type=jnp.float32)

def layer_norm(x):
    center = x - lax.optimization_barrier(jnp.mean(x, -1, keepdims=True))
    return center * lax.rsqrt(lax.optimization_barrier(jnp.mean(center * center, -1, keepdims=True)) + 1e-06)

def rope_tables(pos, head):
    half = head // 2
    freqs = jnp.exp(-math.log(10000.0) * jnp.arange(half, dtype=jnp.float32) / half)
    angle = pos.astype(jnp.float32)[:, None] * freqs[None, :]
    return (jnp.cos(angle), jnp.sin(angle))

def rotate(t, cosv, sinv):
    half = t.shape[-1] // 2
    first, second = (t[..., :half], t[..., half:])
    c = cosv[:, None, :]
    s = sinv[:, None, :]
    return jnp.concatenate([first * c - second * s, first * s + second * c], -1)

def time_features(steps, width):
    tau = (steps.astype(jnp.float32) + 1.0) / TSTEPS
    half = width // 2
    freqs = jnp.exp(-math.log(10000.0) * jnp.arange(half, dtype=jnp.float32) / half)
    angle = 1000.0 * tau[:, None] * freqs[None, :]
    return jnp.concatenate([jnp.cos(angle), jnp.sin(angle)], -1)

def sequence_fn(xin, mod, fmod, length, wq, wo, wu, wd, gains):
    sh1, sc1, g1, sh2, sc2, g2 = jnp.split(mod, 6)
    fsh, fsc = jnp.split(fmod, 2)
    pos = jnp.arange(L, dtype=jnp.int32)
    cosv, sinv = rope_tables(pos, HD)
    h1 = low(layer_norm(xin) * gains[0] * (1.0 + sc1) + sh1)
    qkv = low_back(matmul(h1, wq))
    query = low(rotate(qkv[:, :D].reshape(L, H, HD), cosv, sinv))
    keyed = low(rotate(qkv[:, D:2 * D].reshape(L, H, HD), cosv, sinv))
    valued = low(qkv[:, 2 * D:].reshape(L, H, HD))
    scores = low_back(jnp.einsum('qhd,khd->hqk', query, keyed, precision=lax.Precision.HIGHEST) * HD ** (-0.5))
    scores = jnp.where((pos < length)[None, None, :], scores, -1e+30)
    probs = low(jax.nn.softmax(scores, axis=-1))
    mixed = jnp.einsum('hqk,khd->qhd', probs, valued, precision=lax.Precision.HIGHEST).reshape(L, D)
    mixed = low(low_back(mixed))
    x1 = xin + g1 * low_back(matmul(mixed, wo))
    h2 = low(layer_norm(x1) * gains[1] * (1.0 + sc2) + sh2)
    upper = low_back(matmul(h2, wu))
    act = low(jax.nn.gelu(upper, approximate=True))
    x2 = x1 + g2 * low_back(matmul(act, wd))
    return layer_norm(x2) * gains[2] * (1.0 + fsc) + fsh

def adamw(weight, first, second, grad, rate):
    first = 0.9 * first + 0.1 * grad
    second = 0.999 * second + 0.001 * grad * grad
    step = first / (1.0 - 0.9 ** STEP) / (jnp.sqrt(second / (1.0 - 0.999 ** STEP)) + 1e-08)
    return (weight - rate * (step + 0.01 * weight), first, second)

def reference(noise_owner, noise_offset, option_scores, seq_lengths, time_index, loss_pick, loss_target, vocab_table, table_mom, table_sq, attn_proj, proj_mom, proj_sq, out_proj, outp_mom, outp_sq, up_proj, up_mom, up_sq, down_proj, down_mom, down_sq, time_proj, time_mom, time_sq, mod_proj, mod_mom, mod_sq, final_proj, final_mom, final_sq, norm_gains, gains_mom, gains_sq):
    ids = (noise_owner * VS + noise_offset).astype(jnp.int32)
    mixing_coefficient = jax.nn.softmax(option_scores / annealed_softness, axis=-1)
    half = L // N_REP
    positions = loss_pick + (jnp.arange(N_REP, dtype=jnp.int32) * half)[None, :, None]
    seq_of = jnp.broadcast_to(jnp.arange(SEQS, dtype=jnp.int32)[:, None, None], loss_pick.shape)
    tau = (time_index.astype(jnp.float32) + 1.0) / TSTEPS
    weight = jnp.where(positions < seq_lengths[seq_of], 1.0 / (0.1 + tau[seq_of]), 0.0).reshape(-1)
    coefficient_aggregate = jnp.sum(weight)
    targets = loss_target.reshape(-1)
    feats = time_features(time_index, FREQ)
    total_rows = weight.shape[0]
    block = math.gcd(total_rows, 512)

    def loss_of(params):
        table, wq, wo, wu, wd, wc, wm, wf, gains = [low(p) for p in params]
        cond = jax.nn.silu(matmul(feats, wc))
        mods = matmul(cond, wm)
        fmods = matmul(cond, wf)

        def one_seq(carry, items):
            ids_s, mix_s, mod, fmod, length = items
            xin = jnp.einsum('lk,lkd->ld', mix_s, table[ids_s], precision=lax.Precision.HIGHEST)
            return (carry, sequence_fn(xin, mod, fmod, length, wq, wo, wu, wd, gains))
        _, hidden = lax.scan(jax.checkpoint(one_seq), 0.0, (ids, mixing_coefficient, mods, fmods, seq_lengths))
        rows = low(hidden[seq_of, positions].reshape(-1, D))

        def head_block(items):
            rows_blk, goal_segment, weight_blk = items
            logits = low_back(matmul(rows_blk, table.T))
            lse = jax.scipy.special.logsumexp(logits, axis=-1)
            picked = jnp.take_along_axis(logits, goal_segment[:, None], 1)[:, 0]
            return jnp.sum(weight_blk * (lse - picked))
        parts = lax.map(jax.checkpoint(head_block), (rows.reshape(-1, block, D), targets.reshape(-1, block), weight.reshape(-1, block)))
        total = jnp.sum(parts)
        return (total / coefficient_aggregate, total)
    params = (vocab_table, attn_proj, out_proj, up_proj, down_proj, time_proj, mod_proj, final_proj, norm_gains)
    value, back, loss_sum = jax.vjp(loss_of, params, has_aux=True)
    grads = back(jnp.ones_like(value))[0]
    squares = jnp.float32(0.0)
    for g in grads:
        squares = squares + jnp.sum(g * g)
    grad_norm = jnp.sqrt(squares)
    clip = jnp.minimum(1.0, 0.01 / (grad_norm + 1e-06))
    moms = (table_mom, proj_mom, outp_mom, up_mom, down_mom, time_mom, mod_mom, final_mom, gains_mom)
    sqs = (table_sq, proj_sq, outp_sq, up_sq, down_sq, time_sq, mod_sq, final_sq, gains_sq)
    rates = (0.02, 0.02, 0.02, 0.02, 0.02, 0.02, 0.02, 0.02, 0.1)
    result = [loss_sum, coefficient_aggregate, grad_norm]
    for weight_now, first, second, grad, rate in zip(params, moms, sqs, grads, rates):
        result.extend(adamw(weight_now, first, second, clip * grad, rate))
    return tuple(result)
```

```python
import functools
import math

import jax
import jax.numpy as jnp
from jax import lax
from jax.experimental import pallas as pl
from jax.experimental.pallas import tpu as pltpu
from jax.sharding import PartitionSpec as P

HD = 64
TSTEPS = 1000
STEP = 5
PLANE = 4
LANES = 128
BOTH = ("dp", "rep")

HIGH = lax.Precision.HIGHEST
annealed_softness = 0.5
bf16 = jnp.bfloat16
f32 = jnp.float32


def dense(a, b):
    return jnp.dot(a, b, preferred_element_type=f32)


def dense_nt(a, b):
    return lax.dot_general(a, b, (((1,), (1,)), ((), ())), preferred_element_type=f32)


def dense_tn(a, b):
    return lax.dot_general(a, b, (((0,), (0,)), ((), ())), preferred_element_type=f32)


def exact(a, b):
    return jnp.dot(a, b, precision=HIGH, preferred_element_type=f32)


def exact_nt(a, b):
    return lax.dot_general(
        a, b, (((1,), (1,)), ((), ())), precision=HIGH, preferred_element_type=f32
    )


def exact_tn(a, b):
    return lax.dot_general(
        a, b, (((0,), (0,)), ((), ())), precision=HIGH, preferred_element_type=f32
    )


def normalize(x):
    center = x - jnp.mean(x, -1, keepdims=True)
    rstd = lax.rsqrt(jnp.mean(center * center, -1, keepdims=True) + 1e-06)
    return (center * rstd, rstd)


def modulate_back(grad_h, normed, rstd, gain, scale):
    dshift = jnp.sum(grad_h, 0)
    weighted = grad_h * normed
    column = jnp.sum(weighted, 0)
    dscale = column * gain
    dgain = column * (1.0 + scale[0])
    grad_n = grad_h * gain * (1.0 + scale)
    grad_x = rstd * (
        grad_n
        - jnp.mean(grad_n, -1, keepdims=True)
        - normed * jnp.mean(grad_n * normed, -1, keepdims=True)
    )
    return (grad_x, dshift, dscale, dgain)


def rope_tables(pos, head):
    half = head // 2
    freqs = jnp.exp(-math.log(10000.0) * jnp.arange(half, dtype=f32) / half)
    angle = pos.astype(f32)[:, None] * freqs[None, :]
    return (jnp.cos(angle), jnp.sin(angle))


def rotate(t, cosv, sinv):
    half = t.shape[-1] // 2
    first, second = (t[..., :half], t[..., half:])
    c = cosv[:, None, :]
    s = sinv[:, None, :]
    return jnp.concatenate([first * c - second * s, first * s + second * c], -1)


def time_features(steps, width):
    tau = (steps.astype(f32) + 1.0) / TSTEPS
    half = width // 2
    freqs = jnp.exp(-math.log(10000.0) * jnp.arange(half, dtype=f32) / half)
    angle = 1000.0 * tau[:, None] * freqs[None, :]
    return jnp.concatenate([jnp.cos(angle), jnp.sin(angle)], -1)


def masked_scores(query, keyed, valid):
    scores = jnp.einsum("qhd,khd->hqk", query, keyed, preferred_element_type=f32) * query.shape[
        -1
    ] ** (-0.5)
    return jnp.where(valid[None, None, :], scores, -1e30)


def attend(query, keyed, valued, valid):
    scores = masked_scores(query, keyed, valid)
    top = jnp.max(scores, -1, keepdims=True)
    expo = jnp.exp(scores - top)
    total = jnp.sum(expo, -1, keepdims=True)
    probs = (expo / total).astype(bf16)
    mixed = jnp.einsum("hqk,khd->qhd", probs, valued, preferred_element_type=f32)
    return (mixed, top[..., 0] + jnp.log(total[..., 0]))


def attend_back(query, keyed, valued, valid, lse, grad_mix):
    scale = query.shape[-1] ** (-0.5)
    probs = jnp.exp(masked_scores(query, keyed, valid) - lse[..., None])
    grad_p = jnp.einsum("qhd,khd->hqk", grad_mix, valued, preferred_element_type=f32)
    delta = jnp.sum(grad_p * probs, -1, keepdims=True)
    grad_s = (probs * (grad_p - delta)).astype(bf16)
    grad_q = jnp.einsum("hqk,khd->qhd", grad_s, keyed, preferred_element_type=f32) * scale
    grad_k = jnp.einsum("hqk,qhd->khd", grad_s, query, preferred_element_type=f32) * scale
    grad_v = jnp.einsum("hqk,qhd->khd", probs.astype(bf16), grad_mix, preferred_element_type=f32)
    return (grad_q, grad_k, grad_v)


def adamw(weight, first, second, grad, rate):
    first = 0.9 * first + 0.1 * grad
    second = 0.999 * second + 0.001 * grad * grad
    step = first / (1.0 - 0.9**STEP) / (jnp.sqrt(second / (1.0 - 0.999**STEP)) + 1e-08)
    return (weight - rate * (step + 0.01 * weight), first, second)


def hop(x, dl=0, dq=0, dr=0):
    reps = lax.axis_size("rep")
    lines = lax.axis_size("dp") // PLANE
    pairs = []
    for l in range(lines):
        for q in range(PLANE):
            for r in range(reps):
                to = (((l + dl) % lines) * PLANE + (q ^ dq)) * reps + (r ^ dr)
                pairs.append(((l * PLANE + q) * reps + r, to))
    return lax.ppermute(x, BOTH, pairs)


def step_line(x, way, reach):
    lines = lax.axis_size("dp") // PLANE
    pairs = []
    for l in range(lines):
        if 0 <= l + way * reach < lines:
            for q in range(PLANE):
                pairs.append((l * PLANE + q, (l + way) * PLANE + q))
    return lax.ppermute(x, "dp", pairs)


def mix_kernel(idx_ref, mix_ref, *refs, groups, cands, counts):
    pieces = refs[: len(counts)]
    out_ref, tab, stage, sem = refs[len(counts) :]

    @pl.when(pl.program_id(0) == 0)
    def _():
        def copy(j):
            return pltpu.make_async_copy(
                pieces[j], stage.at[j % 2, pl.ds(0, counts[j])], sem.at[j % 2]
            )

        copy(0).start()
        base = 0
        for j, rows in enumerate(counts):
            if j + 1 < len(counts):
                copy(j + 1).start()
            copy(j).wait()

            @pl.loop(0, rows // 16)
            def _(t, j=j, base=base):
                part = stage[j % 2, pl.ds(pl.multiple_of(t * 16, 16), 16), :].astype(f32)
                for g in range(groups):
                    tab[pl.ds((base + t * 16) * groups + g, 16, stride=groups), :] = part[
                        :, g * LANES : (g + 1) * LANES
                    ]

            base += rows

    unroll = 4

    @pl.loop(0, idx_ref.shape[-1] // cands // unroll)
    def _(block):
        for u in range(unroll):
            p = block * unroll + u
            total = None
            for c in range(cands):
                row = tab[pl.ds(idx_ref[0, 0, p * cands + c], 8), :]
                term = row * mix_ref[0, 0, p * cands + c]
                total = term if total is None else total + term
            out_ref[0, pl.ds(p * groups, 8), :] = total


def mix_rows(idx, mix, pieces, cands):
    groups = pieces[0].shape[1] // LANES
    lines, _, entries = idx.shape
    counts = tuple(piece.shape[0] for piece in pieces)
    rows = entries // cands * groups + 8
    return pl.pallas_call(
        functools.partial(mix_kernel, groups=groups, cands=cands, counts=counts),
        grid=(lines,),
        in_specs=[pl.BlockSpec((1, 1, entries), lambda i: (i, 0, 0), memory_space=pltpu.SMEM)] * 2
        + [pl.BlockSpec(memory_space=pl.ANY)] * len(pieces),
        out_specs=pl.BlockSpec((1, rows, LANES), lambda i: (i, 0, 0)),
        out_shape=jax.ShapeDtypeStruct((lines, rows, LANES), f32),
        scratch_shapes=[
            pltpu.VMEM((sum(counts) * groups + 8, LANES), f32),
            pltpu.VMEM((2, max(counts), groups * LANES), bf16),
            pltpu.SemaphoreType.DMA((2,)),
        ],
        compiler_params=pltpu.CompilerParams(vmem_limit_bytes=60 * 2**20),
        cost_estimate=pl.CostEstimate(
            flops=lines * entries * 2048, bytes_accessed=40 * 2**20, transcendentals=0
        ),
    )(idx, mix, *pieces)


def spread_kernel(cnt_ref, row_ref, pos_ref, mix_ref, *refs, groups, arrays):
    sources = refs[:arrays]
    head_ref, out_ref, sq_ref, total, rows32, stage, sem = refs[arrays:]
    per, length, _ = sources[0].shape
    n = arrays * per

    def copy(k):
        return pltpu.make_async_copy(sources[k // per].at[k % per], stage.at[k % 2], sem.at[k % 2])

    copy(0).start()

    @pl.loop(0, total.shape[0] // 64)
    def _(t):
        total[pl.ds(pl.multiple_of(t * 64, 64), 64), :] = jnp.zeros((64, LANES), f32)

    unroll = 4
    for k in range(n):
        if k + 1 < n:
            copy(k + 1).start()
        copy(k).wait()

        @pl.loop(0, length // 64)
        def _(t, k=k):
            at = pl.multiple_of(t * 64, 64)
            rows32[pl.ds(at, 64), :] = stage[k % 2, pl.ds(at, 64), :].astype(f32)

        @pl.loop(0, (cnt_ref[k] + unroll - 1) // unroll)
        def _(block, k=k):
            for u in range(unroll):
                e = block * unroll + u
                at = pl.ds(pl.multiple_of(row_ref[k, e] * 8, 8), 8)
                term = mix_ref[k, e] * rows32[pl.ds(pos_ref[k, e], 8), :]
                total[at, :] = total[at, :] + term

    vocab = out_ref.shape[0]

    def finish(at, size, start):
        squares = jnp.zeros((size, LANES), f32)
        for g in range(groups):
            columns = slice(g * LANES, (g + 1) * LANES)
            value = head_ref[pl.ds(at, size), columns] + total[pl.ds(start + g, size, stride=8), :]
            out_ref[pl.ds(at, size), columns] = value
            squares = squares + value * value
        return squares

    squares = lax.fori_loop(
        0,
        vocab // 8,
        lambda t, so_far: so_far + finish(pl.multiple_of(t * 8, 8), 8, t * 64),
        jnp.zeros((8, LANES), f32),
    )
    sq_ref[...] = squares
    if vocab % 8:
        at = vocab // 8 * 8
        sq_ref[0 : vocab % 8, :] += finish(at, vocab % 8, at * 8)


def spread_rows(cnt, row, pos, mix, sources, head, vocab):
    width = head.shape[1]
    groups = width // LANES
    length = sources[0].shape[1]
    smem = pl.BlockSpec(memory_space=pltpu.SMEM)
    vmem = pl.BlockSpec(memory_space=pltpu.VMEM)
    return pl.pallas_call(
        functools.partial(spread_kernel, groups=groups, arrays=len(sources)),
        in_specs=[smem] * 4 + [pl.BlockSpec(memory_space=pl.ANY)] * len(sources) + [vmem],
        out_specs=[vmem, vmem],
        out_shape=[
            jax.ShapeDtypeStruct((vocab, width), f32),
            jax.ShapeDtypeStruct((8, LANES), f32),
        ],
        scratch_shapes=[
            pltpu.VMEM((-(-vocab * 8 // 64) * 64, LANES), f32),
            pltpu.VMEM((length + 8, LANES), f32),
            pltpu.VMEM((2, length, LANES), bf16),
            pltpu.SemaphoreType.DMA((2,)),
        ],
        compiler_params=pltpu.CompilerParams(vmem_limit_bytes=60 * 2**20),
        cost_estimate=pl.CostEstimate(
            flops=2**28, bytes_accessed=40 * 2**20, transcendentals=0
        ),
    )(cnt, row, pos, mix, *sources, head)


def local(
    noise_owner,
    noise_offset,
    option_scores,
    seq_lengths,
    time_index,
    loss_pick,
    loss_target,
    vocab_table,
    table_mom,
    table_sq,
    attn_proj,
    proj_mom,
    proj_sq,
    out_proj,
    outp_mom,
    outp_sq,
    up_proj,
    up_mom,
    up_sq,
    down_proj,
    down_mom,
    down_sq,
    time_proj,
    time_mom,
    time_sq,
    mod_proj,
    mod_mom,
    mod_sq,
    final_proj,
    final_mom,
    final_sq,
    norm_gains,
    gains_mom,
    gains_sq,
):
    devices = lax.axis_size(BOTH)
    reps = lax.axis_size("rep")
    n_dp = lax.axis_size("dp")
    lines = n_dp // PLANE
    dp_idx = lax.axis_index("dp")
    rep_idx = lax.axis_index("rep")
    me = dp_idx * reps + rep_idx
    line = dp_idx // PLANE
    chip = dp_idx % PLANE
    _, half, cands = noise_offset.shape
    vocab, width = vocab_table.shape
    heads = width // HD
    groups = width // LANES
    swaps = [(dq, dr) for dq in range(PLANE) for dr in range(reps)]

    padded = -(-vocab // 16) * 16
    table_low = jnp.pad(vocab_table.astype(bf16), ((0, padded - vocab), (0, 0)))
    cut = padded // 32 * 16
    upper_rows, lower_rows = table_low[:cut], table_low[cut:]
    first, second = {0: upper_rows}, {0: lower_rows}
    first[1] = hop(upper_rows, dq=1)
    second[2] = hop(lower_rows, dq=2)
    first[2] = hop(upper_rows, dq=2)
    second[1] = hop(lower_rows, dq=1)
    first[3] = hop(first[1], dq=2)
    second[3] = hop(second[2], dq=1)
    pieces = []
    for dq in range(PLANE):
        pieces += [first[dq], second[dq]]
        pieces += [hop(first[dq], dr=1), hop(second[dq], dr=1)]

    owner = noise_owner.reshape(-1)
    offset = noise_offset.reshape(-1)
    mixing = jax.nn.softmax(option_scores.reshape(half, cands) / annealed_softness, axis=-1)
    packed_owner = owner.reshape(-1, LANES) * padded + offset.reshape(-1, LANES)
    packed_mix = mixing.reshape(-1, LANES)
    line_owner = jnp.stack(
        [packed_owner] + [hop(packed_owner, dl=-d) for d in range(1, lines)]
    )
    line_mix = jnp.stack([packed_mix] + [hop(packed_mix, dl=-d) for d in range(1, lines)])
    row_owner = line_owner // padded
    slot_of = (((row_owner // reps) % PLANE) ^ chip) * reps + ((row_owner % reps) ^ rep_idx)
    here = (row_owner // (reps * PLANE)) == line
    row_at = jnp.where(here, slot_of * padded + line_owner % padded, 0) * groups
    mix_here = jnp.where(here, line_mix, 0.0)
    partial = mix_rows(
        row_at.reshape(lines, 1, half * cands),
        mix_here.reshape(lines, 1, half * cands),
        pieces,
        cands,
    )[:, : half * groups]
    ahead = back = None
    for d in range(lines - 1, 0, -1):
        to_right = partial[d] if ahead is None else partial[d] + ahead
        to_left = partial[lines - d] if back is None else partial[lines - d] + back
        ahead = step_line(to_right, 1, d)
        back = step_line(to_left, -1, d)
    x0 = (partial[0] + ahead + back).reshape(half, width)

    def gather(value, axis=0):
        return lax.all_gather(value.astype(bf16), BOTH, axis=axis, tiled=True)

    small = (time_proj, mod_proj, final_proj, norm_gains)
    flat = jnp.concatenate([value.reshape(-1) for value in small])
    flat = jnp.pad(flat, (0, -flat.size % (8 * LANES))).reshape(1, -1, LANES)
    small_all = gather(flat).reshape(devices, -1)
    qkv_w = gather(attn_proj)
    out_w = gather(out_proj)
    up_w = gather(up_proj)
    down_w = gather(down_proj)
    unpacked = []
    at = 0
    for value in small:
        part = small_all[:, at : at + value.size].astype(f32).reshape((devices,) + value.shape)
        unpacked.append(part)
        at += value.size
    time_f = unpacked[0].reshape(-1, time_proj.shape[1])
    mod_f = unpacked[1].reshape(-1, mod_proj.shape[1])
    final_f = unpacked[2].reshape(-1, final_proj.shape[1])
    gain_f = unpacked[3].transpose(1, 0, 2).reshape(norm_gains.shape[0], width)

    length = lax.dynamic_slice_in_dim(seq_lengths, dp_idx, 1)
    feats = time_features(time_index, time_f.shape[0])
    cond, silu_back = jax.vjp(jax.nn.silu, exact(feats, time_f))
    my_cond = lax.dynamic_slice_in_dim(cond, dp_idx, 1)
    mods = exact(my_cond, mod_f)
    fmods = exact(my_cond, final_f)
    sh1, sc1, g1, sh2, sc2, g2 = jnp.split(mods, 6, -1)
    fsh, fsc = jnp.split(fmods, 2, -1)

    n1, r1 = normalize(x0)
    h1b = (n1 * gain_f[0] * (1.0 + sc1) + sh1).astype(bf16)
    shaped = dense(h1b, qkv_w).reshape(half, 3, heads, HD)
    pos = rep_idx * half + jnp.arange(half, dtype=jnp.int32)
    far_pos = (1 - rep_idx) * half + jnp.arange(half, dtype=jnp.int32)
    cosv, sinv = rope_tables(pos, HD)
    query = rotate(shaped[:, 0], cosv, sinv).astype(bf16)
    keyed = rotate(shaped[:, 1], cosv, sinv).astype(bf16)
    valued = shaped[:, 2].astype(bf16)
    key_all = jnp.concatenate([keyed, hop(keyed, dr=1)], 0)
    value_all = jnp.concatenate([valued, hop(valued, dr=1)], 0)
    valid = jnp.concatenate([pos, far_pos]) < length
    mixed, lse_att = attend(query, key_all, value_all, valid)
    mixed_b = mixed.astype(bf16).reshape(-1, width)
    attn = dense(mixed_b, out_w)
    x1 = x0 + g1 * attn
    n2, r2 = normalize(x1)
    h2b = (n2 * gain_f[1] * (1.0 + sc2) + sh2).astype(bf16)
    upper = dense(h2b, up_w)
    act, gelu_back = jax.vjp(lambda u: jax.nn.gelu(u, approximate=True), upper)
    act_b = act.astype(bf16)
    mlp = dense(act_b, down_w)
    x2 = x1 + g2 * mlp
    nf, rf = normalize(x2)
    final = nf * gain_f[2] * (1.0 + fsc) + fsh

    picks = loss_pick.shape[-1]
    tau = (time_index.astype(f32) + 1.0) / TSTEPS
    starts = (jnp.arange(reps, dtype=jnp.int32) * half)[None, :, None]
    weight_all = jnp.where(
        loss_pick + starts < seq_lengths[:, None, None], (1.0 / (0.1 + tau))[:, None, None], 0.0
    )
    coefficient_aggregate = jnp.sum(weight_all)

    def of_line(values):
        mine = lax.dynamic_slice(
            values.reshape(lines, PLANE, reps, picks), (0, chip, rep_idx, 0), (lines, 1, 1, picks)
        )
        return from_me(mine.reshape(lines, picks))

    def from_me(values):
        return lax.dynamic_slice_in_dim(jnp.concatenate([values, values], 0), line, lines)

    def from_start(values):
        return lax.dynamic_slice_in_dim(
            jnp.concatenate([values, values], 0), (lines - line) % lines, lines
        )

    targets = of_line(loss_target).reshape(-1)
    weight = of_line(weight_all).reshape(-1)
    my_pick = lax.dynamic_slice(loss_pick, (dp_idx, rep_idx, 0), (1, 1, picks)).reshape(picks)
    spread = (jnp.arange(half, dtype=jnp.int32)[:, None] == my_pick[None, :]).astype(f32)
    rows_b = jnp.take(final, my_pick, axis=0).astype(bf16)
    every = jnp.concatenate([rows_b] + [hop(rows_b, dl=-d) for d in range(1, lines)], 0)
    plane_table = jnp.concatenate(pieces, 0)
    logits = dense_nt(every, plane_table)
    column = jnp.arange(plane_table.shape[0], dtype=jnp.int32)
    exists = (column % padded) < vocab
    t_owner = targets // vocab
    t_slot = (((t_owner // reps) % PLANE) ^ chip) * reps + ((t_owner % reps) ^ rep_idx)
    t_column = jnp.where(
        t_owner // (reps * PLANE) == line, t_slot * padded + targets % vocab, -1
    )
    hit = column[None, :] == t_column[:, None]
    logits = jnp.where(exists[None, :], logits, -1e30)
    top = jnp.max(logits, -1)
    sums = jnp.sum(jnp.exp(logits - top[:, None]), -1)
    tgt = jnp.sum(jnp.where(hit, logits, 0.0), -1)
    stats = from_start(
        jnp.stack([value.reshape(lines, picks) for value in (top, sums, tgt)], 1)
    )
    stats_all = jnp.stack([stats] + [hop(stats, dl=-d) for d in range(1, lines)])
    tops = stats_all[:, :, 0]
    best = jnp.max(tops, 0)
    sum_all = jnp.sum(stats_all[:, :, 1] * jnp.exp(tops - best), 0)
    lse_line = best + jnp.log(sum_all)
    tgt_line = jnp.sum(stats_all[:, :, 2], 0)
    loss_here = jnp.sum(from_start(weight.reshape(lines, picks)) * (lse_line - tgt_line))
    loss_here = jnp.where(line == 0, loss_here, 0.0)
    lse = from_me(lse_line).reshape(-1)
    probs = jnp.exp(logits - lse[:, None])
    dlogit = ((weight / coefficient_aggregate)[:, None] * (probs - hit.astype(f32))).astype(bf16)
    drows_part = dense(dlogit, plane_table).reshape(lines, picks, width)
    drows = drows_part[0]
    for d in range(1, lines):
        drows = drows + hop(drows_part[d], dl=d)
    dlogit_mine = []
    rows_mine = []
    for slot, (dq, dr) in enumerate(swaps):
        block = dlogit[:, slot * padded : (slot + 1) * padded]
        dlogit_mine.append(block if slot == 0 else hop(block, dq=dq, dr=dr))
        rows_mine.append(every if slot == 0 else hop(every, dq=dq, dr=dr))
    head_grad = dense_tn(jnp.concatenate(dlogit_mine, 0), jnp.concatenate(rows_mine, 0))

    def scatter(value):
        return lax.psum_scatter(value, BOTH, scatter_dimension=0, tiled=True)

    grad_final = exact(spread, drows)
    dx2, dfsh, dfsc, dgain_f = modulate_back(grad_final, nf, rf, gain_f[2], fsc)
    dg2 = jnp.sum(dx2 * mlp, 0)
    dmlp = (dx2 * g2).astype(bf16)
    d_down = scatter(dense_tn(act_b, dmlp))
    dupper = gelu_back(dense_nt(dmlp, down_w))[0].astype(bf16)
    d_up = scatter(dense_tn(h2b, dupper))
    dh2 = dense_nt(dupper, up_w)
    dn2x, dsh2, dsc2, dgain_2 = modulate_back(dh2, n2, r2, gain_f[1], sc2)
    dx1 = dx2 + dn2x
    dg1 = jnp.sum(dx1 * attn, 0)
    dattn = (dx1 * g1).astype(bf16)
    d_out = scatter(dense_tn(mixed_b, dattn))
    dmixed = dense_nt(dattn, out_w).astype(bf16).reshape(half, heads, HD)
    dquery, dkey_all, dvalue_all = attend_back(query, key_all, value_all, valid, lse_att, dmixed)
    dkey = dkey_all[:half] + hop(dkey_all[half:].astype(bf16), dr=1).astype(f32)
    dvalue = dvalue_all[:half] + hop(dvalue_all[half:].astype(bf16), dr=1).astype(f32)
    dqkv = jnp.stack([rotate(dquery, cosv, -sinv), rotate(dkey, cosv, -sinv), dvalue], 1)
    dqkv = dqkv.reshape(-1, 3 * width).astype(bf16)
    dh1 = dense_nt(dqkv, qkv_w)
    dn1x, dsh1, dsc1, dgain_1 = modulate_back(dh1, n1, r1, gain_f[0], sc1)
    dx0 = dx1 + dn1x
    d_qkv = scatter(dense_tn(h1b, dqkv))

    cap = max(2, 2 * half * cands // devices)
    member = (owner[:, None] == jnp.arange(devices, dtype=jnp.int32)[None, :]).astype(jnp.int32)
    slot = jnp.sum((jnp.cumsum(member, 0) - member) * member, 1)
    flat_slot = owner * cap + slot
    entry = offset * half + jnp.arange(half * cands, dtype=jnp.int32) // cands + 1
    asked = jnp.zeros((devices * cap,), jnp.int32).at[flat_slot].set(entry)
    asked_mix = jnp.zeros((devices * cap,), f32).at[flat_slot].set(mixing.reshape(-1))

    def exchange(value):
        return lax.all_to_all(
            value.reshape(devices, cap), BOTH, split_axis=0, concat_axis=0, tiled=True
        )

    asked, asked_mix = exchange(asked), exchange(asked_mix)
    dx0_b = dx0.astype(bf16).reshape(half * groups, LANES)
    on_line = [dx0_b] + [hop(dx0_b, dl=-d) for d in range(1, lines)]
    stacks = [
        jnp.stack(on_line[k * lines // 4 : (k + 1) * lines // 4]) for k in range(4)
    ]
    sources = []
    order = []
    for k, stack in enumerate(stacks):
        kind = {0: stack, 1: hop(stack, dq=1), 2: hop(stack, dq=2)}
        kind[3] = hop(kind[1], dq=2) if k % 2 == 0 else hop(kind[2], dq=1)
        for dq in range(PLANE):
            for dr in range(reps):
                sources.append(kind[dq] if dr == 0 else hop(kind[dq], dr=1))
                for d in range(k * lines // 4, (k + 1) * lines // 4):
                    order.append(
                        (((line + d) % lines) * PLANE + (chip ^ dq)) * reps + (rep_idx ^ dr)
                    )
    order = jnp.stack(order)
    asked = jnp.take(asked, order, axis=0)
    asked_mix = jnp.take(asked_mix, order, axis=0)
    count = jnp.sum((asked > 0).astype(jnp.int32), 1)
    asked = jnp.maximum(asked - 1, 0)
    table_grad, table_squares = spread_rows(
        count, asked // half, (asked % half) * groups, asked_mix, sources, head_grad, vocab
    )

    sums_here = jnp.concatenate(
        [dsh1, dsc1, dg1, dsh2, dsc2, dg2, dfsh, dfsc, dgain_1, dgain_2, dgain_f]
    )
    sums_all = lax.all_gather(sums_here.reshape(1, -1, LANES), BOTH, axis=0, tiled=True)
    sums_all = sums_all.reshape(n_dp, reps, -1).sum(1)
    dmods = sums_all[:, : 6 * width]
    dfmods = sums_all[:, 6 * width : 8 * width]

    def my_columns(value, count):
        return lax.dynamic_slice_in_dim(value, me * count, count, axis=1)

    d_mod = exact_tn(my_columns(cond, mod_proj.shape[0]), dmods)
    d_final = exact_tn(my_columns(cond, final_proj.shape[0]), dfmods)
    dcond = exact_nt(dmods, mod_f) + exact_nt(dfmods, final_f)
    d_time = exact_tn(my_columns(feats, time_proj.shape[0]), silu_back(dcond)[0])
    d_gains = my_columns(
        jnp.sum(sums_all[:, 8 * width :], 0).reshape(3, width), norm_gains.shape[1]
    )

    reduced = (d_qkv, d_out, d_up, d_down, d_time, d_mod, d_final, d_gains)
    local_sq = jnp.sum(table_squares)
    for g in reduced:
        local_sq = local_sq + jnp.sum(g * g)
    totals = lax.psum(jnp.stack([local_sq, loss_here]), BOTH)
    grad_norm = jnp.sqrt(totals[0])
    loss_sum = totals[1]
    clip = jnp.minimum(1.0, 0.01 / (grad_norm + 1e-06))
    masters = (attn_proj, out_proj, up_proj, down_proj, time_proj, mod_proj, final_proj, norm_gains)
    coefficients = (vocab_table,) + masters
    moms = (
        table_mom,
        proj_mom,
        outp_mom,
        up_mom,
        down_mom,
        time_mom,
        mod_mom,
        final_mom,
        gains_mom,
    )
    sqs = (table_sq, proj_sq, outp_sq, up_sq, down_sq, time_sq, mod_sq, final_sq, gains_sq)
    rates = (0.02, 0.02, 0.02, 0.02, 0.02, 0.02, 0.02, 0.02, 0.1)
    grads = (table_grad,) + reduced
    result = [loss_sum, coefficient_aggregate, grad_norm]
    for weight_now, first_m, second_m, grad, rate in zip(coefficients, moms, sqs, grads, rates):
        result.extend(adamw(weight_now, first_m, second_m, clip * grad, rate))
    return tuple(result)


def solution(mesh):
    shard = P(BOTH, None)
    columns = P(None, BOTH)
    return jax.shard_map(
        local,
        mesh=mesh,
        in_specs=(P("dp", "rep", None),) * 3 + (P(),) * 4 + (shard,) * 24 + (columns,) * 3,
        out_specs=(P(),) * 3 + (shard,) * 24 + (columns,) * 3,
        check_vma=False,
    )
```

```python
import functools
import math

import jax
import jax.numpy as jnp
from jax import lax
from jax.experimental import pallas as pl
from jax.experimental.pallas import tpu as pltpu
from jax.sharding import PartitionSpec as P

HD = 64
TSTEPS = 1000
STEP = 5
PLANE = 4
LANES = 128
BOTH = ("dp", "rep")

HIGH = lax.Precision.HIGHEST
annealed_softness = 0.5
bf16 = jnp.bfloat16
f32 = jnp.float32


def dense(a, b):
    return jnp.dot(a, b, preferred_element_type=f32)


def dense_nt(a, b):
    return lax.dot_general(a, b, (((1,), (1,)), ((), ())), preferred_element_type=f32)


def dense_tn(a, b):
    return lax.dot_general(a, b, (((0,), (0,)), ((), ())), preferred_element_type=f32)


def exact(a, b):
    return jnp.dot(a, b, precision=HIGH, preferred_element_type=f32)


def exact_nt(a, b):
    return lax.dot_general(
        a, b, (((1,), (1,)), ((), ())), precision=HIGH, preferred_element_type=f32
    )


def exact_tn(a, b):
    return lax.dot_general(
        a, b, (((0,), (0,)), ((), ())), precision=HIGH, preferred_element_type=f32
    )


def normalize(x):
    center = x - jnp.mean(x, -1, keepdims=True)
    rstd = lax.rsqrt(jnp.mean(center * center, -1, keepdims=True) + 1e-06)
    return (center * rstd, rstd)


def modulate_back(grad_h, normed, rstd, gain, scale):
    dshift = jnp.sum(grad_h, 0)
    weighted = grad_h * normed
    column = jnp.sum(weighted, 0)
    dscale = column * gain
    dgain = column * (1.0 + scale[0])
    grad_n = grad_h * gain * (1.0 + scale)
    grad_x = rstd * (
        grad_n
        - jnp.mean(grad_n, -1, keepdims=True)
        - normed * jnp.mean(grad_n * normed, -1, keepdims=True)
    )
    return (grad_x, dshift, dscale, dgain)


def rope_tables(pos, head):
    half = head // 2
    freqs = jnp.exp(-math.log(10000.0) * jnp.arange(half, dtype=f32) / half)
    angle = pos.astype(f32)[:, None] * freqs[None, :]
    return (jnp.cos(angle), jnp.sin(angle))


def time_features(steps, width):
    tau = (steps.astype(f32) + 1.0) / TSTEPS
    half = width // 2
    freqs = jnp.exp(-math.log(10000.0) * jnp.arange(half, dtype=f32) / half)
    angle = 1000.0 * tau[:, None] * freqs[None, :]
    return jnp.concatenate([jnp.cos(angle), jnp.sin(angle)], -1)


def turn(x, cosv, sinv):
    lane = lax.broadcasted_iota(jnp.int32, x.shape, 1)
    quarter = HD // 2
    swapped = jnp.where(
        lane % HD < quarter,
        pltpu.roll(x, LANES - quarter, axis=1),
        pltpu.roll(x, quarter, axis=1),
    )
    return x * cosv + swapped * sinv


def turn_kernel(q_ref, k_ref, v_ref, cos_ref, sin_ref, q_out, k_out, v_out):
    cosv, sinv = cos_ref[...], sin_ref[...]
    for start in range(0, q_ref.shape[1], LANES):
        at = slice(start, start + LANES)
        q_out[:, at] = turn(q_ref[:, at], cosv, sinv).astype(bf16)
        k_out[:, at] = turn(k_ref[:, at], cosv, sinv).astype(bf16)
    v_out[...] = v_ref[...].astype(bf16)


def turn_rows(qkv, cosv, sinv):
    rows, width = qkv.shape[0], qkv.shape[1] // 3
    wide = 3 * LANES if width % (3 * LANES) == 0 else LANES
    blocks = width // wide
    block = lambda shift: pl.BlockSpec((rows, wide), lambda i: (0, i + shift))
    whole = pl.BlockSpec((rows, LANES), lambda i: (0, 0))
    return pl.pallas_call(
        turn_kernel,
        grid=(blocks,),
        in_specs=[block(0), block(blocks), block(2 * blocks), whole, whole],
        out_specs=[block(0)] * 3,
        out_shape=[jax.ShapeDtypeStruct((rows, width), bf16)] * 3,
        cost_estimate=pl.CostEstimate(
            flops=rows * width * 12, bytes_accessed=rows * width * 18, transcendentals=0
        ),
    )(qkv, qkv, qkv, cosv, sinv)


def key_masks(len_ref, core_ref, keys):
    place = lax.broadcasted_iota(jnp.int32, (1, keys), 1)
    own = place + core_ref[0] * keys
    far = place + (1 - core_ref[0]) * keys
    return [jnp.where(at < len_ref[0], 0.0, -1e30).astype(f32) for at in (own, far)]


def attend_kernel(len_ref, core_ref, q_ref, k_ref, kf_ref, v_ref, vf_ref, *refs, tile):
    out_ref, lse_ref = refs[-2:]
    rows = q_ref.shape[0]
    masks = key_masks(len_ref, core_ref, rows)
    keyed = (k_ref[...], kf_ref[...])
    valued = (v_ref[...], vf_ref[...])
    lane = lax.broadcasted_iota(jnp.int32, (tile, LANES), 1)
    for t in range(rows // tile):
        at = pl.ds(t * tile, tile)
        query = q_ref[at, :] * bf16(HD**-0.5)
        mixed, lses = [], []
        for head in range(LANES // HD):
            mine = jnp.where(lane // HD == head, query, bf16(0))
            scores = [dense_nt(mine, k) + mask for k, mask in zip(keyed, masks)]
            top = jnp.maximum(*[jnp.max(s, 1, keepdims=True) for s in scores])
            expo = [jnp.exp(s - top) for s in scores]
            total = sum(jnp.sum(e, 1, keepdims=True) for e in expo)
            inverse = 1.0 / total
            mixed.append(sum(dense((e * inverse).astype(bf16), v) for e, v in zip(expo, valued)))
            lses.append(top + jnp.log(total))
        out_ref[at, :] = jnp.where(lane < HD, mixed[0], mixed[1]).astype(bf16)
        lse_ref[at, :] = jnp.where(lane < HD, lses[0], lses[1])


def attend(length, core, query, keyed, keyed_far, valued, valued_far, ready=()):
    rows, width = query.shape
    smem = pl.BlockSpec(memory_space=pltpu.SMEM)
    block = pl.BlockSpec((rows, LANES), lambda i: (0, i))
    return pl.pallas_call(
        functools.partial(attend_kernel, tile=256),
        grid=(width // LANES,),
        in_specs=[smem, smem] + [block] * 5 + [pl.BlockSpec(memory_space=pl.ANY)] * len(ready),
        out_specs=[block, block],
        out_shape=[
            jax.ShapeDtypeStruct((rows, width), bf16),
            jax.ShapeDtypeStruct((rows, width), f32),
        ],
        compiler_params=pltpu.CompilerParams(vmem_limit_bytes=48 * 2**20),
        cost_estimate=pl.CostEstimate(
            flops=8 * rows * rows * width, bytes_accessed=rows * width * 18,
            transcendentals=2 * rows * rows * width // HD,
        ),
    )(length, core, query, keyed, keyed_far, valued, valued_far, *ready)


def attend_back_kernel(
    len_ref,
    core_ref,
    q_ref,
    k_ref,
    kf_ref,
    v_ref,
    vf_ref,
    lse_ref,
    do_ref,
    cos_ref,
    sin_ref,
    cos_far_ref,
    sin_far_ref,
    *refs,
    tile,
):
    dq_ref, dk_ref, dkf_ref, dv_ref, dvf_ref = refs[-5:]
    rows = q_ref.shape[0]
    masks = key_masks(len_ref, core_ref, rows)
    keyed = (k_ref[...], kf_ref[...])
    valued = (v_ref[...], vf_ref[...])
    lane = lax.broadcasted_iota(jnp.int32, (tile, LANES), 1)
    first = lax.broadcasted_iota(jnp.int32, (rows, LANES), 1) < HD
    dk, dv = [None, None], [None, None]
    for t in range(rows // tile):
        at = pl.ds(t * tile, tile)
        query = q_ref[at, :] * bf16(HD**-0.5)
        grad = do_ref[at, :]
        dqs, dks, dvs = [], [[], []], [[], []]
        for head in range(LANES // HD):
            mine = lane // HD == head
            q_mine = jnp.where(mine, query, bf16(0))
            g_mine = jnp.where(mine, grad, bf16(0))
            lse = lse_ref[at, head * HD : head * HD + 1]
            probs = [jnp.exp(dense_nt(q_mine, k) + mask - lse) for k, mask in zip(keyed, masks)]
            grad_p = [dense_nt(g_mine, v) for v in valued]
            delta = sum(jnp.sum(p * g, 1, keepdims=True) for p, g in zip(probs, grad_p))
            grad_s = [(p * (g - delta)).astype(bf16) for p, g in zip(probs, grad_p)]
            dqs.append(sum(dense(s, k) for s, k in zip(grad_s, keyed)))
            for side in range(2):
                dks[side].append(dense_tn(grad_s[side], query))
                dvs[side].append(dense_tn(probs[side].astype(bf16), grad))
        turned = turn(jnp.where(lane < HD, dqs[0], dqs[1]), cos_ref[at, :], -sin_ref[at, :])
        dq_ref[at, :] = (turned * HD**-0.5).astype(bf16)
        for side in range(2):
            part_k = jnp.where(first, *dks[side])
            part_v = jnp.where(first, *dvs[side])
            dk[side] = part_k if t == 0 else dk[side] + part_k
            dv[side] = part_v if t == 0 else dv[side] + part_v
    dk_ref[...] = turn(dk[0], cos_ref[...], -sin_ref[...])
    dkf_ref[...] = turn(dk[1], cos_far_ref[...], -sin_far_ref[...]).astype(bf16)
    dv_ref[...] = dv[0]
    dvf_ref[...] = dv[1].astype(bf16)


def attend_back(length, core, *arrays, ready=()):
    query = arrays[0]
    rows, width = query.shape
    smem = pl.BlockSpec(memory_space=pltpu.SMEM)
    block = pl.BlockSpec((rows, LANES), lambda i: (0, i))
    return pl.pallas_call(
        functools.partial(attend_back_kernel, tile=256),
        grid=(width // LANES,),
        in_specs=[smem, smem]
        + [block] * 7
        + [pl.BlockSpec((rows, LANES), lambda i: (0, 0))] * 4
        + [pl.BlockSpec(memory_space=pl.ANY)] * len(ready),
        out_specs=[block] * 5,
        out_shape=[jax.ShapeDtypeStruct((rows, width), t) for t in (bf16, f32, bf16, f32, bf16)],
        compiler_params=pltpu.CompilerParams(vmem_limit_bytes=48 * 2**20),
        cost_estimate=pl.CostEstimate(
            flops=20 * rows * rows * width, bytes_accessed=rows * width * 32,
            transcendentals=2 * rows * rows * width // HD,
        ),
    )(length, core, *arrays, *ready)
def adamw(weight, first, second, grad, rate):
    first = 0.9 * first + 0.1 * grad
    second = 0.999 * second + 0.001 * grad * grad
    step = first / (1.0 - 0.9**STEP) / (jnp.sqrt(second / (1.0 - 0.999**STEP)) + 1e-08)
    return (weight - rate * (step + 0.01 * weight), first, second)


def hop(x, dl=0, dq=0, dr=0):
    reps = lax.axis_size("rep")
    lines = lax.axis_size("dp") // PLANE
    pairs = []
    for l in range(lines):
        for q in range(PLANE):
            for r in range(reps):
                to = (((l + dl) % lines) * PLANE + (q ^ dq)) * reps + (r ^ dr)
                pairs.append(((l * PLANE + q) * reps + r, to))
    return lax.ppermute(x, BOTH, pairs)


def step_line(x, way, reach):
    lines = lax.axis_size("dp") // PLANE
    pairs = []
    for l in range(lines):
        if 0 <= l + way * reach < lines:
            for q in range(PLANE):
                pairs.append((l * PLANE + q, (l + way) * PLANE + q))
    return lax.ppermute(x, "dp", pairs)


def pick_half(value, index):
    size = value.shape[1] // 2
    return lax.dynamic_slice_in_dim(value, index * size, size, axis=1)


def chip_product(left, left_far, right):
    rep_idx = lax.axis_index("rep")
    far = hop(pick_half(right, 1 - rep_idx), dr=1)
    return dense_tn(left, pick_half(right, rep_idx)) + dense_tn(left_far, far)


def plane_blocks(value):
    lines = lax.axis_size("dp") // PLANE
    return value.reshape(lines, 2, 2, value.shape[0] // (lines * PLANE), -1)


def split_blocks(blocks, axis, place):
    bit = (lax.axis_index("dp") >> axis) & 1
    far = lax.dynamic_index_in_dim(blocks, 1 - bit, place, False).astype(bf16)
    return lax.dynamic_index_in_dim(blocks, bit, place, False), hop(far, dq=1 << axis)


def reduce_line(blocks):
    lines = blocks.shape[0]
    line = lax.axis_index("dp") // PLANE
    total = lax.dynamic_index_in_dim(blocks, line, 0, False)
    for d in range(1, lines):
        total = total + hop(
            lax.dynamic_index_in_dim(blocks, (line + d) % lines, 0, False), dl=d
        )
    return total


def join_cores(parts):
    rep_idx = lax.axis_index("rep")
    mine = lax.dynamic_index_in_dim(parts, rep_idx, 0, False)
    far = hop(lax.dynamic_index_in_dim(parts, 1 - rep_idx, 0, False), dr=1)
    return jnp.where(rep_idx == 0, mine, far), jnp.where(rep_idx == 0, far, mine)


def add_up(value):
    lines = lax.axis_size("dp") // PLANE
    line = lax.axis_index("dp") // PLANE
    value = value + hop(value, dr=1)
    far = [hop(value, dq=dq) for dq in range(1, PLANE)]
    value = (value + far[0]) + (far[1] + far[2])
    every = jnp.stack([value] + [hop(value, dl=-d) for d in range(1, lines)])
    every = lax.dynamic_slice_in_dim(
        jnp.concatenate([every, every], 0), (lines - line) % lines, lines
    )
    return jnp.sum(every, 0)


def mix_kernel(idx_ref, mix_ref, *refs, groups, cands, counts):
    pieces = refs[: len(counts)]
    out_ref, tab, stage, sem = refs[-4:]

    @pl.when(pl.program_id(0) == 0)
    def _():
        def copy(j):
            return pltpu.make_async_copy(
                pieces[j], stage.at[j % 2, pl.ds(0, counts[j])], sem.at[j % 2]
            )

        copy(0).start()
        base = 0
        for j, rows in enumerate(counts):
            if j + 1 < len(counts):
                copy(j + 1).start()
            copy(j).wait()

            @pl.loop(0, rows // 16)
            def _(t, j=j, base=base):
                part = stage[j % 2, pl.ds(pl.multiple_of(t * 16, 16), 16), :].astype(f32)
                for g in range(groups):
                    tab[pl.ds((base + t * 16) * groups + g, 16, stride=groups), :] = part[
                        :, g * LANES : (g + 1) * LANES
                    ]

            base += rows

    unroll = 4

    @pl.loop(0, idx_ref.shape[-1] // cands // unroll)
    def _(block):
        for u in range(unroll):
            p = block * unroll + u
            total = None
            for c in range(cands):
                row = tab[pl.ds(idx_ref[0, 0, p * cands + c], 8), :]
                term = row * mix_ref[0, 0, p * cands + c]
                total = term if total is None else total + term
            out_ref[0, pl.ds(p * groups, 8), :] = total


def mix_rows(idx, mix, pieces, cands):
    groups = pieces[0].shape[1] // LANES
    lines, _, entries = idx.shape
    counts = tuple(piece.shape[0] for piece in pieces)
    rows = entries // cands * groups + 8
    return pl.pallas_call(
        functools.partial(mix_kernel, groups=groups, cands=cands, counts=counts),
        grid=(lines,),
        in_specs=[pl.BlockSpec((1, 1, entries), lambda i: (i, 0, 0), memory_space=pltpu.SMEM)] * 2
        + [pl.BlockSpec(memory_space=pl.ANY)] * len(pieces),
        out_specs=pl.BlockSpec((1, rows, LANES), lambda i: (i, 0, 0)),
        out_shape=jax.ShapeDtypeStruct((lines, rows, LANES), f32),
        scratch_shapes=[
            pltpu.VMEM((sum(counts) * groups + 8, LANES), f32),
            pltpu.VMEM((2, max(counts), groups * LANES), bf16),
            pltpu.SemaphoreType.DMA((2,)),
        ],
        compiler_params=pltpu.CompilerParams(vmem_limit_bytes=60 * 2**20),
        cost_estimate=pl.CostEstimate(
            flops=lines * entries * 2048, bytes_accessed=40 * 2**20, transcendentals=0
        ),
    )(idx, mix, *pieces)


def spread_kernel(cnt_ref, row_ref, pos_ref, mix_ref, *refs, groups, arrays, last):
    sources = refs[:arrays]
    if last:
        total_in, head_ref, out_ref, sq_ref, total, rows32, stage, sem, total_sem = refs[arrays:]
    else:
        total, rows32, stage, sem = refs[arrays:]
    length = sources[0].shape[1]
    blocks = [source.at[k] for source in sources for k in range(source.shape[0])]
    n = len(blocks)

    def copy(k):
        return pltpu.make_async_copy(blocks[k], stage.at[k % 2], sem.at[k % 2])

    copy(0).start()
    if last:
        load = pltpu.make_async_copy(total_in, total, total_sem)
        load.start()
        load.wait()
    else:

        @pl.loop(0, total.shape[0] // 64)
        def _(t):
            total[pl.ds(pl.multiple_of(t * 64, 64), 64), :] = jnp.zeros((64, LANES), f32)

    unroll = 4
    for k in range(n):
        if k + 1 < n:
            copy(k + 1).start()
        copy(k).wait()

        @pl.loop(0, length // 64)
        def _(t, k=k):
            at = pl.multiple_of(t * 64, 64)
            rows32[pl.ds(at, 64), :] = stage[k % 2, pl.ds(at, 64), :].astype(f32)

        @pl.loop(0, (cnt_ref[k] + unroll - 1) // unroll)
        def _(block, k=k):
            for u in range(unroll):
                e = block * unroll + u
                at = pl.ds(pl.multiple_of(row_ref[k, e] * 8, 8), 8)
                term = mix_ref[k, e] * rows32[pl.ds(pos_ref[k, e], 8), :]
                total[at, :] = total[at, :] + term

    if not last:
        return
    vocab = out_ref.shape[0]

    def finish(at, size, start):
        squares = jnp.zeros((size, LANES), f32)
        for g in range(groups):
            columns = slice(g * LANES, (g + 1) * LANES)
            value = head_ref[pl.ds(at, size), columns] + total[pl.ds(start + g, size, stride=8), :]
            out_ref[pl.ds(at, size), columns] = value
            squares = squares + value * value
        return squares

    squares = lax.fori_loop(
        0,
        vocab // 8,
        lambda t, so_far: so_far + finish(pl.multiple_of(t * 8, 8), 8, t * 64),
        jnp.zeros((8, LANES), f32),
    )
    sq_ref[...] = squares
    if vocab % 8:
        at = vocab // 8 * 8
        sq_ref[0 : vocab % 8, :] += finish(at, vocab % 8, at * 8)


def spread_rows(lists, sources, vocab, width, total=None, head=None):
    groups = width // LANES
    length = sources[0].shape[1]
    total_rows = -(-vocab * 8 // 64) * 64
    last = total is not None
    smem = pl.BlockSpec(memory_space=pltpu.SMEM)
    vmem = pl.BlockSpec(memory_space=pltpu.VMEM)
    hbm = pl.BlockSpec(memory_space=pl.ANY)
    scratch = [
        pltpu.VMEM((length + 8, LANES), f32),
        pltpu.VMEM((2, length, LANES), bf16),
        pltpu.SemaphoreType.DMA((2,)),
    ]
    if last:
        extra_specs, extra = [hbm, vmem], [total, head]
        out_specs = [vmem, vmem]
        out_shape = [
            jax.ShapeDtypeStruct((vocab, width), f32),
            jax.ShapeDtypeStruct((8, LANES), f32),
        ]
        scratch = [pltpu.VMEM((total_rows, LANES), f32)] + scratch + [pltpu.SemaphoreType.DMA]
    else:
        extra_specs, extra = [], []
        out_specs = vmem
        out_shape = jax.ShapeDtypeStruct((total_rows, LANES), f32)
    entries = sum(source.shape[0] for source in sources) * lists[1].shape[1] // 2
    return pl.pallas_call(
        functools.partial(
            spread_kernel,
            groups=groups,
            arrays=len(sources),
            last=last,
        ),
        in_specs=[smem] * 4 + [hbm] * len(sources) + extra_specs,
        out_specs=out_specs,
        out_shape=out_shape,
        scratch_shapes=scratch,
        compiler_params=pltpu.CompilerParams(vmem_limit_bytes=60 * 2**20),
        cost_estimate=pl.CostEstimate(
            flops=entries * 2048, bytes_accessed=entries * 10240, transcendentals=0
        ),
    )(*lists, *sources, *extra)


def local(
    noise_owner,
    noise_offset,
    option_scores,
    seq_lengths,
    time_index,
    loss_pick,
    loss_target,
    vocab_table,
    table_mom,
    table_sq,
    attn_proj,
    proj_mom,
    proj_sq,
    out_proj,
    outp_mom,
    outp_sq,
    up_proj,
    up_mom,
    up_sq,
    down_proj,
    down_mom,
    down_sq,
    time_proj,
    time_mom,
    time_sq,
    mod_proj,
    mod_mom,
    mod_sq,
    final_proj,
    final_mom,
    final_sq,
    norm_gains,
    gains_mom,
    gains_sq,
):
    devices = lax.axis_size(BOTH)
    reps = lax.axis_size("rep")
    n_dp = lax.axis_size("dp")
    lines = n_dp // PLANE
    dp_idx = lax.axis_index("dp")
    rep_idx = lax.axis_index("rep")
    me = dp_idx * reps + rep_idx
    line = dp_idx // PLANE
    chip = dp_idx % PLANE
    _, half, cands = noise_offset.shape
    vocab, width = vocab_table.shape
    heads = width // HD
    groups = width // LANES
    swaps = [(dq, dr) for dq in range(PLANE) for dr in range(reps)]

    padded = -(-vocab // 16) * 16
    table_low = jnp.pad(vocab_table.astype(bf16), ((0, padded - vocab), (0, 0)))
    cut = padded // 32 * 16
    upper_rows, lower_rows = table_low[:cut], table_low[cut:]
    first, second = {0: upper_rows}, {0: lower_rows}
    for dq in (1, 2):
        first[dq] = hop(upper_rows, dq=dq)
        second[dq] = hop(lower_rows, dq=dq)

    owner = noise_owner.reshape(-1)
    offset = noise_offset.reshape(-1)
    mixing = jax.nn.softmax(option_scores.reshape(half, cands) / annealed_softness, axis=-1)
    names = (owner * padded + offset).astype(f32).reshape(-1, LANES)
    packed = jnp.concatenate([names, mixing.reshape(-1, LANES)], 0)
    on_line = jnp.stack([packed] + [hop(packed, dl=-d) for d in range(1, lines)])
    on_line, first, second = lax.optimization_barrier((on_line, first, second))
    first[3] = hop(first[1], dq=2)
    second[3] = hop(second[2], dq=1)
    pieces = []
    for dq in range(PLANE):
        pieces += [first[dq], second[dq]]
        pieces += [hop(first[dq], dr=1), hop(second[dq], dr=1)]
    line_owner = on_line[:, : names.shape[0]].astype(jnp.int32)
    line_mix = on_line[:, names.shape[0] :]
    row_owner = line_owner // padded
    slot_of = (((row_owner // reps) % PLANE) ^ chip) * reps + ((row_owner % reps) ^ rep_idx)
    here = (row_owner // (reps * PLANE)) == line
    row_at = jnp.where(here, slot_of * padded + line_owner % padded, 0) * groups
    mix_here = jnp.where(here, line_mix, 0.0)
    row_at = row_at.reshape(lines, 1, half * cands)
    mix_here = mix_here.reshape(lines, 1, half * cands)
    parts = {}

    def mix_some(which):
        out = mix_rows(
            jnp.stack([row_at[d] for d in which]),
            jnp.stack([mix_here[d] for d in which]),
            pieces,
            cands,
        )
        for k, d in enumerate(which):
            parts[d] = out[k, : half * groups]

    mix_some((1, lines - 1))
    mix_some(tuple(range(2, lines - 1)) + (0,))
    ahead = back = None
    for d in range(lines - 1, 0, -1):
        to_right = parts[d] if ahead is None else parts[d] + ahead
        to_left = parts[lines - d] if back is None else parts[lines - d] + back
        ahead = step_line(to_right, 1, d)
        back = step_line(to_left, -1, d)
        if d == lines - 1:
            ahead, back, owner, offset = lax.optimization_barrier((ahead, back, owner, offset))

    cap = max(2, 2 * half * cands // devices)
    member = (owner[:, None] == jnp.arange(devices, dtype=jnp.int32)[None, :]).astype(jnp.int32)
    slot = jnp.sum((jnp.cumsum(member, 0) - member) * member, 1)
    flat_slot = owner * cap + slot
    entry = offset * half + jnp.arange(half * cands, dtype=jnp.int32) // cands + 1
    empty = jnp.zeros((devices * cap,), f32)
    lists = [
        empty.at[flat_slot].set(value).reshape(devices, cap)
        for value in (entry.astype(f32), mixing.reshape(-1))
    ]
    asked = jnp.concatenate(lists, 1)
    ahead, back, asked = lax.optimization_barrier((ahead, back, asked))
    x0 = (parts[0] + ahead + back).reshape(half, width)

    def gather(value, axis=0):
        return lax.all_gather(value.astype(bf16), BOTH, axis=axis, tiled=True)

    small = (time_proj, mod_proj, final_proj, norm_gains)
    flat = jnp.concatenate([value.reshape(-1) for value in small])
    flat = jnp.pad(flat, (0, -flat.size % (8 * LANES))).reshape(1, -1, LANES)
    small_all = gather(flat).reshape(devices, -1)
    qkv_w = gather(attn_proj)
    out_w = gather(out_proj)
    up_w = gather(up_proj)
    down_w = gather(down_proj)
    unpacked = []
    at = 0
    for value in small:
        part = small_all[:, at : at + value.size].astype(f32).reshape((devices,) + value.shape)
        unpacked.append(part)
        at += value.size
    time_f = unpacked[0].reshape(-1, time_proj.shape[1])
    mod_f = unpacked[1].reshape(-1, mod_proj.shape[1])
    final_f = unpacked[2].reshape(-1, final_proj.shape[1])
    gain_f = unpacked[3].transpose(1, 0, 2).reshape(norm_gains.shape[0], width)

    length = lax.dynamic_slice_in_dim(seq_lengths, dp_idx, 1)
    feats = time_features(time_index, time_f.shape[0])
    cond, silu_back = jax.vjp(jax.nn.silu, exact(feats, time_f))
    my_cond = lax.dynamic_slice_in_dim(cond, dp_idx, 1)
    mods = exact(my_cond, mod_f)
    fmods = exact(my_cond, final_f)
    sh1, sc1, g1, sh2, sc2, g2 = jnp.split(mods, 6, -1)
    fsh, fsc = jnp.split(fmods, 2, -1)

    n1, r1 = normalize(x0)
    h1b = (n1 * gain_f[0] * (1.0 + sc1) + sh1).astype(bf16)
    qkv = dense(h1b, qkv_w)
    places = jnp.arange(half, dtype=jnp.int32)
    turns = []
    for core in (rep_idx, 1 - rep_idx):
        cosv, sinv = rope_tables(core * half + places, HD)
        turns += [jnp.tile(cosv, (1, 4)), jnp.concatenate([-sinv, sinv] * 2, 1)]
    query, keyed, valued = turn_rows(qkv, turns[0], turns[1])
    attended = (query, keyed, hop(keyed, dr=1), valued, hop(valued, dr=1))
    core = rep_idx.reshape(1)
    mixed_b, lse_att = attend(length, core, *attended)
    asked = lax.all_to_all(asked, BOTH, split_axis=0, concat_axis=0, tiled=True)
    attn = dense(mixed_b, out_w)
    x1 = x0 + g1 * attn
    n2, r2 = normalize(x1)
    h2b = (n2 * gain_f[1] * (1.0 + sc2) + sh2).astype(bf16)
    upper = dense(h2b, up_w)
    act, gelu_back = jax.vjp(lambda u: jax.nn.gelu(u, approximate=True), upper)
    act_b = act.astype(bf16)
    mlp = dense(act_b, down_w)
    x2 = x1 + g2 * mlp
    nf, rf = normalize(x2)
    final = nf * gain_f[2] * (1.0 + fsc) + fsh

    picks = loss_pick.shape[-1]
    tau = (time_index.astype(f32) + 1.0) / TSTEPS
    starts = (jnp.arange(reps, dtype=jnp.int32) * half)[None, :, None]
    weight_all = jnp.where(
        loss_pick + starts < seq_lengths[:, None, None], (1.0 / (0.1 + tau))[:, None, None], 0.0
    )
    coefficient_aggregate = jnp.sum(weight_all)

    def of_line(values, at_chip, at_core):
        mine = lax.dynamic_slice(
            values.reshape(lines, PLANE, reps, picks), (0, at_chip, at_core, 0), (lines, 1, 1, picks)
        )
        return from_me(mine.reshape(lines, picks))

    def from_me(values):
        return lax.dynamic_slice_in_dim(jnp.concatenate([values, values], 0), line, lines)

    def from_start(values):
        return lax.dynamic_slice_in_dim(
            jnp.concatenate([values, values], 0), (lines - line) % lines, lines
        )

    targets = of_line(loss_target, chip, rep_idx).reshape(-1)
    weight = of_line(weight_all, chip, rep_idx).reshape(-1)
    my_pick = lax.dynamic_slice(loss_pick, (dp_idx, rep_idx, 0), (1, 1, picks)).reshape(picks)
    spread = (jnp.arange(half, dtype=jnp.int32)[:, None] == my_pick[None, :]).astype(f32)
    final, asked = lax.optimization_barrier((final, asked))
    asked, asked_mix = asked[:, :cap].astype(jnp.int32), asked[:, cap:]
    rows_b = jnp.take(final, my_pick, axis=0).astype(bf16)
    every = jnp.concatenate([rows_b] + [hop(rows_b, dl=-d) for d in range(1, lines)], 0)
    plane_table = jnp.concatenate(pieces, 0)
    logits = dense_nt(every, plane_table)
    column = jnp.arange(plane_table.shape[0], dtype=jnp.int32)
    exists = (column % padded) < vocab
    t_owner = targets // vocab
    t_slot = (((t_owner // reps) % PLANE) ^ chip) * reps + ((t_owner % reps) ^ rep_idx)
    t_column = jnp.where(
        t_owner // (reps * PLANE) == line, t_slot * padded + targets % vocab, -1
    )
    hit = column[None, :] == t_column[:, None]
    logits = jnp.where(exists[None, :], logits, -1e30)
    top = jnp.max(logits, -1)
    sums = jnp.sum(jnp.exp(logits - top[:, None]), -1)
    tgt = jnp.sum(jnp.where(hit, logits, 0.0), -1)
    stats = from_start(
        jnp.stack([value.reshape(lines, picks) for value in (top, sums, tgt)], 1)
    )
    stats_all = jnp.stack([stats] + [hop(stats, dl=-d) for d in range(1, lines)])
    tops = stats_all[:, :, 0]
    best = jnp.max(tops, 0)
    sum_all = jnp.sum(stats_all[:, :, 1] * jnp.exp(tops - best), 0)
    lse_line = best + jnp.log(sum_all)
    tgt_line = jnp.sum(stats_all[:, :, 2], 0)
    loss_here = jnp.sum(from_start(weight.reshape(lines, picks)) * (lse_line - tgt_line))
    loss_here = jnp.where(line == 0, loss_here, 0.0)
    lse = from_me(lse_line).reshape(-1)
    probs = jnp.exp(logits - lse[:, None])
    dlogit = ((weight / coefficient_aggregate)[:, None] * (probs - hit.astype(f32))).astype(bf16)
    drows_part = dense(dlogit, plane_table).reshape(lines, picks, width)
    drows = drows_part[0]
    for d in range(1, lines):
        drows = drows + hop(drows_part[d], dl=d)
    every, lse, drows = lax.optimization_barrier((every, lse, drows))
    lse_x, lse_y = hop(lse, dq=1), hop(lse, dq=2)
    every_x, every_y = hop(every, dq=1), hop(every, dq=2)
    lse_plane = jnp.stack([lse, lse_x, lse_y, hop(lse_x, dq=2)])
    rows_plane = jnp.stack([every, every_x, every_y, hop(every_x, dq=2)])
    lse_all = jnp.concatenate([lse_plane, hop(lse_plane, dr=1)], 0).reshape(-1)
    rows_all = jnp.concatenate([rows_plane, hop(rows_plane, dr=1)], 0).reshape(-1, width)
    among = [(chip ^ dq, rep_idx ^ dr) for dr in range(reps) for dq in range(PLANE)]
    targets_all = jnp.concatenate([of_line(loss_target, q, r).reshape(-1) for q, r in among])
    weight_rows = jnp.concatenate([of_line(weight_all, q, r).reshape(-1) for q, r in among])

    grad_final = exact(spread, drows)
    dx2, dfsh, dfsc, dgain_f = modulate_back(grad_final, nf, rf, gain_f[2], fsc)
    dg2 = jnp.sum(dx2 * mlp, 0)
    dmlp = (dx2 * g2).astype(bf16)
    g_down = chip_product(act_b, hop(act_b, dr=1), dmlp)
    dupper = gelu_back(dense_nt(dmlp, down_w))[0].astype(bf16)
    g_up = chip_product(h2b, hop(h2b, dr=1), dupper)
    dh2 = dense_nt(dupper, up_w)
    dn2x, dsh2, dsc2, dgain_2 = modulate_back(dh2, n2, r2, gain_f[1], sc2)
    dx1 = dx2 + dn2x
    dg1 = jnp.sum(dx1 * attn, 0)
    dattn = (dx1 * g1).astype(bf16)
    dattn, g_down, g_up, rows_all, lse_all = lax.optimization_barrier(
        (dattn, g_down, g_up, rows_all, lse_all)
    )
    down_1 = split_blocks(plane_blocks(g_down), 1, 1)
    up_1 = split_blocks(plane_blocks(g_up), 0, 2)
    g_out = chip_product(mixed_b, hop(mixed_b, dr=1), dattn)
    dmixed = dense_nt(dattn, out_w).astype(bf16)
    dquery, dkey, dkey_far, dvalue, dvalue_far = attend_back(
        length, core, *attended, lse_att, dmixed, *turns
    )
    dquery, dkey, dkey_far, dvalue, dvalue_far, down_1, up_1, g_out = lax.optimization_barrier(
        (dquery, dkey, dkey_far, dvalue, dvalue_far, down_1, up_1, g_out)
    )
    down_2 = split_blocks(down_1[0] + down_1[1].astype(f32), 0, 1)
    up_2 = split_blocks(up_1[0] + up_1[1].astype(f32), 1, 1)
    dkey = (dkey + hop(dkey_far, dr=1).astype(f32)).astype(bf16)
    dvalue = (dvalue + hop(dvalue_far, dr=1).astype(f32)).astype(bf16)
    dqkv = jnp.concatenate([dquery, dkey, dvalue], 1)
    dh1 = dense_nt(dqkv, qkv_w)
    dn1x, dsh1, dsc1, dgain_1 = modulate_back(dh1, n1, r1, gain_f[0], sc1)
    dx0 = dx1 + dn1x
    g_qkv = chip_product(h1b, hop(h1b, dr=1), dqkv)


    dx0_b = dx0.astype(bf16).reshape(1, half * groups, LANES)
    dx0_b, rows_all, lse_all, down_2, up_2 = lax.optimization_barrier(
        (dx0_b, rows_all, lse_all, down_2, up_2)
    )
    others = lines - 1
    cut = -(-2 * others // 3)
    on_line = jnp.concatenate([hop(dx0_b, dl=-d) for d in range(1, lines)], 0)
    own_x, own_y = hop(dx0_b, dq=1), hop(dx0_b, dq=2)
    g_last = jnp.concatenate([g_qkv, g_out], 1)
    last_1 = split_blocks(plane_blocks(g_last), 0, 2)
    on_line, own_x, own_y, last_1 = lax.optimization_barrier((on_line, own_x, own_y, last_1))
    last_2 = split_blocks(last_1[0] + last_1[1].astype(f32), 1, 1)
    own_xy = hop(own_y, dq=1)
    line_x, line_y = hop(on_line, dq=1), hop(on_line, dq=2)
    early = [(dx0_b, 0, 0), (own_x, 1, 0), (own_y, 2, 0), (own_xy, 3, 0), (on_line, 0, 1)]
    order = []

    def from_cores(gathered):
        sources = []
        for value, dq, first_d in gathered:
            sources.extend(add_source(value, dq, first_d))
        return sources

    def add_source(value, dq, first_d):
        for dr in range(reps):
            for d in range(first_d, first_d + value.shape[0]):
                order.append(
                    (((line + d) % lines) * PLANE + (chip ^ dq)) * reps + (rep_idx ^ dr)
                )
        return [value, hop(value, dr=1)]

    def lists_of(order):
        order = jnp.stack(order)
        entries = jnp.take(asked, order, axis=0)
        count = jnp.sum((entries > 0).astype(jnp.int32), 1)
        entries = jnp.maximum(entries - 1, 0)
        return (
            count,
            entries // half,
            (entries % half) * groups,
            jnp.take(asked_mix, order, axis=0),
        )

    sources = from_cores(early)
    begun = spread_rows(lists_of(order), sources, vocab, width)
    order.clear()
    line_x, line_y, begun = lax.optimization_barrier((line_x, line_y, begun))
    shards = [two[0] + two[1].astype(f32) for two in (down_2, up_2, last_2)]
    both = shards[1].shape[1]
    tall = shards[0].shape[1] // both
    pile = shards[0].reshape(lines, tall, both, -1)
    total = reduce_line(
        jnp.concatenate([pile[:, k] for k in range(tall)] + shards[1:], 2)
    )
    down_end = tall * pile.shape[3]
    pile = jnp.stack(jnp.split(total[:, :down_end], tall, 1))
    d_down = jnp.concatenate(join_cores(pile.reshape(reps, -1, pile.shape[2])), 1)
    left, right = join_cores(total[:, down_end:].reshape(reps, both // reps, -1))
    joined = []
    at = 0
    for columns in (up_proj.shape[1], attn_proj.shape[1], out_proj.shape[1]):
        part = slice(at, at + columns // 2)
        joined.append(jnp.concatenate([left[:, part], right[:, part]], 1))
        at += columns // 2
    d_up, d_qkv, d_out = joined
    late = [(line_x, 1, 1), (line_y, 2, 1), (hop(line_x[:cut], dq=2), 3, 1)]
    if cut < others:
        late.append((hop(line_y[cut:], dq=1), 3, 1 + cut))
    logits_mine = dense_nt(rows_all, table_low)
    own_column = jnp.where(targets_all // vocab == me, targets_all % vocab, -1)
    hit_mine = jnp.arange(padded, dtype=jnp.int32)[None, :] == own_column[:, None]
    dlogit_mine = (
        (weight_rows / coefficient_aggregate)[:, None]
        * (jnp.exp(logits_mine - lse_all[:, None]) - hit_mine.astype(f32))
    ).astype(bf16)
    head_grad = dense_tn(dlogit_mine, rows_all)
    sources = from_cores(late)
    table_grad, table_squares = spread_rows(
        lists_of(order), sources, vocab, width, begun, head_grad
    )

    sums_here = jnp.concatenate(
        [dsh1, dsc1, dg1, dsh2, dsc2, dg2, dfsh, dfsc, dgain_1, dgain_2, dgain_f]
    )
    sums_all = lax.all_gather(sums_here.reshape(1, -1, LANES), BOTH, axis=0, tiled=True)
    sums_all = sums_all.reshape(n_dp, reps, -1).sum(1)
    dmods = sums_all[:, : 6 * width]
    dfmods = sums_all[:, 6 * width : 8 * width]

    def my_columns(value, count):
        return lax.dynamic_slice_in_dim(value, me * count, count, axis=1)

    d_mod = exact_tn(my_columns(cond, mod_proj.shape[0]), dmods)
    d_final = exact_tn(my_columns(cond, final_proj.shape[0]), dfmods)
    dcond = exact_nt(dmods, mod_f) + exact_nt(dfmods, final_f)
    d_time = exact_tn(my_columns(feats, time_proj.shape[0]), silu_back(dcond)[0])
    d_gains = my_columns(
        jnp.sum(sums_all[:, 8 * width :], 0).reshape(3, width), norm_gains.shape[1]
    )

    reduced = (d_qkv, d_out, d_up, d_down, d_time, d_mod, d_final, d_gains)
    local_sq = jnp.sum(table_squares)
    for g in reduced:
        local_sq = local_sq + jnp.sum(g * g)
    totals = add_up(jnp.stack([local_sq, loss_here]))
    grad_norm = jnp.sqrt(totals[0])
    loss_sum = totals[1]
    clip = jnp.minimum(1.0, 0.01 / (grad_norm + 1e-06))
    masters = (attn_proj, out_proj, up_proj, down_proj, time_proj, mod_proj, final_proj, norm_gains)
    coefficients = (vocab_table,) + masters
    moms = (
        table_mom,
        proj_mom,
        outp_mom,
        up_mom,
        down_mom,
        time_mom,
        mod_mom,
        final_mom,
        gains_mom,
    )
    sqs = (table_sq, proj_sq, outp_sq, up_sq, down_sq, time_sq, mod_sq, final_sq, gains_sq)
    rates = (0.02, 0.02, 0.02, 0.02, 0.02, 0.02, 0.02, 0.02, 0.1)
    grads = (table_grad,) + reduced
    result = [loss_sum, coefficient_aggregate, grad_norm]
    for weight_now, first_m, second_m, grad, rate in zip(coefficients, moms, sqs, grads, rates):
        result.extend(adamw(weight_now, first_m, second_m, clip * grad, rate))
    return tuple(result)


def solution(mesh):
    shard = P(BOTH, None)
    columns = P(None, BOTH)
    return jax.shard_map(
        local,
        mesh=mesh,
        in_specs=(P("dp", "rep", None),) * 3 + (P(),) * 4 + (shard,) * 24 + (columns,) * 3,
        out_specs=(P(),) * 3 + (shard,) * 24 + (columns,) * 3,
        check_vma=False,
    )
```

```python
import functools
import math

import jax
import jax.numpy as jnp
from jax import lax
from jax.experimental import pallas as pl
from jax.experimental.pallas import tpu as pltpu
from jax.sharding import PartitionSpec as P

HD = 64
TSTEPS = 1000
STEP = 5
PLANE = 4
LANES = 128
BOTH = ("dp", "rep")

HIGH = lax.Precision.HIGHEST
annealed_softness = 0.5
bf16 = jnp.bfloat16
f32 = jnp.float32


def dense(a, b):
    return jnp.dot(a, b, preferred_element_type=f32)


def dense_nt(a, b):
    return lax.dot_general(a, b, (((1,), (1,)), ((), ())), preferred_element_type=f32)


def dense_tn(a, b):
    return lax.dot_general(a, b, (((0,), (0,)), ((), ())), preferred_element_type=f32)


def exact(a, b):
    return jnp.dot(a, b, precision=HIGH, preferred_element_type=f32)


def exact_nt(a, b):
    return lax.dot_general(
        a, b, (((1,), (1,)), ((), ())), precision=HIGH, preferred_element_type=f32
    )


def exact_tn(a, b):
    return lax.dot_general(
        a, b, (((0,), (0,)), ((), ())), precision=HIGH, preferred_element_type=f32
    )


def normalize(x):
    center = x - jnp.mean(x, -1, keepdims=True)
    rstd = lax.rsqrt(jnp.mean(center * center, -1, keepdims=True) + 1e-06)
    return (center * rstd, rstd)


def modulate_back(grad_h, normed, rstd, gain, scale):
    dshift = jnp.sum(grad_h, 0)
    weighted = grad_h * normed
    column = jnp.sum(weighted, 0)
    dscale = column * gain
    dgain = column * (1.0 + scale[0])
    grad_n = grad_h * gain * (1.0 + scale)
    grad_x = rstd * (
        grad_n
        - jnp.mean(grad_n, -1, keepdims=True)
        - normed * jnp.mean(grad_n * normed, -1, keepdims=True)
    )
    return (grad_x, dshift, dscale, dgain)


def rope_tables(pos, head):
    half = head // 2
    freqs = jnp.exp(-math.log(10000.0) * jnp.arange(half, dtype=f32) / half)
    angle = pos.astype(f32)[:, None] * freqs[None, :]
    return (jnp.cos(angle), jnp.sin(angle))


def time_features(steps, width):
    tau = (steps.astype(f32) + 1.0) / TSTEPS
    half = width // 2
    freqs = jnp.exp(-math.log(10000.0) * jnp.arange(half, dtype=f32) / half)
    angle = 1000.0 * tau[:, None] * freqs[None, :]
    return jnp.concatenate([jnp.cos(angle), jnp.sin(angle)], -1)


def turn(x, cosv, sinv):
    lane = lax.broadcasted_iota(jnp.int32, x.shape, 1)
    quarter = HD // 2
    swapped = jnp.where(
        lane % HD < quarter,
        pltpu.roll(x, LANES - quarter, axis=1),
        pltpu.roll(x, quarter, axis=1),
    )
    return x * cosv + swapped * sinv


def turn_kernel(q_ref, k_ref, v_ref, cos_ref, sin_ref, q_out, k_out, v_out):
    cosv, sinv = cos_ref[...], sin_ref[...]
    for start in range(0, q_ref.shape[1], LANES):
        at = slice(start, start + LANES)
        q_out[:, at] = turn(q_ref[:, at], cosv, sinv).astype(bf16)
        k_out[:, at] = turn(k_ref[:, at], cosv, sinv).astype(bf16)
    v_out[...] = v_ref[...].astype(bf16)


def turn_rows(qkv, cosv, sinv):
    rows, width = qkv.shape[0], qkv.shape[1] // 3
    wide = 3 * LANES if width % (3 * LANES) == 0 else LANES
    blocks = width // wide
    block = lambda shift: pl.BlockSpec((rows, wide), lambda i: (0, i + shift))
    whole = pl.BlockSpec((rows, LANES), lambda i: (0, 0))
    return pl.pallas_call(
        turn_kernel,
        grid=(blocks,),
        in_specs=[block(0), block(blocks), block(2 * blocks), whole, whole],
        out_specs=[block(0)] * 3,
        out_shape=[jax.ShapeDtypeStruct((rows, width), bf16)] * 3,
        cost_estimate=pl.CostEstimate(
            flops=rows * width * 12, bytes_accessed=rows * width * 18, transcendentals=0
        ),
    )(qkv, qkv, qkv, cosv, sinv)


def key_masks(len_ref, core_ref, keys):
    place = lax.broadcasted_iota(jnp.int32, (1, keys), 1)
    own = place + core_ref[0] * keys
    far = place + (1 - core_ref[0]) * keys
    return [jnp.where(at < len_ref[0], 0.0, -1e30).astype(f32) for at in (own, far)]


def attend_kernel(len_ref, core_ref, q_ref, k_ref, kf_ref, v_ref, vf_ref, *refs, tile):
    out_ref, lse_ref = refs[-2:]
    rows = q_ref.shape[0]
    masks = key_masks(len_ref, core_ref, rows)
    keyed = (k_ref[...], kf_ref[...])
    valued = (v_ref[...], vf_ref[...])
    lane = lax.broadcasted_iota(jnp.int32, (tile, LANES), 1)
    for t in range(rows // tile):
        at = pl.ds(t * tile, tile)
        query = q_ref[at, :] * bf16(HD**-0.5)
        mixed, lses = [], []
        for head in range(LANES // HD):
            mine = jnp.where(lane // HD == head, query, bf16(0))
            scores = [dense_nt(mine, k) + mask for k, mask in zip(keyed, masks)]
            top = jnp.maximum(*[jnp.max(s, 1, keepdims=True) for s in scores])
            expo = [jnp.exp(s - top) for s in scores]
            total = sum(jnp.sum(e, 1, keepdims=True) for e in expo)
            inverse = 1.0 / total
            mixed.append(sum(dense((e * inverse).astype(bf16), v) for e, v in zip(expo, valued)))
            lses.append(top + jnp.log(total))
        out_ref[at, :] = jnp.where(lane < HD, mixed[0], mixed[1]).astype(bf16)
        lse_ref[at, :] = jnp.where(lane < HD, lses[0], lses[1])


def attend(length, core, query, keyed, keyed_far, valued, valued_far, ready=()):
    rows, width = query.shape
    smem = pl.BlockSpec(memory_space=pltpu.SMEM)
    block = pl.BlockSpec((rows, LANES), lambda i: (0, i))
    return pl.pallas_call(
        functools.partial(attend_kernel, tile=256),
        grid=(width // LANES,),
        in_specs=[smem, smem] + [block] * 5 + [pl.BlockSpec(memory_space=pl.ANY)] * len(ready),
        out_specs=[block, block],
        out_shape=[
            jax.ShapeDtypeStruct((rows, width), bf16),
            jax.ShapeDtypeStruct((rows, width), f32),
        ],
        compiler_params=pltpu.CompilerParams(vmem_limit_bytes=48 * 2**20),
        cost_estimate=pl.CostEstimate(
            flops=8 * rows * rows * width, bytes_accessed=rows * width * 18,
            transcendentals=2 * rows * rows * width // HD,
        ),
    )(length, core, query, keyed, keyed_far, valued, valued_far, *ready)


def attend_back_kernel(
    len_ref,
    core_ref,
    q_ref,
    k_ref,
    kf_ref,
    v_ref,
    vf_ref,
    lse_ref,
    do_ref,
    cos_ref,
    sin_ref,
    cos_far_ref,
    sin_far_ref,
    *refs,
    tile,
):
    dq_ref, dk_ref, dkf_ref, dv_ref, dvf_ref = refs[-5:]
    rows = q_ref.shape[0]
    masks = key_masks(len_ref, core_ref, rows)
    keyed = (k_ref[...], kf_ref[...])
    valued = (v_ref[...], vf_ref[...])
    lane = lax.broadcasted_iota(jnp.int32, (tile, LANES), 1)
    first = lax.broadcasted_iota(jnp.int32, (rows, LANES), 1) < HD
    dk, dv = [None, None], [None, None]
    for t in range(rows // tile):
        at = pl.ds(t * tile, tile)
        query = q_ref[at, :] * bf16(HD**-0.5)
        grad = do_ref[at, :]
        dqs, dks, dvs = [], [[], []], [[], []]
        for head in range(LANES // HD):
            mine = lane // HD == head
            q_mine = jnp.where(mine, query, bf16(0))
            g_mine = jnp.where(mine, grad, bf16(0))
            lse = lse_ref[at, head * HD : head * HD + 1]
            probs = [jnp.exp(dense_nt(q_mine, k) + mask - lse) for k, mask in zip(keyed, masks)]
            grad_p = [dense_nt(g_mine, v) for v in valued]
            delta = sum(jnp.sum(p * g, 1, keepdims=True) for p, g in zip(probs, grad_p))
            grad_s = [(p * (g - delta)).astype(bf16) for p, g in zip(probs, grad_p)]
            dqs.append(sum(dense(s, k) for s, k in zip(grad_s, keyed)))
            for side in range(2):
                dks[side].append(dense_tn(grad_s[side], query))
                dvs[side].append(dense_tn(probs[side].astype(bf16), grad))
        turned = turn(jnp.where(lane < HD, dqs[0], dqs[1]), cos_ref[at, :], -sin_ref[at, :])
        dq_ref[at, :] = (turned * HD**-0.5).astype(bf16)
        for side in range(2):
            part_k = jnp.where(first, *dks[side])
            part_v = jnp.where(first, *dvs[side])
            dk[side] = part_k if t == 0 else dk[side] + part_k
            dv[side] = part_v if t == 0 else dv[side] + part_v
    dk_ref[...] = turn(dk[0], cos_ref[...], -sin_ref[...])
    dkf_ref[...] = turn(dk[1], cos_far_ref[...], -sin_far_ref[...]).astype(bf16)
    dv_ref[...] = dv[0]
    dvf_ref[...] = dv[1].astype(bf16)


def attend_back(length, core, *arrays, ready=()):
    query = arrays[0]
    rows, width = query.shape
    smem = pl.BlockSpec(memory_space=pltpu.SMEM)
    block = pl.BlockSpec((rows, LANES), lambda i: (0, i))
    return pl.pallas_call(
        functools.partial(attend_back_kernel, tile=256),
        grid=(width // LANES,),
        in_specs=[smem, smem]
        + [block] * 7
        + [pl.BlockSpec((rows, LANES), lambda i: (0, 0))] * 4
        + [pl.BlockSpec(memory_space=pl.ANY)] * len(ready),
        out_specs=[block] * 5,
        out_shape=[jax.ShapeDtypeStruct((rows, width), t) for t in (bf16, f32, bf16, f32, bf16)],
        compiler_params=pltpu.CompilerParams(vmem_limit_bytes=48 * 2**20),
        cost_estimate=pl.CostEstimate(
            flops=20 * rows * rows * width, bytes_accessed=rows * width * 32,
            transcendentals=2 * rows * rows * width // HD,
        ),
    )(length, core, *arrays, *ready)
def adamw(weight, first, second, grad, rate):
    first = 0.9 * first + 0.1 * grad
    second = 0.999 * second + 0.001 * grad * grad
    step = first / (1.0 - 0.9**STEP) / (jnp.sqrt(second / (1.0 - 0.999**STEP)) + 1e-08)
    return (weight - rate * (step + 0.01 * weight), first, second)


def hop(x, dl=0, dq=0, dr=0):
    reps = lax.axis_size("rep")
    lines = lax.axis_size("dp") // PLANE
    pairs = []
    for l in range(lines):
        for q in range(PLANE):
            for r in range(reps):
                to = (((l + dl) % lines) * PLANE + (q ^ dq)) * reps + (r ^ dr)
                pairs.append(((l * PLANE + q) * reps + r, to))
    return lax.ppermute(x, BOTH, pairs)


def step_line(x, way, reach):
    lines = lax.axis_size("dp") // PLANE
    pairs = []
    for l in range(lines):
        if 0 <= l + way * reach < lines:
            for q in range(PLANE):
                pairs.append((l * PLANE + q, (l + way) * PLANE + q))
    return lax.ppermute(x, "dp", pairs)


def pick_half(value, index):
    size = value.shape[1] // 2
    return lax.dynamic_slice_in_dim(value, index * size, size, axis=1)


def chip_product(left, left_far, right):
    rep_idx = lax.axis_index("rep")
    far = hop(pick_half(right, 1 - rep_idx), dr=1)
    return dense_tn(left, pick_half(right, rep_idx)) + dense_tn(left_far, far)


def plane_blocks(value):
    lines = lax.axis_size("dp") // PLANE
    return value.reshape(lines, 2, 2, value.shape[0] // (lines * PLANE), -1)


def split_blocks(blocks, axis, place):
    bit = (lax.axis_index("dp") >> axis) & 1
    far = lax.dynamic_index_in_dim(blocks, 1 - bit, place, False).astype(bf16)
    return lax.dynamic_index_in_dim(blocks, bit, place, False), hop(far, dq=1 << axis)


def gather_line(value):
    lines = lax.axis_size("dp") // PLANE
    line = lax.axis_index("dp") // PLANE

    def pass_on(x, way, k):
        pairs = []
        for l in range(lines):
            if 0 <= l - way * (k - 1) < lines and 0 <= l + way < lines:
                for q in range(PLANE):
                    pairs.append((l * PLANE + q, (l + way) * PLANE + q))
        return lax.ppermute(x, "dp", pairs)

    before, after = [value], [value]
    for k in range(1, lines):
        before.append(pass_on(before[-1], 1, k))
        after.append(pass_on(after[-1], -1, k))
    return jnp.concatenate(
        [jnp.where(line + d < lines, after[d], before[lines - d]) for d in range(1, lines)], 0
    )


def block_at(blocks, shift):
    line = lax.axis_index("dp") // PLANE
    return lax.dynamic_index_in_dim(blocks, jnp.mod(line + shift, blocks.shape[0]), 0, False)


def reduce_step(blocks, sums, reach):
    to_right, to_left = block_at(blocks, reach), block_at(blocks, -reach)
    if sums is not None:
        to_right, to_left = to_right + sums[0], to_left + sums[1]
    return step_line(to_right, 1, reach), step_line(to_left, -1, reach)


def join_cores(parts):
    rep_idx = lax.axis_index("rep")
    mine = lax.dynamic_index_in_dim(parts, rep_idx, 0, False)
    far = hop(lax.dynamic_index_in_dim(parts, 1 - rep_idx, 0, False), dr=1)
    return jnp.where(rep_idx == 0, mine, far), jnp.where(rep_idx == 0, far, mine)


def add_up(value):
    lines = lax.axis_size("dp") // PLANE
    line = lax.axis_index("dp") // PLANE
    value = value + hop(value, dr=1)
    far = [hop(value, dq=dq) for dq in range(1, PLANE)]
    value = (value + far[0]) + (far[1] + far[2])
    every = jnp.stack([value] + [hop(value, dl=-d) for d in range(1, lines)])
    every = lax.dynamic_slice_in_dim(
        jnp.concatenate([every, every], 0), (lines - line) % lines, lines
    )
    return jnp.sum(every, 0)


def mix_kernel(idx_ref, mix_ref, *refs, groups, cands, counts):
    pieces = refs[: len(counts)]
    out_ref, tab, stage, sem = refs[-4:]

    @pl.when(pl.program_id(0) == 0)
    def _():
        def copy(j):
            return pltpu.make_async_copy(
                pieces[j], stage.at[j % 2, pl.ds(0, counts[j])], sem.at[j % 2]
            )

        copy(0).start()
        base = 0
        for j, rows in enumerate(counts):
            if j + 1 < len(counts):
                copy(j + 1).start()
            copy(j).wait()

            @pl.loop(0, rows // 16)
            def _(t, j=j, base=base):
                part = stage[j % 2, pl.ds(pl.multiple_of(t * 16, 16), 16), :].astype(f32)
                for g in range(groups):
                    tab[pl.ds((base + t * 16) * groups + g, 16, stride=groups), :] = part[
                        :, g * LANES : (g + 1) * LANES
                    ]

            base += rows

    unroll = 4

    @pl.loop(0, idx_ref.shape[-1] // cands // unroll)
    def _(block):
        for u in range(unroll):
            p = block * unroll + u
            total = None
            for c in range(cands):
                row = tab[pl.ds(idx_ref[0, 0, p * cands + c], 8), :]
                term = row * mix_ref[0, 0, p * cands + c]
                total = term if total is None else total + term
            out_ref[0, pl.ds(p * groups, 8), :] = total


def mix_rows(idx, mix, pieces, cands):
    groups = pieces[0].shape[1] // LANES
    lines, _, entries = idx.shape
    counts = tuple(piece.shape[0] for piece in pieces)
    rows = entries // cands * groups + 8
    return pl.pallas_call(
        functools.partial(mix_kernel, groups=groups, cands=cands, counts=counts),
        grid=(lines,),
        in_specs=[pl.BlockSpec((1, 1, entries), lambda i: (i, 0, 0), memory_space=pltpu.SMEM)] * 2
        + [pl.BlockSpec(memory_space=pl.ANY)] * len(pieces),
        out_specs=pl.BlockSpec((1, rows, LANES), lambda i: (i, 0, 0)),
        out_shape=jax.ShapeDtypeStruct((lines, rows, LANES), f32),
        scratch_shapes=[
            pltpu.VMEM((sum(counts) * groups + 8, LANES), f32),
            pltpu.VMEM((2, max(counts), groups * LANES), bf16),
            pltpu.SemaphoreType.DMA((2,)),
        ],
        compiler_params=pltpu.CompilerParams(vmem_limit_bytes=60 * 2**20),
        cost_estimate=pl.CostEstimate(
            flops=lines * entries * 2048, bytes_accessed=40 * 2**20, transcendentals=0
        ),
    )(idx, mix, *pieces)


def spread_kernel(cnt_ref, row_ref, pos_ref, mix_ref, *refs, groups, arrays, first, last):
    sources = refs[:arrays]
    refs = list(refs[arrays:])
    total_in = None if first else refs.pop(0)
    if last:
        head_ref, out_ref, sq_ref = refs[:3]
        refs = refs[3:]
    total, rows32, stage, sem, total_sem = refs
    length = sources[0].shape[1]
    blocks = [source.at[k] for source in sources for k in range(source.shape[0])]
    n = len(blocks)

    def copy(k):
        return pltpu.make_async_copy(blocks[k], stage.at[k % 2], sem.at[k % 2])

    copy(0).start()
    if not first:
        load = pltpu.make_async_copy(total_in, total, total_sem)
        load.start()
        load.wait()
    else:

        @pl.loop(0, total.shape[0] // 64)
        def _(t):
            total[pl.ds(pl.multiple_of(t * 64, 64), 64), :] = jnp.zeros((64, LANES), f32)

    unroll = 4
    for k in range(n):
        if k + 1 < n:
            copy(k + 1).start()
        copy(k).wait()

        @pl.loop(0, length // 64)
        def _(t, k=k):
            at = pl.multiple_of(t * 64, 64)
            rows32[pl.ds(at, 64), :] = stage[k % 2, pl.ds(at, 64), :].astype(f32)

        @pl.loop(0, (cnt_ref[k] + unroll - 1) // unroll)
        def _(block, k=k):
            for u in range(unroll):
                e = block * unroll + u
                at = pl.ds(pl.multiple_of(row_ref[k, e] * 8, 8), 8)
                term = mix_ref[k, e] * rows32[pl.ds(pos_ref[k, e], 8), :]
                total[at, :] = total[at, :] + term

    if not last:
        return
    vocab = out_ref.shape[0]

    def finish(at, size, start):
        squares = jnp.zeros((size, LANES), f32)
        for g in range(groups):
            columns = slice(g * LANES, (g + 1) * LANES)
            value = head_ref[pl.ds(at, size), columns] + total[pl.ds(start + g, size, stride=8), :]
            out_ref[pl.ds(at, size), columns] = value
            squares = squares + value * value
        return squares

    squares = lax.fori_loop(
        0,
        vocab // 8,
        lambda t, so_far: so_far + finish(pl.multiple_of(t * 8, 8), 8, t * 64),
        jnp.zeros((8, LANES), f32),
    )
    sq_ref[...] = squares
    if vocab % 8:
        at = vocab // 8 * 8
        sq_ref[0 : vocab % 8, :] += finish(at, vocab % 8, at * 8)


def spread_rows(lists, sources, vocab, width, total=None, head=None):
    groups = width // LANES
    length = sources[0].shape[1]
    total_rows = -(-vocab * 8 // 64) * 64
    first, last = total is None, head is not None
    smem = pl.BlockSpec(memory_space=pltpu.SMEM)
    vmem = pl.BlockSpec(memory_space=pltpu.VMEM)
    hbm = pl.BlockSpec(memory_space=pl.ANY)
    scratch = [
        pltpu.VMEM((length + 8, LANES), f32),
        pltpu.VMEM((2, length, LANES), bf16),
        pltpu.SemaphoreType.DMA((2,)),
    ]
    extra_specs, extra = ([], []) if first else ([hbm], [total])
    scratch.append(pltpu.SemaphoreType.DMA)
    if last:
        extra_specs, extra = extra_specs + [vmem], extra + [head]
        out_specs = [vmem, vmem]
        out_shape = [
            jax.ShapeDtypeStruct((vocab, width), f32),
            jax.ShapeDtypeStruct((8, LANES), f32),
        ]
        scratch = [pltpu.VMEM((total_rows, LANES), f32)] + scratch
    else:
        out_specs = vmem
        out_shape = jax.ShapeDtypeStruct((total_rows, LANES), f32)
    entries = sum(source.shape[0] for source in sources) * lists[1].shape[1] // 2
    return pl.pallas_call(
        functools.partial(
            spread_kernel,
            groups=groups,
            arrays=len(sources),
            first=first,
            last=last,
        ),
        in_specs=[smem] * 4 + [hbm] * len(sources) + extra_specs,
        out_specs=out_specs,
        out_shape=out_shape,
        scratch_shapes=scratch,
        compiler_params=pltpu.CompilerParams(vmem_limit_bytes=60 * 2**20),
        cost_estimate=pl.CostEstimate(
            flops=entries * 2048, bytes_accessed=entries * 10240, transcendentals=0
        ),
    )(*lists, *sources, *extra)


def local(
    noise_owner,
    noise_offset,
    option_scores,
    seq_lengths,
    time_index,
    loss_pick,
    loss_target,
    vocab_table,
    table_mom,
    table_sq,
    attn_proj,
    proj_mom,
    proj_sq,
    out_proj,
    outp_mom,
    outp_sq,
    up_proj,
    up_mom,
    up_sq,
    down_proj,
    down_mom,
    down_sq,
    time_proj,
    time_mom,
    time_sq,
    mod_proj,
    mod_mom,
    mod_sq,
    final_proj,
    final_mom,
    final_sq,
    norm_gains,
    gains_mom,
    gains_sq,
):
    devices = lax.axis_size(BOTH)
    reps = lax.axis_size("rep")
    n_dp = lax.axis_size("dp")
    lines = n_dp // PLANE
    dp_idx = lax.axis_index("dp")
    rep_idx = lax.axis_index("rep")
    me = dp_idx * reps + rep_idx
    line = dp_idx // PLANE
    chip = dp_idx % PLANE
    _, half, cands = noise_offset.shape
    vocab, width = vocab_table.shape
    heads = width // HD
    groups = width // LANES
    swaps = [(dq, dr) for dq in range(PLANE) for dr in range(reps)]

    def gather(value, axis=0):
        return lax.all_gather(value.astype(bf16), BOTH, axis=axis, tiled=True)

    few = mod_proj.shape[0]
    gains_flat = norm_gains.reshape(-1)
    gains_flat = jnp.pad(gains_flat, (0, few * LANES - gains_flat.size))
    small_all = gather(
        jnp.concatenate(
            [mod_proj, final_proj, time_proj.reshape(few, -1), gains_flat.reshape(few, LANES)], 1
        )
    )
    wide_all = gather(jnp.concatenate([attn_proj, out_proj, up_proj], 1))
    down_w = gather(down_proj)
    qkv_w = wide_all[:, : 3 * width]
    out_w = wide_all[:, 3 * width : 4 * width]
    up_w = wide_all[:, 4 * width :]

    padded = -(-vocab // 16) * 16
    table_low = jnp.pad(vocab_table.astype(bf16), ((0, padded - vocab), (0, 0)))
    cut = padded // 32 * 16
    upper_rows, lower_rows = table_low[:cut], table_low[cut:]
    first, second = {0: upper_rows}, {0: lower_rows}
    for dq in (1, 2):
        first[dq] = hop(upper_rows, dq=dq)
        second[dq] = hop(lower_rows, dq=dq)

    owner = noise_owner.reshape(-1)
    offset = noise_offset.reshape(-1)
    mixing = jax.nn.softmax(option_scores.reshape(half, cands) / annealed_softness, axis=-1)
    names = (owner * padded + offset).astype(f32).reshape(-1, LANES)
    packed = jnp.concatenate([names, mixing.reshape(-1, LANES)], 0)
    on_line = jnp.stack([packed] + [hop(packed, dl=-d) for d in range(1, lines)])
    on_line, owner, offset = lax.optimization_barrier((on_line, owner, offset))
    cap = max(2, 2 * half * cands // devices)
    member = (owner[:, None] == jnp.arange(devices, dtype=jnp.int32)[None, :]).astype(jnp.int32)
    slot = jnp.sum((jnp.cumsum(member, 0) - member) * member, 1)
    flat_slot = owner * cap + slot
    first, second, flat_slot = lax.optimization_barrier((first, second, flat_slot))
    first[3] = hop(first[1], dq=2)
    second[3] = hop(second[2], dq=1)
    pieces = []
    for dq in range(PLANE):
        pieces += [first[dq], second[dq]]
        pieces += [hop(first[dq], dr=1), hop(second[dq], dr=1)]
    line_owner = on_line[:, : names.shape[0]].astype(jnp.int32)
    line_mix = on_line[:, names.shape[0] :]
    row_owner = line_owner // padded
    slot_of = (((row_owner // reps) % PLANE) ^ chip) * reps + ((row_owner % reps) ^ rep_idx)
    here = (row_owner // (reps * PLANE)) == line
    row_at = jnp.where(here, slot_of * padded + line_owner % padded, 0) * groups
    mix_here = jnp.where(here, line_mix, 0.0)
    row_at = row_at.reshape(lines, 1, half * cands)
    mix_here = mix_here.reshape(lines, 1, half * cands)
    parts = {}

    def mix_some(which):
        out = mix_rows(
            jnp.stack([row_at[d] for d in which]),
            jnp.stack([mix_here[d] for d in which]),
            pieces,
            cands,
        )
        for k, d in enumerate(which):
            parts[d] = out[k, : half * groups]

    mix_some((1, lines - 1))
    far_parts = [hop(parts[d].astype(bf16), dl=d) for d in (1, lines - 1)]
    mix_some(tuple(range(2, lines - 1)) + (0,))
    for d in range(2, lines - 1):
        far_parts.append(hop(parts[d].astype(bf16), dl=d))
    far_parts[:2], flat_slot, small_all = lax.optimization_barrier(
        (far_parts[:2], flat_slot, small_all)
    )
    entry = offset * half + jnp.arange(half * cands, dtype=jnp.int32) // cands + 1
    empty = jnp.zeros((devices * cap,), f32)
    lists = [
        empty.at[flat_slot].set(value).reshape(devices, cap)
        for value in (entry.astype(f32), mixing.reshape(-1))
    ]
    asked = jnp.concatenate(lists, 1)
    far_parts, asked = lax.optimization_barrier((far_parts, asked))
    x0 = (parts[0] + sum(far.astype(f32) for far in far_parts)).reshape(half, width)

    mod_f = small_all[:, : 6 * width].astype(f32)
    final_f = small_all[:, 6 * width : 8 * width].astype(f32)
    time_f = small_all[:, 8 * width : -LANES].astype(f32).reshape(-1, time_proj.shape[1])
    gain_f = small_all[:, -LANES:].astype(f32).reshape(devices, -1)[:, : norm_gains.size]
    gain_f = gain_f.reshape((devices,) + norm_gains.shape)
    gain_f = gain_f.transpose(1, 0, 2).reshape(norm_gains.shape[0], width)

    length = lax.dynamic_slice_in_dim(seq_lengths, dp_idx, 1)
    feats = time_features(time_index, time_f.shape[0])
    cond, silu_back = jax.vjp(jax.nn.silu, exact(feats, time_f))
    my_cond = lax.dynamic_slice_in_dim(cond, dp_idx, 1)
    mods = exact(my_cond, mod_f)
    fmods = exact(my_cond, final_f)
    sh1, sc1, g1, sh2, sc2, g2 = jnp.split(mods, 6, -1)
    fsh, fsc = jnp.split(fmods, 2, -1)

    n1, r1 = normalize(x0)
    h1b = (n1 * gain_f[0] * (1.0 + sc1) + sh1).astype(bf16)
    qkv = dense(h1b, qkv_w)
    places = jnp.arange(half, dtype=jnp.int32)
    turns = []
    for core in (rep_idx, 1 - rep_idx):
        cosv, sinv = rope_tables(core * half + places, HD)
        turns += [jnp.tile(cosv, (1, 4)), jnp.concatenate([-sinv, sinv] * 2, 1)]
    query, keyed, valued = turn_rows(qkv, turns[0], turns[1])
    attended = (query, keyed, hop(keyed, dr=1), valued, hop(valued, dr=1))
    core = rep_idx.reshape(1)
    mixed_b, lse_att = attend(length, core, *attended)
    mixed_b, h1_far = lax.optimization_barrier((mixed_b, hop(h1b, dr=1)))
    attn = dense(mixed_b, out_w)
    x1 = x0 + g1 * attn
    n2, r2 = normalize(x1)
    h2b = (n2 * gain_f[1] * (1.0 + sc2) + sh2).astype(bf16)
    upper = dense(h2b, up_w)
    act, gelu_back = jax.vjp(lambda u: jax.nn.gelu(u, approximate=True), upper)
    act_b = act.astype(bf16)
    act_b, mixed_far, h2_far = lax.optimization_barrier(
        (act_b, hop(mixed_b, dr=1), hop(h2b, dr=1))
    )
    mlp = dense(act_b, down_w)
    x2 = x1 + g2 * mlp
    nf, rf = normalize(x2)
    final = nf * gain_f[2] * (1.0 + fsc) + fsh

    picks = loss_pick.shape[-1]
    tau = (time_index.astype(f32) + 1.0) / TSTEPS
    starts = (jnp.arange(reps, dtype=jnp.int32) * half)[None, :, None]
    weight_all = jnp.where(
        loss_pick + starts < seq_lengths[:, None, None], (1.0 / (0.1 + tau))[:, None, None], 0.0
    )
    coefficient_aggregate = jnp.sum(weight_all)

    def of_line(values, at_chip, at_core):
        mine = lax.dynamic_slice(
            values.reshape(lines, PLANE, reps, picks), (0, at_chip, at_core, 0), (lines, 1, 1, picks)
        )
        return from_me(mine.reshape(lines, picks))

    def from_me(values):
        return lax.dynamic_slice_in_dim(jnp.concatenate([values, values], 0), line, lines)

    def from_start(values):
        return lax.dynamic_slice_in_dim(
            jnp.concatenate([values, values], 0), (lines - line) % lines, lines
        )

    targets = of_line(loss_target, chip, rep_idx).reshape(-1)
    weight = of_line(weight_all, chip, rep_idx).reshape(-1)
    my_pick = lax.dynamic_slice(loss_pick, (dp_idx, rep_idx, 0), (1, 1, picks)).reshape(picks)
    spread = (jnp.arange(half, dtype=jnp.int32)[:, None] == my_pick[None, :]).astype(f32)
    rows_b = jnp.take(final, my_pick, axis=0).astype(bf16)
    every = jnp.concatenate([rows_b] + [hop(rows_b, dl=-d) for d in range(1, lines)], 0)
    asked = lax.all_to_all(asked, BOTH, split_axis=0, concat_axis=0, tiled=True)
    every, act_far, asked = lax.optimization_barrier((every, hop(act_b, dr=1), asked))
    asked, asked_mix = asked[:, :cap].astype(jnp.int32), asked[:, cap:]
    plane_table = jnp.concatenate(pieces, 0)
    logits = dense_nt(every, plane_table)
    column = jnp.arange(plane_table.shape[0], dtype=jnp.int32)
    exists = (column % padded) < vocab
    t_owner = targets // vocab
    t_slot = (((t_owner // reps) % PLANE) ^ chip) * reps + ((t_owner % reps) ^ rep_idx)
    t_column = jnp.where(
        t_owner // (reps * PLANE) == line, t_slot * padded + targets % vocab, -1
    )
    hit = column[None, :] == t_column[:, None]
    logits = jnp.where(exists[None, :], logits, -1e30)
    top = jnp.max(logits, -1)
    sums = jnp.sum(jnp.exp(logits - top[:, None]), -1)
    tgt = jnp.sum(jnp.where(hit, logits, 0.0), -1)
    stats = from_start(
        jnp.stack([value.reshape(lines, picks) for value in (top, sums, tgt)], 1)
    )
    stats_all = jnp.stack([stats] + [hop(stats, dl=-d) for d in range(1, lines)])
    tops = stats_all[:, :, 0]
    best = jnp.max(tops, 0)
    sum_all = jnp.sum(stats_all[:, :, 1] * jnp.exp(tops - best), 0)
    lse_line = best + jnp.log(sum_all)
    tgt_line = jnp.sum(stats_all[:, :, 2], 0)
    loss_here = jnp.sum(from_start(weight.reshape(lines, picks)) * (lse_line - tgt_line))
    loss_here = jnp.where(line == 0, loss_here, 0.0)
    lse = from_me(lse_line).reshape(-1)
    probs = jnp.exp(logits - lse[:, None])
    dlogit = ((weight / coefficient_aggregate)[:, None] * (probs - hit.astype(f32))).astype(bf16)
    drows_part = dense(dlogit, plane_table).reshape(lines, picks, width)
    drows = drows_part[0]
    for d in range(1, lines):
        drows = drows + hop(drows_part[d], dl=d)
    every, lse, drows = lax.optimization_barrier((every, lse, drows))
    pieces_of_lse = []
    for _ in range(3):
        rounded = lax.reduce_precision(lse, 8, 7)
        pieces_of_lse.append(rounded.astype(bf16))
        lse = lse - rounded
    extra = jnp.pad(jnp.stack(pieces_of_lse, 1), ((0, 0), (0, LANES - 3)))
    told = jnp.concatenate([every, extra], 1)
    told_x, told_y = hop(told, dq=1), hop(told, dq=2)
    told = jnp.stack([told, told_x, told_y, hop(told_x, dq=2)])
    told = jnp.concatenate([told, hop(told, dr=1)], 0).reshape(-1, width + LANES)
    among = [(chip ^ dq, rep_idx ^ dr) for dr in range(reps) for dq in range(PLANE)]
    targets_all = jnp.concatenate([of_line(loss_target, q, r).reshape(-1) for q, r in among])
    weight_rows = jnp.concatenate([of_line(weight_all, q, r).reshape(-1) for q, r in among])

    grad_final = exact(spread, drows)
    dx2, dfsh, dfsc, dgain_f = modulate_back(grad_final, nf, rf, gain_f[2], fsc)
    dg2 = jnp.sum(dx2 * mlp, 0)
    dmlp = (dx2 * g2).astype(bf16)
    g_down = chip_product(act_b, act_far, dmlp)
    dupper = gelu_back(dense_nt(dmlp, down_w))[0].astype(bf16)
    g_up = chip_product(h2b, h2_far, dupper)
    dh2 = dense_nt(dupper, up_w)
    dn2x, dsh2, dsc2, dgain_2 = modulate_back(dh2, n2, r2, gain_f[1], sc2)
    dx1 = dx2 + dn2x
    dg1 = jnp.sum(dx1 * attn, 0)
    dattn = (dx1 * g1).astype(bf16)
    dattn, g_down, g_up = lax.optimization_barrier((dattn, g_down, g_up))
    down_1 = split_blocks(plane_blocks(g_down), 1, 1)
    up_1 = split_blocks(plane_blocks(g_up), 0, 2)
    g_out = chip_product(mixed_b, mixed_far, dattn)
    dmixed = dense_nt(dattn, out_w).astype(bf16)
    dquery, dkey, dkey_far, dvalue, dvalue_far = attend_back(
        length, core, *attended, lse_att, dmixed, *turns
    )
    dquery, dkey, dkey_far, dvalue, dvalue_far, down_1, up_1, g_out = lax.optimization_barrier(
        (dquery, dkey, dkey_far, dvalue, dvalue_far, down_1, up_1, g_out)
    )
    down_2 = split_blocks(down_1[0] + down_1[1].astype(f32), 0, 1)
    up_2 = split_blocks(up_1[0] + up_1[1].astype(f32), 1, 1)
    dkey = (dkey + hop(dkey_far, dr=1).astype(f32)).astype(bf16)
    dvalue = (dvalue + hop(dvalue_far, dr=1).astype(f32)).astype(bf16)
    dqkv = jnp.concatenate([dquery, dkey, dvalue], 1)
    dh1 = dense_nt(dqkv, qkv_w)
    dn1x, dsh1, dsc1, dgain_1 = modulate_back(dh1, n1, r1, gain_f[0], sc1)
    dx0 = dx1 + dn1x
    g_qkv = chip_product(h1b, h1_far, dqkv)


    dx0_b = dx0.astype(bf16).reshape(1, half * groups, LANES)
    dx0_b, down_2, up_2 = lax.optimization_barrier((dx0_b, down_2, up_2))
    others = lines - 1
    cut = -(-2 * others // 3)
    sums_here = jnp.concatenate(
        [dsh1, dsc1, dg1, dsh2, dsc2, dg2, dfsh, dfsc, dgain_1, dgain_2, dgain_f]
    )
    on_line = gather_line(dx0_b)
    own_x, own_y = hop(dx0_b, dq=1), hop(dx0_b, dq=2)
    own_xy = hop(own_y, dq=1)
    g_last = jnp.concatenate([g_qkv, g_out], 1)
    last_1 = split_blocks(plane_blocks(g_last), 1, 1)
    sums_all = lax.all_gather(sums_here.reshape(1, -1, LANES), BOTH, axis=0, tiled=True)
    last_2 = split_blocks(last_1[0] + last_1[1].astype(f32), 0, 1)
    on_line, own_x, own_y, own_xy, last_2, told, sums_all = lax.optimization_barrier(
        (on_line, own_x, own_y, own_xy, last_2, told, sums_all)
    )
    rows_all = told[:, :width]
    lse_all = jnp.sum(told[:, width : width + 3].astype(f32), 1)
    line_x, line_y = hop(on_line, dq=1), hop(on_line, dq=2)
    shards = [two[0] + two[1].astype(f32) for two in (down_2, up_2, last_2)]
    both = shards[1].shape[1]
    tall = shards[0].shape[1] // both
    pile = shards[0].reshape(lines, tall, both, -1)
    blocks = jnp.concatenate([pile[:, k] for k in range(tall)] + shards[1:], 2)
    sums = reduce_step(blocks, None, lines - 1)
    early = [(dx0_b, 0, 0), (own_x, 1, 0), (own_y, 2, 0), (own_xy, 3, 0), (on_line, 0, 1)]
    order = []

    def from_cores(gathered):
        sources = []
        for value, dq, first_d in gathered:
            sources.extend(add_source(value, dq, first_d))
        return sources

    def add_source(value, dq, first_d):
        for dr in range(reps):
            for d in range(first_d, first_d + value.shape[0]):
                order.append(
                    (((line + d) % lines) * PLANE + (chip ^ dq)) * reps + (rep_idx ^ dr)
                )
        return [value, hop(value, dr=1)]

    def lists_of(order):
        order = jnp.stack(order)
        entries = jnp.take(asked, order, axis=0)
        count = jnp.sum((entries > 0).astype(jnp.int32), 1)
        entries = jnp.maximum(entries - 1, 0)
        return (
            count,
            entries // half,
            (entries % half) * groups,
            jnp.take(asked_mix, order, axis=0),
        )

    sources = from_cores(early)
    begun = spread_rows(lists_of(order), sources, vocab, width)
    order.clear()
    logits_mine = dense_nt(rows_all, table_low)
    own_column = jnp.where(targets_all // vocab == me, targets_all % vocab, -1)
    hit_mine = jnp.arange(padded, dtype=jnp.int32)[None, :] == own_column[:, None]
    dlogit_mine = (
        (weight_rows / coefficient_aggregate)[:, None]
        * (jnp.exp(logits_mine - lse_all[:, None]) - hit_mine.astype(f32))
    ).astype(bf16)
    head_grad = dense_tn(dlogit_mine, rows_all)
    line_x, line_y, begun, head_grad, sums = lax.optimization_barrier(
        (line_x, line_y, begun, head_grad, sums)
    )
    for d in range(lines - 2, 1, -1):
        sums = reduce_step(blocks, sums, d)
    near = hop(line_x[:cut], dq=2)
    rest = [hop(line_y[cut:], dq=1)] if cut < others else []
    sources = from_cores([(line_x, 1, 1), (line_y, 2, 1)])
    begun = spread_rows(lists_of(order), sources, vocab, width, begun)
    order.clear()
    near, rest, begun, sums = lax.optimization_barrier((near, rest, begun, sums))
    sums = reduce_step(blocks, sums, 1)
    total = block_at(blocks, 0) + sums[0] + sums[1]
    down_end = tall * pile.shape[3]
    pile = jnp.stack(jnp.split(total[:, :down_end], tall, 1))
    d_down = jnp.concatenate(join_cores(pile.reshape(reps, -1, pile.shape[2])), 1)
    left, right = join_cores(total[:, down_end:].reshape(reps, both // reps, -1))
    joined = []
    at = 0
    for columns in (up_proj.shape[1], attn_proj.shape[1], out_proj.shape[1]):
        part = slice(at, at + columns // 2)
        joined.append(jnp.concatenate([left[:, part], right[:, part]], 1))
        at += columns // 2
    d_up, d_qkv, d_out = joined
    sources = from_cores([(near, 3, 1)] + [(value, 3, 1 + cut) for value in rest])
    table_grad, table_squares = spread_rows(
        lists_of(order), sources, vocab, width, begun, head_grad
    )

    sums_all = sums_all.reshape(n_dp, reps, -1).sum(1)
    dmods = sums_all[:, : 6 * width]
    dfmods = sums_all[:, 6 * width : 8 * width]

    def my_columns(value, count):
        return lax.dynamic_slice_in_dim(value, me * count, count, axis=1)

    d_mod = exact_tn(my_columns(cond, mod_proj.shape[0]), dmods)
    d_final = exact_tn(my_columns(cond, final_proj.shape[0]), dfmods)
    dcond = exact_nt(dmods, mod_f) + exact_nt(dfmods, final_f)
    d_time = exact_tn(my_columns(feats, time_proj.shape[0]), silu_back(dcond)[0])
    d_gains = my_columns(
        jnp.sum(sums_all[:, 8 * width :], 0).reshape(3, width), norm_gains.shape[1]
    )

    reduced = (d_qkv, d_out, d_up, d_down, d_time, d_mod, d_final, d_gains)
    local_sq = jnp.sum(table_squares)
    for g in reduced:
        local_sq = local_sq + jnp.sum(g * g)
    totals = add_up(jnp.stack([local_sq, loss_here]))
    grad_norm = jnp.sqrt(totals[0])
    loss_sum = totals[1]
    clip = jnp.minimum(1.0, 0.01 / (grad_norm + 1e-06))
    masters = (attn_proj, out_proj, up_proj, down_proj, time_proj, mod_proj, final_proj, norm_gains)
    coefficients = (vocab_table,) + masters
    moms = (
        table_mom,
        proj_mom,
        outp_mom,
        up_mom,
        down_mom,
        time_mom,
        mod_mom,
        final_mom,
        gains_mom,
    )
    sqs = (table_sq, proj_sq, outp_sq, up_sq, down_sq, time_sq, mod_sq, final_sq, gains_sq)
    rates = (0.02, 0.02, 0.02, 0.02, 0.02, 0.02, 0.02, 0.02, 0.1)
    grads = (table_grad,) + reduced
    result = [loss_sum, coefficient_aggregate, grad_norm]
    for weight_now, first_m, second_m, grad, rate in zip(coefficients, moms, sqs, grads, rates):
        result.extend(adamw(weight_now, first_m, second_m, clip * grad, rate))
    return tuple(result)


def solution(mesh):
    shard = P(BOTH, None)
    columns = P(None, BOTH)
    return jax.shard_map(
        local,
        mesh=mesh,
        in_specs=(P("dp", "rep", None),) * 3 + (P(),) * 4 + (shard,) * 24 + (columns,) * 3,
        out_specs=(P(),) * 3 + (shard,) * 24 + (columns,) * 3,
        check_vma=False,
    )
```

```python
import functools
import math

import jax
import jax.numpy as jnp
from jax import lax
from jax.experimental import pallas as pl
from jax.experimental.pallas import tpu as pltpu
from jax.sharding import PartitionSpec as P

HD = 64
TSTEPS = 1000
STEP = 5
PLANE = 4
LANES = 128
BOTH = ("dp", "rep")

HIGH = lax.Precision.HIGHEST
annealed_softness = 0.5
bf16 = jnp.bfloat16
f32 = jnp.float32


def dense(a, b):
    return jnp.dot(a, b, preferred_element_type=f32)


def dense_nt(a, b):
    return lax.dot_general(a, b, (((1,), (1,)), ((), ())), preferred_element_type=f32)


def dense_tn(a, b):
    return lax.dot_general(a, b, (((0,), (0,)), ((), ())), preferred_element_type=f32)


def exact(a, b):
    return jnp.dot(a, b, precision=HIGH, preferred_element_type=f32)


def exact_nt(a, b):
    return lax.dot_general(
        a, b, (((1,), (1,)), ((), ())), precision=HIGH, preferred_element_type=f32
    )


def exact_tn(a, b):
    return lax.dot_general(
        a, b, (((0,), (0,)), ((), ())), precision=HIGH, preferred_element_type=f32
    )


def normalize(x):
    center = x - jnp.mean(x, -1, keepdims=True)
    rstd = lax.rsqrt(jnp.mean(center * center, -1, keepdims=True) + 1e-06)
    return (center * rstd, rstd)


def modulate_back(grad_h, normed, rstd, gain, scale):
    dshift = jnp.sum(grad_h, 0)
    weighted = grad_h * normed
    column = jnp.sum(weighted, 0)
    dscale = column * gain
    dgain = column * (1.0 + scale[0])
    grad_n = grad_h * gain * (1.0 + scale)
    grad_x = rstd * (
        grad_n
        - jnp.mean(grad_n, -1, keepdims=True)
        - normed * jnp.mean(grad_n * normed, -1, keepdims=True)
    )
    return (grad_x, dshift, dscale, dgain)


def rope_tables(pos, head):
    half = head // 2
    freqs = jnp.exp(-math.log(10000.0) * jnp.arange(half, dtype=f32) / half)
    angle = pos.astype(f32)[:, None] * freqs[None, :]
    return (jnp.cos(angle), jnp.sin(angle))


def time_features(steps, width):
    tau = (steps.astype(f32) + 1.0) / TSTEPS
    half = width // 2
    freqs = jnp.exp(-math.log(10000.0) * jnp.arange(half, dtype=f32) / half)
    angle = 1000.0 * tau[:, None] * freqs[None, :]
    return jnp.concatenate([jnp.cos(angle), jnp.sin(angle)], -1)


def turn(x, cosv, sinv):
    lane = lax.broadcasted_iota(jnp.int32, x.shape, 1)
    quarter = HD // 2
    swapped = jnp.where(
        lane % HD < quarter,
        pltpu.roll(x, LANES - quarter, axis=1),
        pltpu.roll(x, quarter, axis=1),
    )
    return x * cosv + swapped * sinv


def turn_kernel(q_ref, k_ref, v_ref, cos_ref, sin_ref, q_out, k_out, v_out):
    cosv, sinv = cos_ref[...], sin_ref[...]
    for start in range(0, q_ref.shape[1], LANES):
        at = slice(start, start + LANES)
        q_out[:, at] = turn(q_ref[:, at], cosv, sinv).astype(bf16)
        k_out[:, at] = turn(k_ref[:, at], cosv, sinv).astype(bf16)
    v_out[...] = v_ref[...].astype(bf16)


def turn_rows(qkv, cosv, sinv):
    rows, width = qkv.shape[0], qkv.shape[1] // 3
    wide = 3 * LANES if width % (3 * LANES) == 0 else LANES
    blocks = width // wide
    block = lambda shift: pl.BlockSpec((rows, wide), lambda i: (0, i + shift))
    whole = pl.BlockSpec((rows, LANES), lambda i: (0, 0))
    return pl.pallas_call(
        turn_kernel,
        grid=(blocks,),
        in_specs=[block(0), block(blocks), block(2 * blocks), whole, whole],
        out_specs=[block(0)] * 3,
        out_shape=[jax.ShapeDtypeStruct((rows, width), bf16)] * 3,
        cost_estimate=pl.CostEstimate(
            flops=rows * width * 12, bytes_accessed=rows * width * 18, transcendentals=0
        ),
    )(qkv, qkv, qkv, cosv, sinv)


def key_masks(len_ref, core_ref, keys):
    place = lax.broadcasted_iota(jnp.int32, (1, keys), 1)
    own = place + core_ref[0] * keys
    far = place + (1 - core_ref[0]) * keys
    return [jnp.where(at < len_ref[0], 0.0, -1e30).astype(f32) for at in (own, far)]


def attend_kernel(len_ref, core_ref, q_ref, k_ref, kf_ref, v_ref, vf_ref, *refs, tile):
    out_ref, lse_ref = refs[-2:]
    rows = q_ref.shape[0]
    masks = key_masks(len_ref, core_ref, rows)
    keyed = (k_ref[...], kf_ref[...])
    valued = (v_ref[...], vf_ref[...])
    lane = lax.broadcasted_iota(jnp.int32, (tile, LANES), 1)
    for t in range(rows // tile):
        at = pl.ds(t * tile, tile)
        query = q_ref[at, :] * bf16(HD**-0.5)
        mixed, lses = [], []
        for head in range(LANES // HD):
            mine = jnp.where(lane // HD == head, query, bf16(0))
            scores = [dense_nt(mine, k) + mask for k, mask in zip(keyed, masks)]
            top = jnp.maximum(*[jnp.max(s, 1, keepdims=True) for s in scores])
            expo = [jnp.exp(s - top) for s in scores]
            total = sum(jnp.sum(e, 1, keepdims=True) for e in expo)
            inverse = 1.0 / total
            mixed.append(sum(dense((e * inverse).astype(bf16), v) for e, v in zip(expo, valued)))
            lses.append(top + jnp.log(total))
        out_ref[at, :] = jnp.where(lane < HD, mixed[0], mixed[1]).astype(bf16)
        lse_ref[at, :] = jnp.where(lane < HD, lses[0], lses[1])


def attend(length, core, query, keyed, keyed_far, valued, valued_far, ready=()):
    rows, width = query.shape
    smem = pl.BlockSpec(memory_space=pltpu.SMEM)
    block = pl.BlockSpec((rows, LANES), lambda i: (0, i))
    return pl.pallas_call(
        functools.partial(attend_kernel, tile=256),
        grid=(width // LANES,),
        in_specs=[smem, smem] + [block] * 5 + [pl.BlockSpec(memory_space=pl.ANY)] * len(ready),
        out_specs=[block, block],
        out_shape=[
            jax.ShapeDtypeStruct((rows, width), bf16),
            jax.ShapeDtypeStruct((rows, width), f32),
        ],
        compiler_params=pltpu.CompilerParams(vmem_limit_bytes=48 * 2**20),
        cost_estimate=pl.CostEstimate(
            flops=8 * rows * rows * width, bytes_accessed=rows * width * 18,
            transcendentals=2 * rows * rows * width // HD,
        ),
    )(length, core, query, keyed, keyed_far, valued, valued_far, *ready)


def attend_back_kernel(
    len_ref,
    core_ref,
    q_ref,
    k_ref,
    kf_ref,
    v_ref,
    vf_ref,
    lse_ref,
    do_ref,
    cos_ref,
    sin_ref,
    cos_far_ref,
    sin_far_ref,
    *refs,
    tile,
):
    dq_ref, dk_ref, dkf_ref, dv_ref, dvf_ref = refs[-5:]
    rows = q_ref.shape[0]
    masks = key_masks(len_ref, core_ref, rows)
    keyed = (k_ref[...], kf_ref[...])
    valued = (v_ref[...], vf_ref[...])
    lane = lax.broadcasted_iota(jnp.int32, (tile, LANES), 1)
    first = lax.broadcasted_iota(jnp.int32, (rows, LANES), 1) < HD
    dk, dv = [None, None], [None, None]
    for t in range(rows // tile):
        at = pl.ds(t * tile, tile)
        query = q_ref[at, :] * bf16(HD**-0.5)
        grad = do_ref[at, :]
        dqs, dks, dvs = [], [[], []], [[], []]
        for head in range(LANES // HD):
            mine = lane // HD == head
            q_mine = jnp.where(mine, query, bf16(0))
            g_mine = jnp.where(mine, grad, bf16(0))
            lse = lse_ref[at, head * HD : head * HD + 1]
            probs = [jnp.exp(dense_nt(q_mine, k) + mask - lse) for k, mask in zip(keyed, masks)]
            grad_p = [dense_nt(g_mine, v) for v in valued]
            delta = sum(jnp.sum(p * g, 1, keepdims=True) for p, g in zip(probs, grad_p))
            grad_s = [(p * (g - delta)).astype(bf16) for p, g in zip(probs, grad_p)]
            dqs.append(sum(dense(s, k) for s, k in zip(grad_s, keyed)))
            for side in range(2):
                dks[side].append(dense_tn(grad_s[side], query))
                dvs[side].append(dense_tn(probs[side].astype(bf16), grad))
        turned = turn(jnp.where(lane < HD, dqs[0], dqs[1]), cos_ref[at, :], -sin_ref[at, :])
        dq_ref[at, :] = (turned * HD**-0.5).astype(bf16)
        for side in range(2):
            part_k = jnp.where(first, *dks[side])
            part_v = jnp.where(first, *dvs[side])
            dk[side] = part_k if t == 0 else dk[side] + part_k
            dv[side] = part_v if t == 0 else dv[side] + part_v
    dk_ref[...] = turn(dk[0], cos_ref[...], -sin_ref[...])
    dkf_ref[...] = turn(dk[1], cos_far_ref[...], -sin_far_ref[...]).astype(bf16)
    dv_ref[...] = dv[0]
    dvf_ref[...] = dv[1].astype(bf16)


def attend_back(length, core, *arrays, ready=()):
    query = arrays[0]
    rows, width = query.shape
    smem = pl.BlockSpec(memory_space=pltpu.SMEM)
    block = pl.BlockSpec((rows, LANES), lambda i: (0, i))
    return pl.pallas_call(
        functools.partial(attend_back_kernel, tile=256),
        grid=(width // LANES,),
        in_specs=[smem, smem]
        + [block] * 7
        + [pl.BlockSpec((rows, LANES), lambda i: (0, 0))] * 4
        + [pl.BlockSpec(memory_space=pl.ANY)] * len(ready),
        out_specs=[block] * 5,
        out_shape=[jax.ShapeDtypeStruct((rows, width), t) for t in (bf16, f32, bf16, f32, bf16)],
        compiler_params=pltpu.CompilerParams(vmem_limit_bytes=48 * 2**20),
        cost_estimate=pl.CostEstimate(
            flops=20 * rows * rows * width, bytes_accessed=rows * width * 32,
            transcendentals=2 * rows * rows * width // HD,
        ),
    )(length, core, *arrays, *ready)
def adamw(weight, first, second, grad, rate):
    first = 0.9 * first + 0.1 * grad
    second = 0.999 * second + 0.001 * grad * grad
    step = first / (1.0 - 0.9**STEP) / (jnp.sqrt(second / (1.0 - 0.999**STEP)) + 1e-08)
    return (weight - rate * (step + 0.01 * weight), first, second)


def adamw_kernel(clip_ref, *refs, rates):
    n = len(rates)
    for k, rate in enumerate(rates):
        weight, first, second, grad = [ref[...] for ref in refs[4 * k : 4 * k + 4]]
        outs = refs[4 * n + 3 * k : 4 * n + 3 * k + 3]
        for out, value in zip(outs, adamw(weight, first, second, clip_ref[0] * grad, rate)):
            out[...] = value


def adamw_all(clip, quads, rates):
    vmem = pl.BlockSpec(memory_space=pltpu.VMEM)
    flat = [value for quad in quads for value in quad]
    shapes = [jax.ShapeDtypeStruct(quad[0].shape, f32) for quad in quads for _ in range(3)]
    return pl.pallas_call(
        functools.partial(adamw_kernel, rates=rates),
        in_specs=[pl.BlockSpec(memory_space=pltpu.SMEM)] + [vmem] * len(flat),
        out_specs=[vmem] * len(shapes),
        out_shape=shapes,
        compiler_params=pltpu.CompilerParams(vmem_limit_bytes=48 * 2**20),
    )(clip.reshape(1), *flat)


def hop(x, dl=0, dq=0, dr=0):
    reps = lax.axis_size("rep")
    lines = lax.axis_size("dp") // PLANE
    pairs = []
    for l in range(lines):
        for q in range(PLANE):
            for r in range(reps):
                to = (((l + dl) % lines) * PLANE + (q ^ dq)) * reps + (r ^ dr)
                pairs.append(((l * PLANE + q) * reps + r, to))
    return lax.ppermute(x, BOTH, pairs)


def step_line(x, way, reach):
    lines = lax.axis_size("dp") // PLANE
    pairs = []
    for l in range(lines):
        if 0 <= l + way * reach < lines:
            for q in range(PLANE):
                pairs.append((l * PLANE + q, (l + way) * PLANE + q))
    return lax.ppermute(x, "dp", pairs)


def pick_half(value, index):
    size = value.shape[1] // 2
    return lax.dynamic_slice_in_dim(value, index * size, size, axis=1)


def chip_product(left, left_far, right):
    rep_idx = lax.axis_index("rep")
    far = hop(pick_half(right, 1 - rep_idx), dr=1)
    return dense_tn(left, pick_half(right, rep_idx)) + dense_tn(left_far, far)


def plane_blocks(value):
    lines = lax.axis_size("dp") // PLANE
    return value.reshape(lines, 2, 2, value.shape[0] // (lines * PLANE), -1)


def split_blocks(blocks, axis, place):
    bit = (lax.axis_index("dp") >> axis) & 1
    far = lax.dynamic_index_in_dim(blocks, 1 - bit, place, False).astype(bf16)
    return lax.dynamic_index_in_dim(blocks, bit, place, False), hop(far, dq=1 << axis)


def gather_line(value):
    lines = lax.axis_size("dp") // PLANE
    line = lax.axis_index("dp") // PLANE

    def pass_on(x, way, k):
        pairs = []
        for l in range(lines):
            if 0 <= l - way * (k - 1) < lines and 0 <= l + way < lines:
                for q in range(PLANE):
                    pairs.append((l * PLANE + q, (l + way) * PLANE + q))
        return lax.ppermute(x, "dp", pairs)

    before, after = [value], [value]
    for k in range(1, lines):
        before.append(pass_on(before[-1], 1, k))
        after.append(pass_on(after[-1], -1, k))
    return jnp.concatenate(
        [jnp.where(line + d < lines, after[d], before[lines - d]) for d in range(1, lines)], 0
    )


def block_at(blocks, shift):
    line = lax.axis_index("dp") // PLANE
    return lax.dynamic_index_in_dim(blocks, jnp.mod(line + shift, blocks.shape[0]), 0, False)


def reduce_step(blocks, sums, reach):
    to_right, to_left = block_at(blocks, reach), block_at(blocks, -reach)
    if sums is not None:
        to_right, to_left = to_right + sums[0], to_left + sums[1]
    return step_line(to_right, 1, reach), step_line(to_left, -1, reach)


def join_cores(parts):
    rep_idx = lax.axis_index("rep")
    mine = lax.dynamic_index_in_dim(parts, rep_idx, 0, False)
    far = hop(lax.dynamic_index_in_dim(parts, 1 - rep_idx, 0, False), dr=1)
    return jnp.where(rep_idx == 0, mine, far), jnp.where(rep_idx == 0, far, mine)


def add_up(value):
    lines = lax.axis_size("dp") // PLANE
    line = lax.axis_index("dp") // PLANE
    value = value + hop(value, dr=1)
    far = [hop(value, dq=dq) for dq in range(1, PLANE)]
    value = (value + far[0]) + (far[1] + far[2])
    every = jnp.stack([value] + [hop(value, dl=-d) for d in range(1, lines)])
    every = lax.dynamic_slice_in_dim(
        jnp.concatenate([every, every], 0), (lines - line) % lines, lines
    )
    return jnp.sum(every, 0)


def mix_kernel(idx_ref, mix_ref, *refs, groups, cands, counts, keep):
    n = len(counts)
    pieces, refs = refs[:n], refs[n:]
    if keep:
        out_ref, whole_ref, tab, stage, sem, keep_sem = refs
    else:
        out_ref, tab, stage, sem = refs
    slots = stage.shape[0]
    bases = [sum(counts[:j]) for j in range(n)]

    @pl.when(pl.program_id(0) == 0)
    def _():
        def slot(j):
            return stage.at[j % slots, pl.ds(0, counts[j])]

        def copy(j):
            return pltpu.make_async_copy(pieces[j], slot(j), sem.at[j % slots])

        def store(j):
            whole = whole_ref.at[pl.ds(bases[j], counts[j])]
            return pltpu.make_async_copy(slot(j), whole, keep_sem.at[j % slots])

        for j in range(min(2, n)):
            copy(j).start()
        for j in range(n):
            copy(j).wait()
            if keep:
                store(j).start()

            @pl.loop(0, counts[j] // 16)
            def _(t, j=j):
                part = stage[j % slots, pl.ds(pl.multiple_of(t * 16, 16), 16), :].astype(f32)
                for g in range(groups):
                    tab[pl.ds((bases[j] + t * 16) * groups + g, 16, stride=groups), :] = part[
                        :, g * LANES : (g + 1) * LANES
                    ]

            if keep and j >= 2:
                store(j - 2).wait()
            if j + 2 < n:
                copy(j + 2).start()
        if keep:
            for j in range(max(0, n - 2), n):
                store(j).wait()

    unroll = 4

    @pl.loop(0, idx_ref.shape[-1] // cands // unroll)
    def _(block):
        for u in range(unroll):
            p = block * unroll + u
            total = None
            for c in range(cands):
                row = tab[pl.ds(idx_ref[0, 0, p * cands + c], 8), :]
                term = row * mix_ref[0, 0, p * cands + c]
                total = term if total is None else total + term
            out_ref[0, pl.ds(p * groups, 8), :] = total


def mix_rows(idx, mix, pieces, cands, keep):
    width = pieces[0].shape[1]
    groups = width // LANES
    lines, _, entries = idx.shape
    counts = tuple(piece.shape[0] for piece in pieces)
    rows = entries // cands * groups + 8
    out_specs = [pl.BlockSpec((1, rows, LANES), lambda i: (i, 0, 0))]
    out_shape = [jax.ShapeDtypeStruct((lines, rows, LANES), f32)]
    slots = 4
    scratch = [
        pltpu.VMEM((sum(counts) * groups + 8, LANES), f32),
        pltpu.VMEM((slots, max(counts), width), bf16),
        pltpu.SemaphoreType.DMA((slots,)),
    ]
    if keep:
        out_specs.append(pl.BlockSpec(memory_space=pl.ANY))
        out_shape.append(jax.ShapeDtypeStruct((sum(counts), width), bf16))
        scratch.append(pltpu.SemaphoreType.DMA((slots,)))
    return pl.pallas_call(
        functools.partial(mix_kernel, groups=groups, cands=cands, counts=counts, keep=keep),
        grid=(lines,),
        in_specs=[pl.BlockSpec((1, 1, entries), lambda i: (i, 0, 0), memory_space=pltpu.SMEM)] * 2
        + [pl.BlockSpec(memory_space=pl.ANY)] * len(pieces),
        out_specs=out_specs,
        out_shape=out_shape,
        scratch_shapes=scratch,
        compiler_params=pltpu.CompilerParams(vmem_limit_bytes=60 * 2**20),
        cost_estimate=pl.CostEstimate(
            flops=lines * entries * 2048, bytes_accessed=40 * 2**20, transcendentals=0
        ),
    )(idx, mix, *pieces)


def spread_kernel(cnt_ref, row_ref, pos_ref, mix_ref, *refs, groups, arrays, first, last):
    sources = refs[:arrays]
    refs = list(refs[arrays:])
    total_in = None if first else refs.pop(0)
    if last:
        head_ref, out_ref, sq_ref = refs[:3]
        refs = refs[3:]
    total, rows32, stage, sem, total_sem = refs
    length = sources[0].shape[1]
    blocks = [source.at[k] for source in sources for k in range(source.shape[0])]
    n = len(blocks)

    def copy(k):
        return pltpu.make_async_copy(blocks[k], stage.at[k % 2], sem.at[k % 2])

    copy(0).start()
    if not first:
        load = pltpu.make_async_copy(total_in, total, total_sem)
        load.start()
        load.wait()
    else:

        @pl.loop(0, total.shape[0] // 64)
        def _(t):
            total[pl.ds(pl.multiple_of(t * 64, 64), 64), :] = jnp.zeros((64, LANES), f32)

    unroll = 4
    for k in range(n):
        if k + 1 < n:
            copy(k + 1).start()
        copy(k).wait()

        @pl.loop(0, length // 64)
        def _(t, k=k):
            at = pl.multiple_of(t * 64, 64)
            rows32[pl.ds(at, 64), :] = stage[k % 2, pl.ds(at, 64), :].astype(f32)

        @pl.loop(0, (cnt_ref[k] + unroll - 1) // unroll)
        def _(block, k=k):
            for u in range(unroll):
                e = block * unroll + u
                at = pl.ds(pl.multiple_of(row_ref[k, e] * 8, 8), 8)
                term = mix_ref[k, e] * rows32[pl.ds(pos_ref[k, e], 8), :]
                total[at, :] = total[at, :] + term

    if not last:
        return
    vocab = out_ref.shape[0]

    def finish(at, size, start):
        squares = jnp.zeros((size, LANES), f32)
        for g in range(groups):
            columns = slice(g * LANES, (g + 1) * LANES)
            value = head_ref[pl.ds(at, size), columns] + total[pl.ds(start + g, size, stride=8), :]
            out_ref[pl.ds(at, size), columns] = value
            squares = squares + value * value
        return squares

    squares = lax.fori_loop(
        0,
        vocab // 8,
        lambda t, so_far: so_far + finish(pl.multiple_of(t * 8, 8), 8, t * 64),
        jnp.zeros((8, LANES), f32),
    )
    sq_ref[...] = squares
    if vocab % 8:
        at = vocab // 8 * 8
        sq_ref[0 : vocab % 8, :] += finish(at, vocab % 8, at * 8)


def spread_rows(lists, sources, vocab, width, total=None, head=None):
    groups = width // LANES
    length = sources[0].shape[1]
    total_rows = -(-vocab * 8 // 64) * 64
    first, last = total is None, head is not None
    smem = pl.BlockSpec(memory_space=pltpu.SMEM)
    vmem = pl.BlockSpec(memory_space=pltpu.VMEM)
    hbm = pl.BlockSpec(memory_space=pl.ANY)
    scratch = [
        pltpu.VMEM((length + 8, LANES), f32),
        pltpu.VMEM((2, length, LANES), bf16),
        pltpu.SemaphoreType.DMA((2,)),
    ]
    extra_specs, extra = ([], []) if first else ([hbm], [total])
    scratch.append(pltpu.SemaphoreType.DMA)
    if last:
        extra_specs, extra = extra_specs + [vmem], extra + [head]
        out_specs = [vmem, vmem]
        out_shape = [
            jax.ShapeDtypeStruct((vocab, width), f32),
            jax.ShapeDtypeStruct((8, LANES), f32),
        ]
        scratch = [pltpu.VMEM((total_rows, LANES), f32)] + scratch
    else:
        out_specs = vmem
        out_shape = jax.ShapeDtypeStruct((total_rows, LANES), f32)
    entries = sum(source.shape[0] for source in sources) * lists[1].shape[1] // 2
    return pl.pallas_call(
        functools.partial(
            spread_kernel,
            groups=groups,
            arrays=len(sources),
            first=first,
            last=last,
        ),
        in_specs=[smem] * 4 + [hbm] * len(sources) + extra_specs,
        out_specs=out_specs,
        out_shape=out_shape,
        scratch_shapes=scratch,
        compiler_params=pltpu.CompilerParams(vmem_limit_bytes=60 * 2**20),
        cost_estimate=pl.CostEstimate(
            flops=entries * 2048, bytes_accessed=entries * 10240, transcendentals=0
        ),
    )(*lists, *sources, *extra)


def local(
    noise_owner,
    noise_offset,
    option_scores,
    seq_lengths,
    time_index,
    loss_pick,
    loss_target,
    vocab_table,
    table_mom,
    table_sq,
    attn_proj,
    proj_mom,
    proj_sq,
    out_proj,
    outp_mom,
    outp_sq,
    up_proj,
    up_mom,
    up_sq,
    down_proj,
    down_mom,
    down_sq,
    time_proj,
    time_mom,
    time_sq,
    mod_proj,
    mod_mom,
    mod_sq,
    final_proj,
    final_mom,
    final_sq,
    norm_gains,
    gains_mom,
    gains_sq,
):
    devices = lax.axis_size(BOTH)
    reps = lax.axis_size("rep")
    n_dp = lax.axis_size("dp")
    lines = n_dp // PLANE
    dp_idx = lax.axis_index("dp")
    rep_idx = lax.axis_index("rep")
    me = dp_idx * reps + rep_idx
    line = dp_idx // PLANE
    chip = dp_idx % PLANE
    _, half, cands = noise_offset.shape
    vocab, width = vocab_table.shape
    heads = width // HD
    groups = width // LANES
    swaps = [(dq, dr) for dq in range(PLANE) for dr in range(reps)]

    def from_me(values):
        return lax.dynamic_slice_in_dim(jnp.concatenate([values, values], 0), line, lines)

    def gather(value, axis=0):
        return lax.all_gather(value.astype(bf16), BOTH, axis=axis, tiled=True)

    few = mod_proj.shape[0]
    gains_flat = norm_gains.reshape(-1)
    gains_flat = jnp.pad(gains_flat, (0, few * LANES - gains_flat.size))
    small_all = gather(
        jnp.concatenate(
            [mod_proj, final_proj, time_proj.reshape(few, -1), gains_flat.reshape(few, LANES)], 1
        )
    )
    qkv_w = gather(attn_proj)

    padded = -(-vocab // 16) * 16
    table_low = jnp.pad(vocab_table.astype(bf16), ((0, padded - vocab), (0, 0)))
    cut = padded // 32 * 16
    upper_rows, lower_rows = table_low[:cut], table_low[cut:]
    first, second = {0: upper_rows}, {0: lower_rows}
    for dq in (1, 2):
        first[dq] = hop(upper_rows, dq=dq)
        second[dq] = hop(lower_rows, dq=dq)

    owner = noise_owner.reshape(-1)
    offset = noise_offset.reshape(-1)
    mixing = jax.nn.softmax(option_scores.reshape(half, cands) / annealed_softness, axis=-1)
    names = (owner * padded + offset).astype(f32).reshape(-1, LANES)
    packed = jnp.concatenate([names, mixing.reshape(-1, LANES)], 0)
    groups_of_line = [[l * PLANE + q for l in range(lines)] for q in range(PLANE)]
    on_line = lax.all_gather(packed, "dp", axis_index_groups=groups_of_line)
    cap = max(2, 2 * half * cands // devices)
    member = (owner[:, None] == jnp.arange(devices, dtype=jnp.int32)[None, :]).astype(jnp.int32)
    slot = jnp.sum((jnp.cumsum(member, 0) - member) * member, 1)
    flat_slot = owner * cap + slot
    first, second, flat_slot = lax.optimization_barrier((first, second, flat_slot))
    first[3] = hop(first[1], dq=2)
    second[3] = hop(second[2], dq=1)
    pieces = []
    for dq in range(PLANE):
        pieces += [first[dq], second[dq]]
        pieces += [hop(first[dq], dr=1), hop(second[dq], dr=1)]
    on_line = from_me(on_line)
    line_owner = on_line[:, : names.shape[0]].astype(jnp.int32)
    line_mix = on_line[:, names.shape[0] :]
    row_owner = line_owner // padded
    slot_of = (((row_owner // reps) % PLANE) ^ chip) * reps + ((row_owner % reps) ^ rep_idx)
    here = (row_owner // (reps * PLANE)) == line
    row_at = jnp.where(here, slot_of * padded + line_owner % padded, 0) * groups
    mix_here = jnp.where(here, line_mix, 0.0)
    row_at = row_at.reshape(lines, 1, half * cands)
    mix_here = mix_here.reshape(lines, 1, half * cands)
    parts = {}

    def mix_some(which, keep):
        out = mix_rows(
            jnp.stack([row_at[d] for d in which]),
            jnp.stack([mix_here[d] for d in which]),
            pieces,
            cands,
            keep,
        )
        for k, d in enumerate(which):
            parts[d] = out[0][k, : half * groups]
        return out[-1]

    outer = (1, lines - 1)
    mix_some(outer, False)
    out_up = jnp.concatenate([out_proj, up_proj], 1)
    parts[1], parts[lines - 1], out_up, down_shard = lax.optimization_barrier(
        (parts[1], parts[lines - 1], out_up.astype(bf16), down_proj.astype(bf16))
    )
    out_up = gather(out_up)
    down_w = gather(down_shard)
    out_w, up_w = out_up[:, :width], out_up[:, width:]
    far_parts = [hop(parts[d].astype(bf16), dl=d) for d in outer]
    inner = tuple(range(2, lines - 1))
    plane_table = mix_some(inner + (0,), True)
    far_parts += [hop(parts[d].astype(bf16), dl=d) for d in inner]
    far_parts[:2], flat_slot, small_all = lax.optimization_barrier(
        (far_parts[:2], flat_slot, small_all)
    )
    entry = offset * half + jnp.arange(half * cands, dtype=jnp.int32) // cands + 1
    empty = jnp.zeros((devices * cap,), f32)
    lists = [
        empty.at[flat_slot].set(value).reshape(devices, cap)
        for value in (entry.astype(f32), mixing.reshape(-1))
    ]
    asked = jnp.concatenate(lists, 1)
    far_parts, asked = lax.optimization_barrier((far_parts, asked))
    x0 = (parts[0] + sum(far.astype(f32) for far in far_parts)).reshape(half, width)

    mod_f = small_all[:, : 6 * width].astype(f32)
    final_f = small_all[:, 6 * width : 8 * width].astype(f32)
    time_f = small_all[:, 8 * width : -LANES].astype(f32).reshape(-1, time_proj.shape[1])
    gain_f = small_all[:, -LANES:].astype(f32).reshape(devices, -1)[:, : norm_gains.size]
    gain_f = gain_f.reshape((devices,) + norm_gains.shape)
    gain_f = gain_f.transpose(1, 0, 2).reshape(norm_gains.shape[0], width)

    length = lax.dynamic_slice_in_dim(seq_lengths, dp_idx, 1)
    feats = time_features(time_index, time_f.shape[0])
    cond, silu_back = jax.vjp(jax.nn.silu, exact(feats, time_f))
    my_cond = lax.dynamic_slice_in_dim(cond, dp_idx, 1)
    mods = exact(my_cond, mod_f)
    fmods = exact(my_cond, final_f)
    sh1, sc1, g1, sh2, sc2, g2 = jnp.split(mods, 6, -1)
    fsh, fsc = jnp.split(fmods, 2, -1)

    n1, r1 = normalize(x0)
    h1b = (n1 * gain_f[0] * (1.0 + sc1) + sh1).astype(bf16)
    qkv = dense(h1b, qkv_w)
    places = jnp.arange(half, dtype=jnp.int32)
    turns = []
    for core in (rep_idx, 1 - rep_idx):
        cosv, sinv = rope_tables(core * half + places, HD)
        turns += [jnp.tile(cosv, (1, 4)), jnp.concatenate([-sinv, sinv] * 2, 1)]
    query, keyed, valued = turn_rows(qkv, turns[0], turns[1])
    attended = (query, keyed, hop(keyed, dr=1), valued, hop(valued, dr=1))
    core = rep_idx.reshape(1)
    mixed_b, lse_att = attend(length, core, *attended)
    mixed_b, h1_far = lax.optimization_barrier((mixed_b, hop(h1b, dr=1)))
    attn = dense(mixed_b, out_w)
    x1 = x0 + g1 * attn
    n2, r2 = normalize(x1)
    h2b = (n2 * gain_f[1] * (1.0 + sc2) + sh2).astype(bf16)
    upper = dense(h2b, up_w)
    act, gelu_back = jax.vjp(lambda u: jax.nn.gelu(u, approximate=True), upper)
    act_b = act.astype(bf16)
    act_b, mixed_far, h2_far = lax.optimization_barrier(
        (act_b, hop(mixed_b, dr=1), hop(h2b, dr=1))
    )
    mlp = dense(act_b, down_w)
    x2 = x1 + g2 * mlp
    nf, rf = normalize(x2)
    final = nf * gain_f[2] * (1.0 + fsc) + fsh

    picks = loss_pick.shape[-1]
    tau = (time_index.astype(f32) + 1.0) / TSTEPS
    starts = (jnp.arange(reps, dtype=jnp.int32) * half)[None, :, None]
    weight_all = jnp.where(
        loss_pick + starts < seq_lengths[:, None, None], (1.0 / (0.1 + tau))[:, None, None], 0.0
    )
    coefficient_aggregate = jnp.sum(weight_all)

    def of_line(values, at_chip, at_core):
        mine = lax.dynamic_slice(
            values.reshape(lines, PLANE, reps, picks), (0, at_chip, at_core, 0), (lines, 1, 1, picks)
        )
        return from_me(mine.reshape(lines, picks))

    def from_start(values):
        return lax.dynamic_slice_in_dim(
            jnp.concatenate([values, values], 0), (lines - line) % lines, lines
        )

    targets = of_line(loss_target, chip, rep_idx).reshape(-1)
    weight = of_line(weight_all, chip, rep_idx).reshape(-1)
    my_pick = lax.dynamic_slice(loss_pick, (dp_idx, rep_idx, 0), (1, 1, picks)).reshape(picks)
    spread = (jnp.arange(half, dtype=jnp.int32)[:, None] == my_pick[None, :]).astype(f32)
    rows_b = jnp.take(final, my_pick, axis=0).astype(bf16)
    every = jnp.concatenate([rows_b] + [hop(rows_b, dl=-d) for d in range(1, lines)], 0)
    asked = lax.all_to_all(asked, BOTH, split_axis=0, concat_axis=0, tiled=True)
    every, act_far, asked = lax.optimization_barrier((every, hop(act_b, dr=1), asked))
    asked, asked_mix = asked[:, :cap].astype(jnp.int32), asked[:, cap:]
    logits = dense_nt(every, plane_table)
    column = jnp.arange(plane_table.shape[0], dtype=jnp.int32)
    exists = (column % padded) < vocab
    t_owner = targets // vocab
    t_slot = (((t_owner // reps) % PLANE) ^ chip) * reps + ((t_owner % reps) ^ rep_idx)
    t_column = jnp.where(
        t_owner // (reps * PLANE) == line, t_slot * padded + targets % vocab, -1
    )
    hit = column[None, :] == t_column[:, None]
    logits = jnp.where(exists[None, :], logits, -1e30)
    top = jnp.max(logits, -1)
    sums = jnp.sum(jnp.exp(logits - top[:, None]), -1)
    tgt = jnp.sum(jnp.where(hit, logits, 0.0), -1)
    stats = from_start(
        jnp.stack([value.reshape(lines, picks) for value in (top, sums, tgt)], 1)
    )
    stats_all = jnp.stack([stats] + [hop(stats, dl=-d) for d in range(1, lines)])
    tops = stats_all[:, :, 0]
    best = jnp.max(tops, 0)
    sum_all = jnp.sum(stats_all[:, :, 1] * jnp.exp(tops - best), 0)
    lse_line = best + jnp.log(sum_all)
    tgt_line = jnp.sum(stats_all[:, :, 2], 0)
    loss_here = jnp.sum(from_start(weight.reshape(lines, picks)) * (lse_line - tgt_line))
    loss_here = jnp.where(line == 0, loss_here, 0.0)
    lse = from_me(lse_line).reshape(-1)
    probs = jnp.exp(logits - lse[:, None])
    dlogit = ((weight / coefficient_aggregate)[:, None] * (probs - hit.astype(f32))).astype(bf16)
    drows_part = dense(dlogit, plane_table).reshape(lines, picks, width)
    drows = drows_part[0]
    for d in range(1, lines):
        drows = drows + hop(drows_part[d], dl=d)
    every, lse, drows = lax.optimization_barrier((every, lse, drows))
    pieces_of_lse = []
    for _ in range(3):
        rounded = lax.reduce_precision(lse, 8, 7)
        pieces_of_lse.append(rounded.astype(bf16))
        lse = lse - rounded
    extra = jnp.pad(jnp.stack(pieces_of_lse, 1), ((0, 0), (0, LANES - 3)))
    told = jnp.concatenate([every, extra], 1)
    told_x, told_y = hop(told, dq=1), hop(told, dq=2)
    among = [(chip ^ dq, rep_idx ^ dr) for dr in range(reps) for dq in range(PLANE)]
    targets_all = jnp.concatenate([of_line(loss_target, q, r).reshape(-1) for q, r in among])
    weight_rows = jnp.concatenate([of_line(weight_all, q, r).reshape(-1) for q, r in among])

    grad_final = exact(spread, drows)
    dx2, dfsh, dfsc, dgain_f = modulate_back(grad_final, nf, rf, gain_f[2], fsc)
    dg2 = jnp.sum(dx2 * mlp, 0)
    dmlp = (dx2 * g2).astype(bf16)
    g_down = chip_product(act_b, act_far, dmlp)
    dupper = gelu_back(dense_nt(dmlp, down_w))[0].astype(bf16)
    g_up = chip_product(h2b, h2_far, dupper)
    dh2 = dense_nt(dupper, up_w)
    dn2x, dsh2, dsc2, dgain_2 = modulate_back(dh2, n2, r2, gain_f[1], sc2)
    dx1 = dx2 + dn2x
    dg1 = jnp.sum(dx1 * attn, 0)
    dattn = (dx1 * g1).astype(bf16)
    dattn, g_down, g_up, told_x, told_y = lax.optimization_barrier(
        (dattn, g_down, g_up, told_x, told_y)
    )
    down_1 = split_blocks(plane_blocks(g_down), 1, 1)
    up_1 = split_blocks(plane_blocks(g_up), 0, 2)
    g_out = chip_product(mixed_b, mixed_far, dattn)
    dmixed = dense_nt(dattn, out_w).astype(bf16)
    dquery, dkey, dkey_far, dvalue, dvalue_far = attend_back(
        length, core, *attended, lse_att, dmixed, *turns
    )
    told_xy = hop(told_x, dq=2)
    dquery, dkey, dkey_far, dvalue, dvalue_far, down_1, up_1, g_out = lax.optimization_barrier(
        (dquery, dkey, dkey_far, dvalue, dvalue_far, down_1, up_1, g_out)
    )
    down_2 = split_blocks(down_1[0] + down_1[1].astype(f32), 0, 1)
    up_2 = split_blocks(up_1[0] + up_1[1].astype(f32), 1, 1)
    dkey = (dkey + hop(dkey_far, dr=1).astype(f32)).astype(bf16)
    dvalue = (dvalue + hop(dvalue_far, dr=1).astype(f32)).astype(bf16)
    dqkv = jnp.concatenate([dquery, dkey, dvalue], 1)
    dh1 = dense_nt(dqkv, qkv_w)
    dn1x, dsh1, dsc1, dgain_1 = modulate_back(dh1, n1, r1, gain_f[0], sc1)
    dx0 = dx1 + dn1x
    g_qkv = chip_product(h1b, h1_far, dqkv)


    dx0_b = dx0.astype(bf16).reshape(1, half * groups, LANES)
    dx0_b, down_2, up_2 = lax.optimization_barrier((dx0_b, down_2, up_2))
    others = lines - 1
    cut = -(-2 * others // 3)
    sums_here = jnp.concatenate(
        [dsh1, dsc1, dg1, dsh2, dsc2, dg2, dfsh, dfsc, dgain_1, dgain_2, dgain_f]
    )
    on_line = gather_line(dx0_b)
    own_x, own_y = hop(dx0_b, dq=1), hop(dx0_b, dq=2)
    own_xy = hop(own_y, dq=1)
    told = jnp.stack([told, told_x, told_y, told_xy])
    told = jnp.concatenate([told, hop(told, dr=1)], 0).reshape(-1, width + LANES)
    g_last = jnp.concatenate([g_qkv, g_out], 1)
    last_1 = split_blocks(plane_blocks(g_last), 1, 1)
    sums_all = lax.all_gather(sums_here.reshape(1, -1, LANES), BOTH, axis=0, tiled=True)
    last_2 = split_blocks(last_1[0] + last_1[1].astype(f32), 0, 1)
    on_line, own_x, own_y, own_xy, last_2, told, sums_all = lax.optimization_barrier(
        (on_line, own_x, own_y, own_xy, last_2, told, sums_all)
    )
    rows_all = told[:, :width]
    lse_all = jnp.sum(told[:, width : width + 3].astype(f32), 1)
    line_x, line_y = hop(on_line, dq=1), hop(on_line, dq=2)
    shards = [two[0] + two[1].astype(f32) for two in (down_2, up_2, last_2)]
    both = shards[1].shape[1]
    tall = shards[0].shape[1] // both
    pile = shards[0].reshape(lines, tall, both, -1)
    blocks = jnp.concatenate([pile[:, k] for k in range(tall)] + shards[1:], 2)
    sums = reduce_step(blocks, None, lines - 1)
    early = [(dx0_b, 0, 0), (own_x, 1, 0), (own_y, 2, 0), (own_xy, 3, 0), (on_line, 0, 1)]
    order = []

    def from_cores(gathered):
        sources = []
        for value, dq, first_d in gathered:
            sources.extend(add_source(value, dq, first_d))
        return sources

    def add_source(value, dq, first_d):
        for dr in range(reps):
            for d in range(first_d, first_d + value.shape[0]):
                order.append(
                    (((line + d) % lines) * PLANE + (chip ^ dq)) * reps + (rep_idx ^ dr)
                )
        return [value, hop(value, dr=1)]

    def lists_of(order):
        order = jnp.stack(order)
        entries = jnp.take(asked, order, axis=0)
        count = jnp.sum((entries > 0).astype(jnp.int32), 1)
        entries = jnp.maximum(entries - 1, 0)
        return (
            count,
            entries // half,
            (entries % half) * groups,
            jnp.take(asked_mix, order, axis=0),
        )

    sources = from_cores(early)
    begun = spread_rows(lists_of(order), sources, vocab, width)
    order.clear()
    logits_mine = dense_nt(rows_all, table_low)
    own_column = jnp.where(targets_all // vocab == me, targets_all % vocab, -1)
    hit_mine = jnp.arange(padded, dtype=jnp.int32)[None, :] == own_column[:, None]
    dlogit_mine = (
        (weight_rows / coefficient_aggregate)[:, None]
        * (jnp.exp(logits_mine - lse_all[:, None]) - hit_mine.astype(f32))
    ).astype(bf16)
    head_grad = dense_tn(dlogit_mine, rows_all)
    line_x, line_y, begun, head_grad, sums = lax.optimization_barrier(
        (line_x, line_y, begun, head_grad, sums)
    )
    for d in range(lines - 2, 1, -1):
        sums = reduce_step(blocks, sums, d)
    near = hop(line_x[:cut], dq=2)
    rest = [hop(line_y[cut:], dq=1)] if cut < others else []
    sources = from_cores([(line_x, 1, 1), (line_y, 2, 1)])
    begun = spread_rows(lists_of(order), sources, vocab, width, begun)
    order.clear()
    near, rest, begun, sums = lax.optimization_barrier((near, rest, begun, sums))
    sources = from_cores([(near, 3, 1)] + [(value, 3, 1 + cut) for value in rest])
    sources, sums = lax.optimization_barrier((sources, sums))
    sums = reduce_step(blocks, sums, 1)
    table_grad, table_squares = spread_rows(
        lists_of(order), sources, vocab, width, begun, head_grad
    )
    sums, table_grad, table_squares = lax.optimization_barrier((sums, table_grad, table_squares))
    total = block_at(blocks, 0) + sums[0] + sums[1]
    down_end = tall * pile.shape[3]
    pile = jnp.stack(jnp.split(total[:, :down_end], tall, 1))
    d_down = jnp.concatenate(join_cores(pile.reshape(reps, -1, pile.shape[2])), 1)
    left, right = join_cores(total[:, down_end:].reshape(reps, both // reps, -1))
    joined = []
    at = 0
    for columns in (up_proj.shape[1], attn_proj.shape[1], out_proj.shape[1]):
        part = slice(at, at + columns // 2)
        joined.append(jnp.concatenate([left[:, part], right[:, part]], 1))
        at += columns // 2
    d_up, d_qkv, d_out = joined

    sums_all = sums_all.reshape(n_dp, reps, -1).sum(1)
    dmods = sums_all[:, : 6 * width]
    dfmods = sums_all[:, 6 * width : 8 * width]

    def my_columns(value, count):
        return lax.dynamic_slice_in_dim(value, me * count, count, axis=1)

    d_mod = exact_tn(my_columns(cond, mod_proj.shape[0]), dmods)
    d_final = exact_tn(my_columns(cond, final_proj.shape[0]), dfmods)
    dcond = exact_nt(dmods, mod_f) + exact_nt(dfmods, final_f)
    d_time = exact_tn(my_columns(feats, time_proj.shape[0]), silu_back(dcond)[0])
    d_gains = my_columns(
        jnp.sum(sums_all[:, 8 * width :], 0).reshape(3, width), norm_gains.shape[1]
    )

    reduced = (d_qkv, d_out, d_up, d_down, d_time, d_mod, d_final, d_gains)
    local_sq = jnp.sum(table_squares)
    for g in reduced:
        local_sq = local_sq + jnp.sum(g * g)
    totals = add_up(jnp.stack([local_sq, loss_here]))
    grad_norm = jnp.sqrt(totals[0])
    loss_sum = totals[1]
    clip = jnp.minimum(1.0, 0.01 / (grad_norm + 1e-06))
    masters = (attn_proj, out_proj, up_proj, down_proj, time_proj, mod_proj, final_proj, norm_gains)
    coefficients = (vocab_table,) + masters
    moms = (
        table_mom,
        proj_mom,
        outp_mom,
        up_mom,
        down_mom,
        time_mom,
        mod_mom,
        final_mom,
        gains_mom,
    )
    sqs = (table_sq, proj_sq, outp_sq, up_sq, down_sq, time_sq, mod_sq, final_sq, gains_sq)
    rates = (0.02, 0.02, 0.02, 0.02, 0.02, 0.02, 0.02, 0.02, 0.1)
    grads = (table_grad,) + reduced
    result = [loss_sum, coefficient_aggregate, grad_norm]
    quads = list(zip(coefficients, moms, sqs, grads))
    weight_now, first_m, second_m, grad = quads[0]
    result.extend(adamw(weight_now, first_m, second_m, clip * grad, rates[0]))
    result.extend(adamw_all(clip, quads[1:], rates[1:]))
    return tuple(result)


def solution(mesh):
    shard = P(BOTH, None)
    columns = P(None, BOTH)
    return jax.shard_map(
        local,
        mesh=mesh,
        in_specs=(P("dp", "rep", None),) * 3 + (P(),) * 4 + (shard,) * 24 + (columns,) * 3,
        out_specs=(P(),) * 3 + (shard,) * 24 + (columns,) * 3,
        check_vma=False,
    )
```

```python
import functools
import math

import jax
import jax.numpy as jnp
from jax import lax
from jax.experimental import pallas as pl
from jax.experimental.pallas import tpu as pltpu
from jax.sharding import PartitionSpec as P

HD = 64
TSTEPS = 1000
STEP = 5
PLANE = 4
LANES = 128
BOTH = ("dp", "rep")

HIGH = lax.Precision.HIGHEST
annealed_softness = 0.5
bf16 = jnp.bfloat16
f32 = jnp.float32


def dense(a, b):
    return jnp.dot(a, b, preferred_element_type=f32)


def dense_nt(a, b):
    return lax.dot_general(a, b, (((1,), (1,)), ((), ())), preferred_element_type=f32)


def dense_tn(a, b):
    return lax.dot_general(a, b, (((0,), (0,)), ((), ())), preferred_element_type=f32)


def exact(a, b):
    return jnp.dot(a, b, precision=HIGH, preferred_element_type=f32)


def exact_nt(a, b):
    return lax.dot_general(
        a, b, (((1,), (1,)), ((), ())), precision=HIGH, preferred_element_type=f32
    )


def exact_tn(a, b):
    return lax.dot_general(
        a, b, (((0,), (0,)), ((), ())), precision=HIGH, preferred_element_type=f32
    )


def normalize(x):
    center = x - jnp.mean(x, -1, keepdims=True)
    rstd = lax.rsqrt(jnp.mean(center * center, -1, keepdims=True) + 1e-06)
    return (center * rstd, rstd)


def modulate_back(grad_h, normed, rstd, gain, scale):
    dshift = jnp.sum(grad_h, 0)
    weighted = grad_h * normed
    column = jnp.sum(weighted, 0)
    dscale = column * gain
    dgain = column * (1.0 + scale[0])
    grad_n = grad_h * gain * (1.0 + scale)
    grad_x = rstd * (
        grad_n
        - jnp.mean(grad_n, -1, keepdims=True)
        - normed * jnp.mean(grad_n * normed, -1, keepdims=True)
    )
    return (grad_x, dshift, dscale, dgain)


def rope_tables(pos, head):
    half = head // 2
    freqs = jnp.exp(-math.log(10000.0) * jnp.arange(half, dtype=f32) / half)
    angle = pos.astype(f32)[:, None] * freqs[None, :]
    return (jnp.cos(angle), jnp.sin(angle))


def time_features(steps, width):
    tau = (steps.astype(f32) + 1.0) / TSTEPS
    half = width // 2
    freqs = jnp.exp(-math.log(10000.0) * jnp.arange(half, dtype=f32) / half)
    angle = 1000.0 * tau[:, None] * freqs[None, :]
    return jnp.concatenate([jnp.cos(angle), jnp.sin(angle)], -1)


def turn(x, cosv, sinv):
    lane = lax.broadcasted_iota(jnp.int32, x.shape, 1)
    quarter = HD // 2
    swapped = jnp.where(
        lane % HD < quarter,
        pltpu.roll(x, LANES - quarter, axis=1),
        pltpu.roll(x, quarter, axis=1),
    )
    return x * cosv + swapped * sinv


def turn_kernel(q_ref, k_ref, v_ref, cos_ref, sin_ref, q_out, k_out, v_out):
    cosv, sinv = cos_ref[...], sin_ref[...]
    for start in range(0, q_ref.shape[1], LANES):
        at = slice(start, start + LANES)
        q_out[:, at] = turn(q_ref[:, at], cosv, sinv).astype(bf16)
        k_out[:, at] = turn(k_ref[:, at], cosv, sinv).astype(bf16)
    v_out[...] = v_ref[...].astype(bf16)


def turn_rows(qkv, cosv, sinv):
    rows, width = qkv.shape[0], qkv.shape[1] // 3
    wide = 3 * LANES if width % (3 * LANES) == 0 else LANES
    blocks = width // wide
    block = lambda shift: pl.BlockSpec((rows, wide), lambda i: (0, i + shift))
    whole = pl.BlockSpec((rows, LANES), lambda i: (0, 0))
    return pl.pallas_call(
        turn_kernel,
        grid=(blocks,),
        in_specs=[block(0), block(blocks), block(2 * blocks), whole, whole],
        out_specs=[block(0)] * 3,
        out_shape=[jax.ShapeDtypeStruct((rows, width), bf16)] * 3,
        cost_estimate=pl.CostEstimate(
            flops=rows * width * 12, bytes_accessed=rows * width * 18, transcendentals=0
        ),
    )(qkv, qkv, qkv, cosv, sinv)


def key_masks(len_ref, core_ref, keys):
    place = lax.broadcasted_iota(jnp.int32, (1, keys), 1)
    own = place + core_ref[0] * keys
    far = place + (1 - core_ref[0]) * keys
    return [jnp.where(at < len_ref[0], 0.0, -1e30).astype(f32) for at in (own, far)]


def attend_kernel(len_ref, core_ref, q_ref, k_ref, kf_ref, v_ref, vf_ref, *refs, tile):
    out_ref, lse_ref = refs[-2:]
    rows = q_ref.shape[0]
    masks = key_masks(len_ref, core_ref, rows)
    keyed = (k_ref[...], kf_ref[...])
    valued = (v_ref[...], vf_ref[...])
    lane = lax.broadcasted_iota(jnp.int32, (tile, LANES), 1)
    for t in range(rows // tile):
        at = pl.ds(t * tile, tile)
        query = q_ref[at, :] * bf16(HD**-0.5)
        mixed, lses = [], []
        for head in range(LANES // HD):
            mine = jnp.where(lane // HD == head, query, bf16(0))
            scores = [dense_nt(mine, k) + mask for k, mask in zip(keyed, masks)]
            top = jnp.maximum(*[jnp.max(s, 1, keepdims=True) for s in scores])
            expo = [jnp.exp(s - top) for s in scores]
            total = sum(jnp.sum(e, 1, keepdims=True) for e in expo)
            inverse = 1.0 / total
            mixed.append(sum(dense((e * inverse).astype(bf16), v) for e, v in zip(expo, valued)))
            lses.append(top + jnp.log(total))
        out_ref[at, :] = jnp.where(lane < HD, mixed[0], mixed[1]).astype(bf16)
        lse_ref[at, :] = jnp.where(lane < HD, lses[0], lses[1])


def attend(length, core, query, keyed, keyed_far, valued, valued_far, ready=()):
    rows, width = query.shape
    smem = pl.BlockSpec(memory_space=pltpu.SMEM)
    block = pl.BlockSpec((rows, LANES), lambda i: (0, i))
    return pl.pallas_call(
        functools.partial(attend_kernel, tile=256),
        grid=(width // LANES,),
        in_specs=[smem, smem] + [block] * 5 + [pl.BlockSpec(memory_space=pl.ANY)] * len(ready),
        out_specs=[block, block],
        out_shape=[
            jax.ShapeDtypeStruct((rows, width), bf16),
            jax.ShapeDtypeStruct((rows, width), f32),
        ],
        compiler_params=pltpu.CompilerParams(vmem_limit_bytes=48 * 2**20),
        cost_estimate=pl.CostEstimate(
            flops=8 * rows * rows * width, bytes_accessed=rows * width * 18,
            transcendentals=2 * rows * rows * width // HD,
        ),
    )(length, core, query, keyed, keyed_far, valued, valued_far, *ready)


def attend_back_kernel(
    len_ref,
    core_ref,
    q_ref,
    k_ref,
    kf_ref,
    v_ref,
    vf_ref,
    lse_ref,
    do_ref,
    cos_ref,
    sin_ref,
    cos_far_ref,
    sin_far_ref,
    *refs,
    tile,
):
    dq_ref, dk_ref, dkf_ref, dv_ref, dvf_ref = refs[-5:]
    rows = q_ref.shape[0]
    masks = key_masks(len_ref, core_ref, rows)
    keyed = (k_ref[...], kf_ref[...])
    valued = (v_ref[...], vf_ref[...])
    lane = lax.broadcasted_iota(jnp.int32, (tile, LANES), 1)
    first = lax.broadcasted_iota(jnp.int32, (rows, LANES), 1) < HD
    dk, dv = [None, None], [None, None]
    for t in range(rows // tile):
        at = pl.ds(t * tile, tile)
        query = q_ref[at, :] * bf16(HD**-0.5)
        grad = do_ref[at, :]
        dqs, dks, dvs = [], [[], []], [[], []]
        for head in range(LANES // HD):
            mine = lane // HD == head
            q_mine = jnp.where(mine, query, bf16(0))
            g_mine = jnp.where(mine, grad, bf16(0))
            lse = lse_ref[at, head * HD : head * HD + 1]
            probs = [jnp.exp(dense_nt(q_mine, k) + mask - lse) for k, mask in zip(keyed, masks)]
            grad_p = [dense_nt(g_mine, v) for v in valued]
            delta = sum(jnp.sum(p * g, 1, keepdims=True) for p, g in zip(probs, grad_p))
            grad_s = [(p * (g - delta)).astype(bf16) for p, g in zip(probs, grad_p)]
            dqs.append(sum(dense(s, k) for s, k in zip(grad_s, keyed)))
            for side in range(2):
                dks[side].append(dense_tn(grad_s[side], query))
                dvs[side].append(dense_tn(probs[side].astype(bf16), grad))
        turned = turn(jnp.where(lane < HD, dqs[0], dqs[1]), cos_ref[at, :], -sin_ref[at, :])
        dq_ref[at, :] = (turned * HD**-0.5).astype(bf16)
        for side in range(2):
            part_k = jnp.where(first, *dks[side])
            part_v = jnp.where(first, *dvs[side])
            dk[side] = part_k if t == 0 else dk[side] + part_k
            dv[side] = part_v if t == 0 else dv[side] + part_v
    dk_ref[...] = turn(dk[0], cos_ref[...], -sin_ref[...])
    dkf_ref[...] = turn(dk[1], cos_far_ref[...], -sin_far_ref[...]).astype(bf16)
    dv_ref[...] = dv[0]
    dvf_ref[...] = dv[1].astype(bf16)


def attend_back(length, core, *arrays, ready=()):
    query = arrays[0]
    rows, width = query.shape
    smem = pl.BlockSpec(memory_space=pltpu.SMEM)
    block = pl.BlockSpec((rows, LANES), lambda i: (0, i))
    return pl.pallas_call(
        functools.partial(attend_back_kernel, tile=256),
        grid=(width // LANES,),
        in_specs=[smem, smem]
        + [block] * 7
        + [pl.BlockSpec((rows, LANES), lambda i: (0, 0))] * 4
        + [pl.BlockSpec(memory_space=pl.ANY)] * len(ready),
        out_specs=[block] * 5,
        out_shape=[jax.ShapeDtypeStruct((rows, width), t) for t in (bf16, f32, bf16, f32, bf16)],
        compiler_params=pltpu.CompilerParams(vmem_limit_bytes=48 * 2**20),
        cost_estimate=pl.CostEstimate(
            flops=20 * rows * rows * width, bytes_accessed=rows * width * 32,
            transcendentals=2 * rows * rows * width // HD,
        ),
    )(length, core, *arrays, *ready)
def adamw(weight, first, second, grad, rate):
    first = 0.9 * first + 0.1 * grad
    second = 0.999 * second + 0.001 * grad * grad
    step = first / (1.0 - 0.9**STEP) / (jnp.sqrt(second / (1.0 - 0.999**STEP)) + 1e-08)
    return (weight - rate * (step + 0.01 * weight), first, second)


def adamw_kernel(clip_ref, *refs, rates):
    n = len(rates)
    for k, rate in enumerate(rates):
        weight, first, second, grad = [ref[...] for ref in refs[4 * k : 4 * k + 4]]
        outs = refs[4 * n + 3 * k : 4 * n + 3 * k + 3]
        for out, value in zip(outs, adamw(weight, first, second, clip_ref[0] * grad, rate)):
            out[...] = value


def adamw_all(clip, quads, rates):
    vmem = pl.BlockSpec(memory_space=pltpu.VMEM)
    flat = [value for quad in quads for value in quad]
    shapes = [jax.ShapeDtypeStruct(quad[0].shape, f32) for quad in quads for _ in range(3)]
    return pl.pallas_call(
        functools.partial(adamw_kernel, rates=rates),
        in_specs=[pl.BlockSpec(memory_space=pltpu.SMEM)] + [vmem] * len(flat),
        out_specs=[vmem] * len(shapes),
        out_shape=shapes,
        compiler_params=pltpu.CompilerParams(vmem_limit_bytes=48 * 2**20),
    )(clip.reshape(1), *flat)


def hop(x, dl=0, dq=0, dr=0):
    reps = lax.axis_size("rep")
    lines = lax.axis_size("dp") // PLANE
    pairs = []
    for l in range(lines):
        for q in range(PLANE):
            for r in range(reps):
                to = (((l + dl) % lines) * PLANE + (q ^ dq)) * reps + (r ^ dr)
                pairs.append(((l * PLANE + q) * reps + r, to))
    return lax.ppermute(x, BOTH, pairs)


def step_line(x, way, reach):
    lines = lax.axis_size("dp") // PLANE
    pairs = []
    for l in range(lines):
        if 0 <= l + way * reach < lines:
            for q in range(PLANE):
                pairs.append((l * PLANE + q, (l + way) * PLANE + q))
    return lax.ppermute(x, "dp", pairs)


def pick_half(value, index):
    size = value.shape[1] // 2
    return lax.dynamic_slice_in_dim(value, index * size, size, axis=1)


def chip_product(left, left_far, right, far=None):
    rep_idx = lax.axis_index("rep")
    if far is None:
        far = hop(pick_half(right, 1 - rep_idx), dr=1)
    return dense_tn(left, pick_half(right, rep_idx)) + dense_tn(left_far, far)


def plane_blocks(value):
    lines = lax.axis_size("dp") // PLANE
    return value.reshape(lines, 2, 2, value.shape[0] // (lines * PLANE), -1)


def split_blocks(blocks, axis, place):
    bit = (lax.axis_index("dp") >> axis) & 1
    far = lax.dynamic_index_in_dim(blocks, 1 - bit, place, False).astype(bf16)
    return lax.dynamic_index_in_dim(blocks, bit, place, False), hop(far, dq=1 << axis)


def block_at(blocks, shift):
    line = lax.axis_index("dp") // PLANE
    return lax.dynamic_index_in_dim(blocks, jnp.mod(line + shift, blocks.shape[0]), 0, False)


def reduce_step(blocks, sums, reach):
    to_right, to_left = block_at(blocks, reach), block_at(blocks, -reach)
    if sums is not None:
        to_right, to_left = to_right + sums[0], to_left + sums[1]
    return step_line(to_right, 1, reach), step_line(to_left, -1, reach)


def join_cores(parts):
    rep_idx = lax.axis_index("rep")
    mine = lax.dynamic_index_in_dim(parts, rep_idx, 0, False)
    far = hop(lax.dynamic_index_in_dim(parts, 1 - rep_idx, 0, False), dr=1)
    return jnp.where(rep_idx == 0, mine, far), jnp.where(rep_idx == 0, far, mine)


def add_up(value):
    lines = lax.axis_size("dp") // PLANE
    line = lax.axis_index("dp") // PLANE
    value = value + hop(value, dr=1)
    far = [hop(value, dq=dq) for dq in range(1, PLANE)]
    value = (value + far[0]) + (far[1] + far[2])
    every = jnp.stack([value] + [hop(value, dl=-d) for d in range(1, lines)])
    every = lax.dynamic_slice_in_dim(
        jnp.concatenate([every, every], 0), (lines - line) % lines, lines
    )
    return jnp.sum(every, 0)


def mix_kernel(idx_ref, mix_ref, *refs, groups, cands, counts, keep):
    n = len(counts)
    pieces, refs = refs[:n], refs[n:]
    if keep:
        out_ref, whole_ref, tab, stage, sem, keep_sem = refs
    else:
        out_ref, tab, stage, sem = refs
    slots = stage.shape[0]
    bases = [sum(counts[:j]) for j in range(n)]

    @pl.when(pl.program_id(0) == 0)
    def _():
        def slot(j):
            return stage.at[j % slots, pl.ds(0, counts[j])]

        def copy(j):
            return pltpu.make_async_copy(pieces[j], slot(j), sem.at[j % slots])

        def store(j):
            whole = whole_ref.at[pl.ds(bases[j], counts[j])]
            return pltpu.make_async_copy(slot(j), whole, keep_sem.at[j % slots])

        for j in range(min(2, n)):
            copy(j).start()
        for j in range(n):
            copy(j).wait()
            if keep:
                store(j).start()

            @pl.loop(0, counts[j] // 16)
            def _(t, j=j):
                part = stage[j % slots, pl.ds(pl.multiple_of(t * 16, 16), 16), :].astype(f32)
                for g in range(groups):
                    tab[pl.ds((bases[j] + t * 16) * groups + g, 16, stride=groups), :] = part[
                        :, g * LANES : (g + 1) * LANES
                    ]

            if keep and j >= 2:
                store(j - 2).wait()
            if j + 2 < n:
                copy(j + 2).start()
        if keep:
            for j in range(max(0, n - 2), n):
                store(j).wait()

    unroll = 4

    @pl.loop(0, idx_ref.shape[-1] // cands // unroll)
    def _(block):
        for u in range(unroll):
            p = block * unroll + u
            total = None
            for c in range(cands):
                row = tab[pl.ds(idx_ref[0, 0, p * cands + c], 8), :]
                term = row * mix_ref[0, 0, p * cands + c]
                total = term if total is None else total + term
            out_ref[0, pl.ds(p * groups, 8), :] = total


def mix_rows(idx, mix, pieces, cands, keep):
    width = pieces[0].shape[1]
    groups = width // LANES
    lines, _, entries = idx.shape
    counts = tuple(piece.shape[0] for piece in pieces)
    rows = entries // cands * groups + 8
    out_specs = [pl.BlockSpec((1, rows, LANES), lambda i: (i, 0, 0))]
    out_shape = [jax.ShapeDtypeStruct((lines, rows, LANES), f32)]
    slots = 4
    scratch = [
        pltpu.VMEM((sum(counts) * groups + 8, LANES), f32),
        pltpu.VMEM((slots, max(counts), width), bf16),
        pltpu.SemaphoreType.DMA((slots,)),
    ]
    if keep:
        out_specs.append(pl.BlockSpec(memory_space=pl.ANY))
        out_shape.append(jax.ShapeDtypeStruct((sum(counts), width), bf16))
        scratch.append(pltpu.SemaphoreType.DMA((slots,)))
    return pl.pallas_call(
        functools.partial(mix_kernel, groups=groups, cands=cands, counts=counts, keep=keep),
        grid=(lines,),
        in_specs=[pl.BlockSpec((1, 1, entries), lambda i: (i, 0, 0), memory_space=pltpu.SMEM)] * 2
        + [pl.BlockSpec(memory_space=pl.ANY)] * len(pieces),
        out_specs=out_specs,
        out_shape=out_shape,
        scratch_shapes=scratch,
        compiler_params=pltpu.CompilerParams(vmem_limit_bytes=60 * 2**20),
        cost_estimate=pl.CostEstimate(
            flops=lines * entries * 2048, bytes_accessed=40 * 2**20, transcendentals=0
        ),
    )(idx, mix, *pieces)


def spread_kernel(cnt_ref, row_ref, pos_ref, mix_ref, *refs, groups, arrays, first, last):
    sources = refs[:arrays]
    refs = list(refs[arrays:])
    total_in = None if first else refs.pop(0)
    if last:
        head_ref, out_ref, sq_ref = refs[:3]
        refs = refs[3:]
    total, rows32, stage, sem, total_sem = refs
    length = sources[0].shape[1]
    blocks = [source.at[k] for source in sources for k in range(source.shape[0])]
    n = len(blocks)

    def copy(k):
        return pltpu.make_async_copy(blocks[k], stage.at[k % 2], sem.at[k % 2])

    copy(0).start()
    if not first:
        load = pltpu.make_async_copy(total_in, total, total_sem)
        load.start()
        load.wait()
    else:

        @pl.loop(0, total.shape[0] // 64)
        def _(t):
            total[pl.ds(pl.multiple_of(t * 64, 64), 64), :] = jnp.zeros((64, LANES), f32)

    unroll = 4
    for k in range(n):
        if k + 1 < n:
            copy(k + 1).start()
        copy(k).wait()

        @pl.loop(0, length // 64)
        def _(t, k=k):
            at = pl.multiple_of(t * 64, 64)
            rows32[pl.ds(at, 64), :] = stage[k % 2, pl.ds(at, 64), :].astype(f32)

        @pl.loop(0, (cnt_ref[k] + unroll - 1) // unroll)
        def _(block, k=k):
            for u in range(unroll):
                e = block * unroll + u
                at = pl.ds(pl.multiple_of(row_ref[k, e] * 8, 8), 8)
                term = mix_ref[k, e] * rows32[pl.ds(pos_ref[k, e], 8), :]
                total[at, :] = total[at, :] + term

    if not last:
        return
    vocab = out_ref.shape[0]

    def finish(at, size, start):
        squares = jnp.zeros((size, LANES), f32)
        for g in range(groups):
            columns = slice(g * LANES, (g + 1) * LANES)
            value = head_ref[pl.ds(at, size), columns] + total[pl.ds(start + g, size, stride=8), :]
            out_ref[pl.ds(at, size), columns] = value
            squares = squares + value * value
        return squares

    squares = lax.fori_loop(
        0,
        vocab // 8,
        lambda t, so_far: so_far + finish(pl.multiple_of(t * 8, 8), 8, t * 64),
        jnp.zeros((8, LANES), f32),
    )
    sq_ref[...] = squares
    if vocab % 8:
        at = vocab // 8 * 8
        sq_ref[0 : vocab % 8, :] += finish(at, vocab % 8, at * 8)


def spread_rows(lists, sources, vocab, width, total=None, head=None):
    groups = width // LANES
    length = sources[0].shape[1]
    total_rows = -(-vocab * 8 // 64) * 64
    first, last = total is None, head is not None
    smem = pl.BlockSpec(memory_space=pltpu.SMEM)
    vmem = pl.BlockSpec(memory_space=pltpu.VMEM)
    hbm = pl.BlockSpec(memory_space=pl.ANY)
    scratch = [
        pltpu.VMEM((length + 8, LANES), f32),
        pltpu.VMEM((2, length, LANES), bf16),
        pltpu.SemaphoreType.DMA((2,)),
    ]
    extra_specs, extra = ([], []) if first else ([hbm], [total])
    scratch.append(pltpu.SemaphoreType.DMA)
    if last:
        extra_specs, extra = extra_specs + [vmem], extra + [head]
        out_specs = [vmem, vmem]
        out_shape = [
            jax.ShapeDtypeStruct((vocab, width), f32),
            jax.ShapeDtypeStruct((8, LANES), f32),
        ]
        scratch = [pltpu.VMEM((total_rows, LANES), f32)] + scratch
    else:
        out_specs = vmem
        out_shape = jax.ShapeDtypeStruct((total_rows, LANES), f32)
    entries = sum(source.shape[0] for source in sources) * lists[1].shape[1] // 2
    return pl.pallas_call(
        functools.partial(
            spread_kernel,
            groups=groups,
            arrays=len(sources),
            first=first,
            last=last,
        ),
        in_specs=[smem] * 4 + [hbm] * len(sources) + extra_specs,
        out_specs=out_specs,
        out_shape=out_shape,
        scratch_shapes=scratch,
        compiler_params=pltpu.CompilerParams(vmem_limit_bytes=60 * 2**20),
        cost_estimate=pl.CostEstimate(
            flops=entries * 2048, bytes_accessed=entries * 10240, transcendentals=0
        ),
    )(*lists, *sources, *extra)


def local(
    noise_owner,
    noise_offset,
    option_scores,
    seq_lengths,
    time_index,
    loss_pick,
    loss_target,
    vocab_table,
    table_mom,
    table_sq,
    attn_proj,
    proj_mom,
    proj_sq,
    out_proj,
    outp_mom,
    outp_sq,
    up_proj,
    up_mom,
    up_sq,
    down_proj,
    down_mom,
    down_sq,
    time_proj,
    time_mom,
    time_sq,
    mod_proj,
    mod_mom,
    mod_sq,
    final_proj,
    final_mom,
    final_sq,
    norm_gains,
    gains_mom,
    gains_sq,
):
    devices = lax.axis_size(BOTH)
    reps = lax.axis_size("rep")
    n_dp = lax.axis_size("dp")
    lines = n_dp // PLANE
    dp_idx = lax.axis_index("dp")
    rep_idx = lax.axis_index("rep")
    me = dp_idx * reps + rep_idx
    line = dp_idx // PLANE
    chip = dp_idx % PLANE
    _, half, cands = noise_offset.shape
    vocab, width = vocab_table.shape
    heads = width // HD
    groups = width // LANES
    swaps = [(dq, dr) for dq in range(PLANE) for dr in range(reps)]

    def from_me(values):
        return lax.dynamic_slice_in_dim(jnp.concatenate([values, values], 0), line, lines)

    def gather(value, axis=0):
        return lax.all_gather(value.astype(bf16), BOTH, axis=axis, tiled=True)

    few = mod_proj.shape[0]
    gains_flat = norm_gains.reshape(-1)
    gains_flat = jnp.pad(gains_flat, (0, few * LANES - gains_flat.size))
    small_all = lax.all_gather(
        jnp.concatenate(
            [mod_proj, final_proj, time_proj.reshape(few, -1), gains_flat.reshape(few, LANES)], 1
        ).astype(bf16),
        BOTH,
    )
    qkv_w = gather(attn_proj)

    padded = -(-vocab // 16) * 16
    table_low = jnp.pad(vocab_table.astype(bf16), ((0, padded - vocab), (0, 0)))
    cut = padded // 32 * 16
    upper_rows, lower_rows = table_low[:cut], table_low[cut:]
    first, second = {0: upper_rows}, {0: lower_rows}
    for dq in (1, 2):
        first[dq] = hop(upper_rows, dq=dq)
        second[dq] = hop(lower_rows, dq=dq)

    owner = noise_owner.reshape(-1)
    offset = noise_offset.reshape(-1)
    mixing = jax.nn.softmax(option_scores.reshape(half, cands) / annealed_softness, axis=-1)
    names = (owner * padded + offset).astype(f32).reshape(-1, LANES)
    packed = jnp.concatenate([names, mixing.reshape(-1, LANES)], 0)
    groups_of_line = [[l * PLANE + q for l in range(lines)] for q in range(PLANE)]
    on_line = lax.all_gather(packed, "dp", axis_index_groups=groups_of_line)
    cap = max(2, 2 * half * cands // devices)
    member = (owner[:, None] == jnp.arange(devices, dtype=jnp.int32)[None, :]).astype(jnp.int32)
    slot = jnp.sum((jnp.cumsum(member, 0) - member) * member, 1)
    flat_slot = owner * cap + slot
    late_shards = (
        jnp.concatenate([out_proj, up_proj], 1).astype(bf16),
        down_proj.astype(bf16),
    )
    first, second, flat_slot, late_shards = lax.optimization_barrier(
        (first, second, flat_slot, late_shards)
    )
    first[3] = hop(first[1], dq=2)
    second[3] = hop(second[2], dq=1)
    pieces = []
    for dq in range(PLANE):
        pieces += [first[dq], second[dq]]
        pieces += [hop(first[dq], dr=1), hop(second[dq], dr=1)]
    on_line = from_me(on_line)
    line_owner = on_line[:, : names.shape[0]].astype(jnp.int32)
    line_mix = on_line[:, names.shape[0] :]
    row_owner = line_owner // padded
    slot_of = (((row_owner // reps) % PLANE) ^ chip) * reps + ((row_owner % reps) ^ rep_idx)
    here = (row_owner // (reps * PLANE)) == line
    row_at = jnp.where(here, slot_of * padded + line_owner % padded, 0) * groups
    mix_here = jnp.where(here, line_mix, 0.0)
    row_at = row_at.reshape(lines, 1, half * cands)
    mix_here = mix_here.reshape(lines, 1, half * cands)
    parts = {}

    outer = (1, lines - 1)
    inner = tuple(range(2, lines - 1)) + (0,)
    stacked = [
        (jnp.stack([row_at[d] for d in which]), jnp.stack([mix_here[d] for d in which]))
        for which in (outer, inner)
    ]

    places = jnp.arange(half, dtype=jnp.int32)
    turns = []
    for core in (rep_idx, 1 - rep_idx):
        cosv, sinv = rope_tables(core * half + places, HD)
        turns += [jnp.tile(cosv, (1, 4)), jnp.concatenate([-sinv, sinv] * 2, 1)]
    length = lax.dynamic_slice_in_dim(seq_lengths, dp_idx, 1)
    picks = loss_pick.shape[-1]
    tau = (time_index.astype(f32) + 1.0) / TSTEPS
    starts = (jnp.arange(reps, dtype=jnp.int32) * half)[None, :, None]
    weight_all = jnp.where(
        loss_pick + starts < seq_lengths[:, None, None], (1.0 / (0.1 + tau))[:, None, None], 0.0
    )
    coefficient_aggregate = jnp.sum(weight_all)

    def of_line(values, at_chip, at_core):
        mine = lax.dynamic_slice(
            values.reshape(lines, PLANE, reps, picks), (0, at_chip, at_core, 0), (lines, 1, 1, picks)
        )
        return from_me(mine.reshape(lines, picks))

    def from_start(values):
        return lax.dynamic_slice_in_dim(
            jnp.concatenate([values, values], 0), (lines - line) % lines, lines
        )

    targets = of_line(loss_target, chip, rep_idx).reshape(-1)
    weight = of_line(weight_all, chip, rep_idx).reshape(-1)
    my_pick = lax.dynamic_slice(loss_pick, (dp_idx, rep_idx, 0), (1, 1, picks)).reshape(picks)
    t_owner = targets // vocab
    t_slot = (((t_owner // reps) % PLANE) ^ chip) * reps + ((t_owner % reps) ^ rep_idx)
    t_column = jnp.where(
        t_owner // (reps * PLANE) == line, t_slot * padded + targets % vocab, -1
    )
    among = [(chip ^ dq, rep_idx ^ dr) for dr in range(reps) for dq in range(PLANE)]
    targets_all = jnp.concatenate([of_line(loss_target, q, r).reshape(-1) for q, r in among])
    weight_rows = jnp.concatenate([of_line(weight_all, q, r).reshape(-1) for q, r in among])
    line_facts = (turns, length, weight_all, targets, weight, my_pick, t_column)
    line_facts, targets_all, weight_rows, stacked = lax.optimization_barrier(
        (line_facts, targets_all, weight_rows, stacked)
    )
    turns, length, weight_all, targets, weight, my_pick, t_column = line_facts

    def mix_some(call, keep):
        out = mix_rows(*stacked[call], pieces, cands, keep)
        for k, d in enumerate((outer, inner)[call]):
            parts[d] = out[0][k, : half * groups]
        return out[-1]

    mix_some(0, False)
    parts[1], parts[lines - 1], late_shards = lax.optimization_barrier(
        (parts[1], parts[lines - 1], late_shards)
    )
    out_up = gather(late_shards[0])
    down_w = gather(late_shards[1])
    out_w, up_w = out_up[:, :width], out_up[:, width:]
    far_parts = [hop(parts[d].astype(bf16), dl=d) for d in outer]
    plane_table = mix_some(1, True)
    far_parts += [hop(parts[d].astype(bf16), dl=d) for d in inner[:-1]]
    far_parts[:2], flat_slot, small_all = lax.optimization_barrier(
        (far_parts[:2], flat_slot, small_all)
    )
    small_all = small_all.reshape(devices * few, -1)
    entry = offset * half + jnp.arange(half * cands, dtype=jnp.int32) // cands + 1
    empty = jnp.zeros((devices * cap,), f32)
    lists = [
        empty.at[flat_slot].set(value).reshape(devices, cap)
        for value in (entry.astype(f32), mixing.reshape(-1))
    ]
    asked = jnp.concatenate(lists, 1)
    mod_f = small_all[:, : 6 * width].astype(f32)
    final_f = small_all[:, 6 * width : 8 * width].astype(f32)
    time_f = small_all[:, 8 * width : -LANES].astype(f32).reshape(-1, time_proj.shape[1])
    gain_f = small_all[:, -LANES:].astype(f32).reshape(devices, -1)[:, : norm_gains.size]
    gain_f = gain_f.reshape((devices,) + norm_gains.shape)
    gain_f = gain_f.transpose(1, 0, 2).reshape(norm_gains.shape[0], width)

    feats = time_features(time_index, time_f.shape[0])
    cond, silu_back = jax.vjp(jax.nn.silu, exact(feats, time_f))
    my_cond = lax.dynamic_slice_in_dim(cond, dp_idx, 1)
    mods = exact(my_cond, mod_f)
    fmods = exact(my_cond, final_f)
    far_parts, asked, mods, fmods, gain_f = lax.optimization_barrier(
        (far_parts, asked, mods, fmods, gain_f)
    )
    sh1, sc1, g1, sh2, sc2, g2 = jnp.split(mods, 6, -1)
    fsh, fsc = jnp.split(fmods, 2, -1)
    x0 = (parts[0] + sum(far.astype(f32) for far in far_parts)).reshape(half, width)

    n1, r1 = normalize(x0)
    h1b = (n1 * gain_f[0] * (1.0 + sc1) + sh1).astype(bf16)
    qkv = dense(h1b, qkv_w)
    query, keyed, valued = turn_rows(qkv, turns[0], turns[1])
    attended = (query, keyed, hop(keyed, dr=1), valued, hop(valued, dr=1))
    core = rep_idx.reshape(1)
    mixed_b, lse_att = attend(length, core, *attended)
    mixed_b, h1_far = lax.optimization_barrier((mixed_b, hop(h1b, dr=1)))
    attn = dense(mixed_b, out_w)
    x1 = x0 + g1 * attn
    n2, r2 = normalize(x1)
    h2b = (n2 * gain_f[1] * (1.0 + sc2) + sh2).astype(bf16)
    upper = dense(h2b, up_w)
    act, gelu_back = jax.vjp(lambda u: jax.nn.gelu(u, approximate=True), upper)
    act_b = act.astype(bf16)
    act_b, mixed_far, h2_far = lax.optimization_barrier(
        (act_b, hop(mixed_b, dr=1), hop(h2b, dr=1))
    )
    mlp = dense(act_b, down_w)
    x2 = x1 + g2 * mlp
    nf, rf = normalize(x2)
    final = nf * gain_f[2] * (1.0 + fsc) + fsh

    spread = (jnp.arange(half, dtype=jnp.int32)[:, None] == my_pick[None, :]).astype(f32)
    rows_b = jnp.take(final, my_pick, axis=0).astype(bf16)
    every = jnp.concatenate([rows_b] + [hop(rows_b, dl=-d) for d in range(1, lines)], 0)
    asked = lax.all_to_all(asked, BOTH, split_axis=0, concat_axis=0, tiled=True)
    every, act_far, asked = lax.optimization_barrier((every, hop(act_b, dr=1), asked))
    asked, asked_mix = asked[:, :cap].astype(jnp.int32), asked[:, cap:]
    logits = dense_nt(every, plane_table)
    column = jnp.arange(plane_table.shape[0], dtype=jnp.int32)
    exists = (column % padded) < vocab
    hit = column[None, :] == t_column[:, None]
    logits = jnp.where(exists[None, :], logits, -1e30)
    top = jnp.max(logits, -1)
    sums = jnp.sum(jnp.exp(logits - top[:, None]), -1)
    tgt = jnp.sum(jnp.where(hit, logits, 0.0), -1)
    stats = from_start(
        jnp.stack([value.reshape(lines, picks) for value in (top, sums, tgt)], 1)
    )
    stats_all = jnp.stack([stats] + [hop(stats, dl=-d) for d in range(1, lines)])
    tops = stats_all[:, :, 0]
    best = jnp.max(tops, 0)
    sum_all = jnp.sum(stats_all[:, :, 1] * jnp.exp(tops - best), 0)
    lse_line = best + jnp.log(sum_all)
    tgt_line = jnp.sum(stats_all[:, :, 2], 0)
    loss_here = jnp.sum(from_start(weight.reshape(lines, picks)) * (lse_line - tgt_line))
    loss_here = jnp.where(line == 0, loss_here, 0.0)
    lse = from_me(lse_line).reshape(-1)
    probs = jnp.exp(logits - lse[:, None])
    dlogit = ((weight / coefficient_aggregate)[:, None] * (probs - hit.astype(f32))).astype(bf16)
    drows_part = dense(dlogit, plane_table).reshape(lines, picks, width)
    drows = drows_part[0]
    for d in range(1, lines):
        drows = drows + hop(drows_part[d], dl=d)
    every, lse, drows = lax.optimization_barrier((every, lse, drows))
    pieces_of_lse = []
    for _ in range(3):
        rounded = lax.reduce_precision(lse, 8, 7)
        pieces_of_lse.append(rounded.astype(bf16))
        lse = lse - rounded
    extra = jnp.pad(jnp.stack(pieces_of_lse, 1), ((0, 0), (0, LANES - 3)))
    told = jnp.concatenate([every, extra], 1)
    told_x, told_y = hop(told, dq=1), hop(told, dq=2)
    grad_final = exact(spread, drows)
    dx2, dfsh, dfsc, dgain_f = modulate_back(grad_final, nf, rf, gain_f[2], fsc)
    dg2 = jnp.sum(dx2 * mlp, 0)
    dmlp = (dx2 * g2).astype(bf16)
    g_down = chip_product(act_b, act_far, dmlp)
    dupper = gelu_back(dense_nt(dmlp, down_w))[0].astype(bf16)
    g_up = chip_product(h2b, h2_far, dupper)
    dh2 = dense_nt(dupper, up_w)
    dn2x, dsh2, dsc2, dgain_2 = modulate_back(dh2, n2, r2, gain_f[1], sc2)
    dx1 = dx2 + dn2x
    dg1 = jnp.sum(dx1 * attn, 0)
    dattn = (dx1 * g1).astype(bf16)
    dattn, g_down, g_up, told_x, told_y = lax.optimization_barrier(
        (dattn, g_down, g_up, told_x, told_y)
    )
    down_1 = split_blocks(plane_blocks(g_down), 1, 1)
    up_1 = split_blocks(plane_blocks(g_up), 0, 2)
    g_out = chip_product(mixed_b, mixed_far, dattn)
    dmixed = dense_nt(dattn, out_w).astype(bf16)
    dquery, dkey, dkey_far, dvalue, dvalue_far = attend_back(
        length, core, *attended, lse_att, dmixed, *turns
    )
    told_xy = hop(told_x, dq=2)
    dquery, dkey, dkey_far, dvalue, dvalue_far, down_1, up_1, g_out = lax.optimization_barrier(
        (dquery, dkey, dkey_far, dvalue, dvalue_far, down_1, up_1, g_out)
    )
    down_2 = split_blocks(down_1[0] + down_1[1].astype(f32), 0, 1)
    up_2 = split_blocks(up_1[0] + up_1[1].astype(f32), 1, 1)
    dkey = (dkey + hop(dkey_far, dr=1).astype(f32)).astype(bf16)
    dvalue = (dvalue + hop(dvalue_far, dr=1).astype(f32)).astype(bf16)
    dqkv = jnp.concatenate([dquery, dkey, dvalue], 1)
    dh1 = dense_nt(dqkv, qkv_w)
    dn1x, dsh1, dsc1, dgain_1 = modulate_back(dh1, n1, r1, gain_f[0], sc1)
    dx0 = dx1 + dn1x


    dx0_b = dx0.astype(bf16).reshape(1, half * groups, LANES)
    dqkv_far = hop(pick_half(dqkv, 1 - rep_idx), dr=1)
    told = jnp.stack([told, told_x, told_y, told_xy])
    told = jnp.concatenate([told, hop(told, dr=1)], 0).reshape(-1, width + LANES)
    row_sums = [dsh1, dsc1, dg1, dsh2, dsc2, dg2, dfsh, dfsc, dgain_1, dgain_2, dgain_f]
    dx0_b, down_2, up_2, dqkv_far, told, row_sums = lax.optimization_barrier(
        (dx0_b, down_2, up_2, dqkv_far, told, row_sums)
    )
    sums_here = jnp.concatenate(row_sums)
    g_qkv = chip_product(h1b, h1_far, dqkv, dqkv_far)
    others = lines - 1
    cut = -(-2 * others // 3)
    on_line = jnp.concatenate([hop(dx0_b, dl=-d) for d in range(1, lines)], 0)
    own_x, own_y = hop(dx0_b, dq=1), hop(dx0_b, dq=2)
    g_last = jnp.concatenate([g_qkv, g_out], 1)
    own_x, own_y, g_last = lax.optimization_barrier((own_x, own_y, g_last))
    own_xy = hop(own_y, dq=1)
    last_1 = split_blocks(plane_blocks(g_last), 1, 1)
    sums_all = lax.all_gather(sums_here.reshape(1, -1, LANES), BOTH, axis=0, tiled=True)
    last_2 = split_blocks(last_1[0] + last_1[1].astype(f32), 0, 1)
    on_line, own_x, own_y, own_xy, last_2, dx0_b = lax.optimization_barrier(
        (on_line, own_x, own_y, own_xy, last_2, dx0_b)
    )
    rows_all = told[:, :width]
    lse_all = jnp.sum(told[:, width : width + 3].astype(f32), 1)
    line_x, line_y = hop(on_line, dq=1), hop(on_line, dq=2)
    shards = [two[0] + two[1].astype(f32) for two in (down_2, up_2, last_2)]
    both = shards[1].shape[1]
    tall = shards[0].shape[1] // both
    pile = shards[0].reshape(lines, tall, both, -1)
    blocks = jnp.concatenate([pile[:, k] for k in range(tall)] + shards[1:], 2)
    sums = reduce_step(blocks, None, lines - 1)
    early = [(dx0_b, 0, 0), (own_x, 1, 0), (own_y, 2, 0), (own_xy, 3, 0), (on_line, 0, 1)]
    order = []

    def from_cores(gathered):
        sources = []
        for value, dq, first_d in gathered:
            sources.extend(add_source(value, dq, first_d))
        return sources

    def add_source(value, dq, first_d):
        for dr in range(reps):
            for d in range(first_d, first_d + value.shape[0]):
                order.append(
                    (((line + d) % lines) * PLANE + (chip ^ dq)) * reps + (rep_idx ^ dr)
                )
        return [value, hop(value, dr=1)]

    def lists_of(order):
        order = jnp.stack(order)
        entries = jnp.take(asked, order, axis=0)
        count = jnp.sum((entries > 0).astype(jnp.int32), 1)
        entries = jnp.maximum(entries - 1, 0)
        return (
            count,
            entries // half,
            (entries % half) * groups,
            jnp.take(asked_mix, order, axis=0),
        )

    sources = from_cores(early)
    begun = spread_rows(lists_of(order), sources, vocab, width)
    order.clear()
    logits_mine = dense_nt(rows_all, table_low)
    own_column = jnp.where(targets_all // vocab == me, targets_all % vocab, -1)
    hit_mine = jnp.arange(padded, dtype=jnp.int32)[None, :] == own_column[:, None]
    dlogit_mine = (
        (weight_rows / coefficient_aggregate)[:, None]
        * (jnp.exp(logits_mine - lse_all[:, None]) - hit_mine.astype(f32))
    ).astype(bf16)
    head_grad = dense_tn(dlogit_mine, rows_all)
    line_x, line_y, begun, head_grad, sums, sums_all = lax.optimization_barrier(
        (line_x, line_y, begun, head_grad, sums, sums_all)
    )
    for d in range(lines - 2, 1, -1):
        sums = reduce_step(blocks, sums, d)
    near = hop(line_x[:cut], dq=2)
    rest = [hop(line_y[cut:], dq=1)] if cut < others else []
    sources = from_cores([(line_x, 1, 1), (line_y, 2, 1)])
    begun = spread_rows(lists_of(order), sources, vocab, width, begun)
    order.clear()
    near, rest, begun, sums = lax.optimization_barrier((near, rest, begun, sums))
    sources = from_cores([(near, 3, 1)] + [(value, 3, 1 + cut) for value in rest])
    sources, sums = lax.optimization_barrier((sources, sums))
    sums = reduce_step(blocks, sums, 1)
    table_grad, table_squares = spread_rows(
        lists_of(order), sources, vocab, width, begun, head_grad
    )
    sums, table_grad, table_squares = lax.optimization_barrier((sums, table_grad, table_squares))
    total = block_at(blocks, 0) + sums[0] + sums[1]
    down_end = tall * pile.shape[3]
    pile = jnp.stack(jnp.split(total[:, :down_end], tall, 1))
    d_down = jnp.concatenate(join_cores(pile.reshape(reps, -1, pile.shape[2])), 1)
    left, right = join_cores(total[:, down_end:].reshape(reps, both // reps, -1))
    joined = []
    at = 0
    for columns in (up_proj.shape[1], attn_proj.shape[1], out_proj.shape[1]):
        part = slice(at, at + columns // 2)
        joined.append(jnp.concatenate([left[:, part], right[:, part]], 1))
        at += columns // 2
    d_up, d_qkv, d_out = joined

    sums_all = sums_all.reshape(n_dp, reps, -1).sum(1)
    dmods = sums_all[:, : 6 * width]
    dfmods = sums_all[:, 6 * width : 8 * width]

    def my_columns(value, count):
        return lax.dynamic_slice_in_dim(value, me * count, count, axis=1)

    d_mod = exact_tn(my_columns(cond, mod_proj.shape[0]), dmods)
    d_final = exact_tn(my_columns(cond, final_proj.shape[0]), dfmods)
    dcond = exact_nt(dmods, mod_f) + exact_nt(dfmods, final_f)
    d_time = exact_tn(my_columns(feats, time_proj.shape[0]), silu_back(dcond)[0])
    d_gains = my_columns(
        jnp.sum(sums_all[:, 8 * width :], 0).reshape(3, width), norm_gains.shape[1]
    )

    reduced = (d_qkv, d_out, d_up, d_down, d_time, d_mod, d_final, d_gains)
    local_sq = jnp.sum(table_squares)
    for g in reduced:
        local_sq = local_sq + jnp.sum(g * g)
    totals = add_up(jnp.stack([local_sq, loss_here]))
    grad_norm = jnp.sqrt(totals[0])
    loss_sum = totals[1]
    clip = jnp.minimum(1.0, 0.01 / (grad_norm + 1e-06))
    masters = (attn_proj, out_proj, up_proj, down_proj, time_proj, mod_proj, final_proj, norm_gains)
    coefficients = (vocab_table,) + masters
    moms = (
        table_mom,
        proj_mom,
        outp_mom,
        up_mom,
        down_mom,
        time_mom,
        mod_mom,
        final_mom,
        gains_mom,
    )
    sqs = (table_sq, proj_sq, outp_sq, up_sq, down_sq, time_sq, mod_sq, final_sq, gains_sq)
    rates = (0.02, 0.02, 0.02, 0.02, 0.02, 0.02, 0.02, 0.02, 0.1)
    grads = (table_grad,) + reduced
    result = [loss_sum, coefficient_aggregate, grad_norm]
    quads = list(zip(coefficients, moms, sqs, grads))
    weight_now, first_m, second_m, grad = quads[0]
    result.extend(adamw(weight_now, first_m, second_m, clip * grad, rates[0]))
    result.extend(adamw_all(clip, quads[1:], rates[1:]))
    return tuple(result)


def solution(mesh):
    shard = P(BOTH, None)
    columns = P(None, BOTH)
    return jax.shard_map(
        local,
        mesh=mesh,
        in_specs=(P("dp", "rep", None),) * 3 + (P(),) * 4 + (shard,) * 24 + (columns,) * 3,
        out_specs=(P(),) * 3 + (shard,) * 24 + (columns,) * 3,
        check_vma=False,
    )
```

```python
import functools
import math

import jax
import jax.numpy as jnp
from jax import lax
from jax.experimental import pallas as pl
from jax.experimental.pallas import tpu as pltpu
from jax.sharding import PartitionSpec as P

HD = 64
TSTEPS = 1000
STEP = 5
PLANE = 4
LANES = 128
BOTH = ("dp", "rep")

HIGH = lax.Precision.HIGHEST
annealed_softness = 0.5
bf16 = jnp.bfloat16
f32 = jnp.float32


def dense(a, b):
    return jnp.dot(a, b, preferred_element_type=f32)


def dense_nt(a, b):
    return lax.dot_general(a, b, (((1,), (1,)), ((), ())), preferred_element_type=f32)


def dense_tn(a, b):
    return lax.dot_general(a, b, (((0,), (0,)), ((), ())), preferred_element_type=f32)


def exact(a, b):
    return jnp.dot(a, b, precision=HIGH, preferred_element_type=f32)


def exact_nt(a, b):
    return lax.dot_general(
        a, b, (((1,), (1,)), ((), ())), precision=HIGH, preferred_element_type=f32
    )


def exact_tn(a, b):
    return lax.dot_general(
        a, b, (((0,), (0,)), ((), ())), precision=HIGH, preferred_element_type=f32
    )


def normalize(x):
    center = x - jnp.mean(x, -1, keepdims=True)
    rstd = lax.rsqrt(jnp.mean(center * center, -1, keepdims=True) + 1e-06)
    return (center * rstd, rstd)


def modulate_back(grad_h, normed, rstd, gain, scale):
    dshift = jnp.sum(grad_h, 0)
    weighted = grad_h * normed
    column = jnp.sum(weighted, 0)
    dscale = column * gain
    dgain = column * (1.0 + scale[0])
    grad_n = grad_h * gain * (1.0 + scale)
    grad_x = rstd * (
        grad_n
        - jnp.mean(grad_n, -1, keepdims=True)
        - normed * jnp.mean(grad_n * normed, -1, keepdims=True)
    )
    return (grad_x, dshift, dscale, dgain)


def rope_tables(pos, head):
    half = head // 2
    freqs = jnp.exp(-math.log(10000.0) * jnp.arange(half, dtype=f32) / half)
    angle = pos.astype(f32)[:, None] * freqs[None, :]
    return (jnp.cos(angle), jnp.sin(angle))


def time_features(steps, width):
    tau = (steps.astype(f32) + 1.0) / TSTEPS
    half = width // 2
    freqs = jnp.exp(-math.log(10000.0) * jnp.arange(half, dtype=f32) / half)
    angle = 1000.0 * tau[:, None] * freqs[None, :]
    return jnp.concatenate([jnp.cos(angle), jnp.sin(angle)], -1)


def turn(x, cosv, sinv):
    lane = lax.broadcasted_iota(jnp.int32, x.shape, 1)
    quarter = HD // 2
    swapped = jnp.where(
        lane % HD < quarter,
        pltpu.roll(x, LANES - quarter, axis=1),
        pltpu.roll(x, quarter, axis=1),
    )
    return x * cosv + swapped * sinv


def turn_kernel(q_ref, k_ref, v_ref, cos_ref, sin_ref, q_out, k_out, v_out):
    cosv, sinv = cos_ref[...], sin_ref[...]
    for start in range(0, q_ref.shape[1], LANES):
        at = slice(start, start + LANES)
        q_out[:, at] = turn(q_ref[:, at], cosv, sinv).astype(bf16)
        k_out[:, at] = turn(k_ref[:, at], cosv, sinv).astype(bf16)
    v_out[...] = v_ref[...].astype(bf16)


def turn_rows(qkv, cosv, sinv):
    rows, width = qkv.shape[0], qkv.shape[1] // 3
    wide = 3 * LANES if width % (3 * LANES) == 0 else LANES
    blocks = width // wide
    block = lambda shift: pl.BlockSpec((rows, wide), lambda i: (0, i + shift))
    whole = pl.BlockSpec((rows, LANES), lambda i: (0, 0))
    return pl.pallas_call(
        turn_kernel,
        grid=(blocks,),
        in_specs=[block(0), block(blocks), block(2 * blocks), whole, whole],
        out_specs=[block(0)] * 3,
        out_shape=[jax.ShapeDtypeStruct((rows, width), bf16)] * 3,
        cost_estimate=pl.CostEstimate(
            flops=rows * width * 12, bytes_accessed=rows * width * 18, transcendentals=0
        ),
    )(qkv, qkv, qkv, cosv, sinv)


def key_masks(len_ref, core_ref, keys):
    place = lax.broadcasted_iota(jnp.int32, (1, keys), 1)
    own = place + core_ref[0] * keys
    far = place + (1 - core_ref[0]) * keys
    return [jnp.where(at < len_ref[0], 0.0, -1e30).astype(f32) for at in (own, far)]


def attend_kernel(len_ref, core_ref, q_ref, k_ref, kf_ref, v_ref, vf_ref, *refs, tile):
    out_ref, lse_ref = refs[-2:]
    rows = q_ref.shape[0]
    masks = key_masks(len_ref, core_ref, rows)
    keyed = (k_ref[...], kf_ref[...])
    valued = (v_ref[...], vf_ref[...])
    lane = lax.broadcasted_iota(jnp.int32, (tile, LANES), 1)
    for t in range(rows // tile):
        at = pl.ds(t * tile, tile)
        query = q_ref[at, :] * bf16(HD**-0.5)
        mixed, lses = [], []
        for head in range(LANES // HD):
            mine = jnp.where(lane // HD == head, query, bf16(0))
            scores = [dense_nt(mine, k) + mask for k, mask in zip(keyed, masks)]
            top = jnp.maximum(*[jnp.max(s, 1, keepdims=True) for s in scores])
            expo = [jnp.exp(s - top) for s in scores]
            total = sum(jnp.sum(e, 1, keepdims=True) for e in expo)
            inverse = 1.0 / total
            mixed.append(sum(dense((e * inverse).astype(bf16), v) for e, v in zip(expo, valued)))
            lses.append(top + jnp.log(total))
        out_ref[at, :] = jnp.where(lane < HD, mixed[0], mixed[1]).astype(bf16)
        lse_ref[at, :] = jnp.where(lane < HD, lses[0], lses[1])


def attend(length, core, query, keyed, keyed_far, valued, valued_far, ready=()):
    rows, width = query.shape
    smem = pl.BlockSpec(memory_space=pltpu.SMEM)
    block = pl.BlockSpec((rows, LANES), lambda i: (0, i))
    return pl.pallas_call(
        functools.partial(attend_kernel, tile=256),
        grid=(width // LANES,),
        in_specs=[smem, smem] + [block] * 5 + [pl.BlockSpec(memory_space=pl.ANY)] * len(ready),
        out_specs=[block, block],
        out_shape=[
            jax.ShapeDtypeStruct((rows, width), bf16),
            jax.ShapeDtypeStruct((rows, width), f32),
        ],
        compiler_params=pltpu.CompilerParams(vmem_limit_bytes=48 * 2**20),
        cost_estimate=pl.CostEstimate(
            flops=8 * rows * rows * width, bytes_accessed=rows * width * 18,
            transcendentals=2 * rows * rows * width // HD,
        ),
    )(length, core, query, keyed, keyed_far, valued, valued_far, *ready)


def attend_back_kernel(
    len_ref,
    core_ref,
    q_ref,
    k_ref,
    kf_ref,
    v_ref,
    vf_ref,
    lse_ref,
    do_ref,
    cos_ref,
    sin_ref,
    cos_far_ref,
    sin_far_ref,
    *refs,
    tile,
):
    dq_ref, dk_ref, dkf_ref, dv_ref, dvf_ref = refs[-5:]
    rows = q_ref.shape[0]
    masks = key_masks(len_ref, core_ref, rows)
    keyed = (k_ref[...], kf_ref[...])
    valued = (v_ref[...], vf_ref[...])
    lane = lax.broadcasted_iota(jnp.int32, (tile, LANES), 1)
    first = lax.broadcasted_iota(jnp.int32, (rows, LANES), 1) < HD
    dk, dv = [None, None], [None, None]
    for t in range(rows // tile):
        at = pl.ds(t * tile, tile)
        query = q_ref[at, :] * bf16(HD**-0.5)
        grad = do_ref[at, :]
        dqs, dks, dvs = [], [[], []], [[], []]
        for head in range(LANES // HD):
            mine = lane // HD == head
            q_mine = jnp.where(mine, query, bf16(0))
            g_mine = jnp.where(mine, grad, bf16(0))
            lse = lse_ref[at, head * HD : head * HD + 1]
            probs = [jnp.exp(dense_nt(q_mine, k) + mask - lse) for k, mask in zip(keyed, masks)]
            grad_p = [dense_nt(g_mine, v) for v in valued]
            delta = sum(jnp.sum(p * g, 1, keepdims=True) for p, g in zip(probs, grad_p))
            grad_s = [(p * (g - delta)).astype(bf16) for p, g in zip(probs, grad_p)]
            dqs.append(sum(dense(s, k) for s, k in zip(grad_s, keyed)))
            for side in range(2):
                dks[side].append(dense_tn(grad_s[side], query))
                dvs[side].append(dense_tn(probs[side].astype(bf16), grad))
        turned = turn(jnp.where(lane < HD, dqs[0], dqs[1]), cos_ref[at, :], -sin_ref[at, :])
        dq_ref[at, :] = (turned * HD**-0.5).astype(bf16)
        for side in range(2):
            part_k = jnp.where(first, *dks[side])
            part_v = jnp.where(first, *dvs[side])
            dk[side] = part_k if t == 0 else dk[side] + part_k
            dv[side] = part_v if t == 0 else dv[side] + part_v
    dk_ref[...] = turn(dk[0], cos_ref[...], -sin_ref[...])
    dkf_ref[...] = turn(dk[1], cos_far_ref[...], -sin_far_ref[...]).astype(bf16)
    dv_ref[...] = dv[0]
    dvf_ref[...] = dv[1].astype(bf16)


def attend_back(length, core, *arrays, ready=()):
    query = arrays[0]
    rows, width = query.shape
    smem = pl.BlockSpec(memory_space=pltpu.SMEM)
    block = pl.BlockSpec((rows, LANES), lambda i: (0, i))
    return pl.pallas_call(
        functools.partial(attend_back_kernel, tile=256),
        grid=(width // LANES,),
        in_specs=[smem, smem]
        + [block] * 7
        + [pl.BlockSpec((rows, LANES), lambda i: (0, 0))] * 4
        + [pl.BlockSpec(memory_space=pl.ANY)] * len(ready),
        out_specs=[block] * 5,
        out_shape=[jax.ShapeDtypeStruct((rows, width), t) for t in (bf16, f32, bf16, f32, bf16)],
        compiler_params=pltpu.CompilerParams(vmem_limit_bytes=48 * 2**20),
        cost_estimate=pl.CostEstimate(
            flops=20 * rows * rows * width, bytes_accessed=rows * width * 32,
            transcendentals=2 * rows * rows * width // HD,
        ),
    )(length, core, *arrays, *ready)
def adamw(weight, first, second, grad, rate):
    first = 0.9 * first + 0.1 * grad
    second = 0.999 * second + 0.001 * grad * grad
    step = first / (1.0 - 0.9**STEP) / (jnp.sqrt(second / (1.0 - 0.999**STEP)) + 1e-08)
    return (weight - rate * (step + 0.01 * weight), first, second)


def adamw_kernel(clip_ref, *refs, rates):
    n = len(rates)
    for k, rate in enumerate(rates):
        weight, first, second, grad = [ref[...] for ref in refs[4 * k : 4 * k + 4]]
        outs = refs[4 * n + 3 * k : 4 * n + 3 * k + 3]
        for out, value in zip(outs, adamw(weight, first, second, clip_ref[0] * grad, rate)):
            out[...] = value


def adamw_all(clip, quads, rates):
    vmem = pl.BlockSpec(memory_space=pltpu.VMEM)
    flat = [value for quad in quads for value in quad]
    shapes = [jax.ShapeDtypeStruct(quad[0].shape, f32) for quad in quads for _ in range(3)]
    return pl.pallas_call(
        functools.partial(adamw_kernel, rates=rates),
        in_specs=[pl.BlockSpec(memory_space=pltpu.SMEM)] + [vmem] * len(flat),
        out_specs=[vmem] * len(shapes),
        out_shape=shapes,
        compiler_params=pltpu.CompilerParams(vmem_limit_bytes=48 * 2**20),
    )(clip.reshape(1), *flat)


def hop(x, dl=0, dq=0, dr=0):
    reps = lax.axis_size("rep")
    lines = lax.axis_size("dp") // PLANE
    pairs = []
    for l in range(lines):
        for q in range(PLANE):
            for r in range(reps):
                to = (((l + dl) % lines) * PLANE + (q ^ dq)) * reps + (r ^ dr)
                pairs.append(((l * PLANE + q) * reps + r, to))
    return lax.ppermute(x, BOTH, pairs)


def step_line(x, way, reach):
    lines = lax.axis_size("dp") // PLANE
    pairs = []
    for l in range(lines):
        if 0 <= l + way * reach < lines:
            for q in range(PLANE):
                pairs.append((l * PLANE + q, (l + way) * PLANE + q))
    return lax.ppermute(x, "dp", pairs)


def pick_half(value, index):
    size = value.shape[1] // 2
    return lax.dynamic_slice_in_dim(value, index * size, size, axis=1)


def chip_product(left, left_far, right, far=None):
    rep_idx = lax.axis_index("rep")
    if far is None:
        far = hop(pick_half(right, 1 - rep_idx), dr=1)
    return dense_tn(left, pick_half(right, rep_idx)) + dense_tn(left_far, far)


def plane_blocks(value):
    lines = lax.axis_size("dp") // PLANE
    return value.reshape(lines, 2, 2, value.shape[0] // (lines * PLANE), -1)


def split_blocks(blocks, axis, place):
    bit = (lax.axis_index("dp") >> axis) & 1
    far = lax.dynamic_index_in_dim(blocks, 1 - bit, place, False).astype(bf16)
    return lax.dynamic_index_in_dim(blocks, bit, place, False), hop(far, dq=1 << axis)


def block_at(blocks, shift):
    line = lax.axis_index("dp") // PLANE
    return lax.dynamic_index_in_dim(blocks, jnp.mod(line + shift, blocks.shape[0]), 0, False)


def reduce_step(blocks, sums, reach):
    to_right, to_left = block_at(blocks, reach), block_at(blocks, -reach)
    if sums is not None:
        to_right, to_left = to_right + sums[0], to_left + sums[1]
    return step_line(to_right, 1, reach), step_line(to_left, -1, reach)


def join_cores(parts):
    rep_idx = lax.axis_index("rep")
    mine = lax.dynamic_index_in_dim(parts, rep_idx, 0, False)
    far = hop(lax.dynamic_index_in_dim(parts, 1 - rep_idx, 0, False), dr=1)
    return jnp.where(rep_idx == 0, mine, far), jnp.where(rep_idx == 0, far, mine)


def add_up(value):
    lines = lax.axis_size("dp") // PLANE
    line = lax.axis_index("dp") // PLANE
    value = value + hop(value, dr=1)
    far = [hop(value, dq=dq) for dq in range(1, PLANE)]
    value = (value + far[0]) + (far[1] + far[2])
    every = jnp.stack([value] + [hop(value, dl=-d) for d in range(1, lines)])
    every = lax.dynamic_slice_in_dim(
        jnp.concatenate([every, every], 0), (lines - line) % lines, lines
    )
    return jnp.sum(every, 0)


def mix_kernel(idx_ref, mix_ref, *refs, groups, cands, counts, keep):
    n = len(counts)
    pieces, refs = refs[:n], refs[n:]
    if keep:
        out_ref, whole_ref, tab, stage, sem, keep_sem = refs
    else:
        out_ref, tab, stage, sem = refs
    slots = stage.shape[0]
    bases = [sum(counts[:j]) for j in range(n)]

    @pl.when(pl.program_id(0) == 0)
    def _():
        def slot(j):
            return stage.at[j % slots, pl.ds(0, counts[j])]

        def copy(j):
            return pltpu.make_async_copy(pieces[j], slot(j), sem.at[j % slots])

        def store(j):
            whole = whole_ref.at[pl.ds(bases[j], counts[j])]
            return pltpu.make_async_copy(slot(j), whole, keep_sem.at[j % slots])

        for j in range(min(2, n)):
            copy(j).start()
        for j in range(n):
            copy(j).wait()
            if keep:
                store(j).start()

            @pl.loop(0, counts[j] // 16)
            def _(t, j=j):
                part = stage[j % slots, pl.ds(pl.multiple_of(t * 16, 16), 16), :].astype(f32)
                for g in range(groups):
                    tab[pl.ds((bases[j] + t * 16) * groups + g, 16, stride=groups), :] = part[
                        :, g * LANES : (g + 1) * LANES
                    ]

            if keep and j >= 2:
                store(j - 2).wait()
            if j + 2 < n:
                copy(j + 2).start()
        if keep:
            for j in range(max(0, n - 2), n):
                store(j).wait()

    unroll = 4

    @pl.loop(0, idx_ref.shape[-1] // cands // unroll)
    def _(block):
        for u in range(unroll):
            p = block * unroll + u
            total = None
            for c in range(cands):
                row = tab[pl.ds(idx_ref[0, 0, p * cands + c], 8), :]
                term = row * mix_ref[0, 0, p * cands + c]
                total = term if total is None else total + term
            out_ref[0, pl.ds(p * groups, 8), :] = total


def mix_rows(idx, mix, pieces, cands, keep):
    width = pieces[0].shape[1]
    groups = width // LANES
    lines, _, entries = idx.shape
    counts = tuple(piece.shape[0] for piece in pieces)
    rows = entries // cands * groups + 8
    out_specs = [pl.BlockSpec((1, rows, LANES), lambda i: (i, 0, 0))]
    out_shape = [jax.ShapeDtypeStruct((lines, rows, LANES), f32)]
    slots = 4
    scratch = [
        pltpu.VMEM((sum(counts) * groups + 8, LANES), f32),
        pltpu.VMEM((slots, max(counts), width), bf16),
        pltpu.SemaphoreType.DMA((slots,)),
    ]
    if keep:
        out_specs.append(pl.BlockSpec(memory_space=pl.ANY))
        out_shape.append(jax.ShapeDtypeStruct((sum(counts), width), bf16))
        scratch.append(pltpu.SemaphoreType.DMA((slots,)))
    return pl.pallas_call(
        functools.partial(mix_kernel, groups=groups, cands=cands, counts=counts, keep=keep),
        grid=(lines,),
        in_specs=[pl.BlockSpec((1, 1, entries), lambda i: (i, 0, 0), memory_space=pltpu.SMEM)] * 2
        + [pl.BlockSpec(memory_space=pl.ANY)] * len(pieces),
        out_specs=out_specs,
        out_shape=out_shape,
        scratch_shapes=scratch,
        compiler_params=pltpu.CompilerParams(vmem_limit_bytes=60 * 2**20),
        cost_estimate=pl.CostEstimate(
            flops=lines * entries * 2048, bytes_accessed=40 * 2**20, transcendentals=0
        ),
    )(idx, mix, *pieces)


def spread_kernel(cnt_ref, row_ref, pos_ref, mix_ref, *refs, groups, arrays, first, last):
    sources = refs[:arrays]
    refs = list(refs[arrays:])
    total_in = None if first else refs.pop(0)
    if last:
        head_ref, out_ref, sq_ref = refs[:3]
        refs = refs[3:]
    total, rows32, stage, sem, total_sem = refs
    length = sources[0].shape[1]
    blocks = [source.at[k] for source in sources for k in range(source.shape[0])]
    n = len(blocks)

    def copy(k):
        return pltpu.make_async_copy(blocks[k], stage.at[k % 2], sem.at[k % 2])

    copy(0).start()
    if not first:
        load = pltpu.make_async_copy(total_in, total, total_sem)
        load.start()
        load.wait()
    else:

        @pl.loop(0, total.shape[0] // 64)
        def _(t):
            total[pl.ds(pl.multiple_of(t * 64, 64), 64), :] = jnp.zeros((64, LANES), f32)

    unroll = 4
    for k in range(n):
        if k + 1 < n:
            copy(k + 1).start()
        copy(k).wait()

        @pl.loop(0, length // 64)
        def _(t, k=k):
            at = pl.multiple_of(t * 64, 64)
            rows32[pl.ds(at, 64), :] = stage[k % 2, pl.ds(at, 64), :].astype(f32)

        @pl.loop(0, (cnt_ref[k] + unroll - 1) // unroll)
        def _(block, k=k):
            for u in range(unroll):
                e = block * unroll + u
                at = pl.ds(pl.multiple_of(row_ref[k, e] * 8, 8), 8)
                term = mix_ref[k, e] * rows32[pl.ds(pos_ref[k, e], 8), :]
                total[at, :] = total[at, :] + term

    if not last:
        return
    vocab = out_ref.shape[0]

    def finish(at, size, start):
        squares = jnp.zeros((size, LANES), f32)
        for g in range(groups):
            columns = slice(g * LANES, (g + 1) * LANES)
            value = head_ref[pl.ds(at, size), columns] + total[pl.ds(start + g, size, stride=8), :]
            out_ref[pl.ds(at, size), columns] = value
            squares = squares + value * value
        return squares

    squares = lax.fori_loop(
        0,
        vocab // 8,
        lambda t, so_far: so_far + finish(pl.multiple_of(t * 8, 8), 8, t * 64),
        jnp.zeros((8, LANES), f32),
    )
    sq_ref[...] = squares
    if vocab % 8:
        at = vocab // 8 * 8
        sq_ref[0 : vocab % 8, :] += finish(at, vocab % 8, at * 8)


def spread_rows(lists, sources, vocab, width, total=None, head=None):
    groups = width // LANES
    length = sources[0].shape[1]
    total_rows = -(-vocab * 8 // 64) * 64
    first, last = total is None, head is not None
    smem = pl.BlockSpec(memory_space=pltpu.SMEM)
    vmem = pl.BlockSpec(memory_space=pltpu.VMEM)
    hbm = pl.BlockSpec(memory_space=pl.ANY)
    scratch = [
        pltpu.VMEM((length + 8, LANES), f32),
        pltpu.VMEM((2, length, LANES), bf16),
        pltpu.SemaphoreType.DMA((2,)),
    ]
    extra_specs, extra = ([], []) if first else ([hbm], [total])
    scratch.append(pltpu.SemaphoreType.DMA)
    if last:
        extra_specs, extra = extra_specs + [vmem], extra + [head]
        out_specs = [vmem, vmem]
        out_shape = [
            jax.ShapeDtypeStruct((vocab, width), f32),
            jax.ShapeDtypeStruct((8, LANES), f32),
        ]
        scratch = [pltpu.VMEM((total_rows, LANES), f32)] + scratch
    else:
        out_specs = vmem
        out_shape = jax.ShapeDtypeStruct((total_rows, LANES), f32)
    entries = sum(source.shape[0] for source in sources) * lists[1].shape[1] // 2
    return pl.pallas_call(
        functools.partial(
            spread_kernel,
            groups=groups,
            arrays=len(sources),
            first=first,
            last=last,
        ),
        in_specs=[smem] * 4 + [hbm] * len(sources) + extra_specs,
        out_specs=out_specs,
        out_shape=out_shape,
        scratch_shapes=scratch,
        compiler_params=pltpu.CompilerParams(vmem_limit_bytes=60 * 2**20),
        cost_estimate=pl.CostEstimate(
            flops=entries * 2048,
            bytes_accessed=entries * (65536 if first else 10240),
            transcendentals=0,
        ),
    )(*lists, *sources, *extra)


def local(
    noise_owner,
    noise_offset,
    option_scores,
    seq_lengths,
    time_index,
    loss_pick,
    loss_target,
    vocab_table,
    table_mom,
    table_sq,
    attn_proj,
    proj_mom,
    proj_sq,
    out_proj,
    outp_mom,
    outp_sq,
    up_proj,
    up_mom,
    up_sq,
    down_proj,
    down_mom,
    down_sq,
    time_proj,
    time_mom,
    time_sq,
    mod_proj,
    mod_mom,
    mod_sq,
    final_proj,
    final_mom,
    final_sq,
    norm_gains,
    gains_mom,
    gains_sq,
):
    devices = lax.axis_size(BOTH)
    reps = lax.axis_size("rep")
    n_dp = lax.axis_size("dp")
    lines = n_dp // PLANE
    dp_idx = lax.axis_index("dp")
    rep_idx = lax.axis_index("rep")
    me = dp_idx * reps + rep_idx
    line = dp_idx // PLANE
    chip = dp_idx % PLANE
    _, half, cands = noise_offset.shape
    vocab, width = vocab_table.shape
    heads = width // HD
    groups = width // LANES
    swaps = [(dq, dr) for dq in range(PLANE) for dr in range(reps)]

    def from_me(values):
        return lax.dynamic_slice_in_dim(jnp.concatenate([values, values], 0), line, lines)

    def gather(value, axis=0):
        return lax.all_gather(value.astype(bf16), BOTH, axis=axis, tiled=True)

    few = mod_proj.shape[0]
    gains_flat = norm_gains.reshape(-1)
    gains_flat = jnp.pad(gains_flat, (0, few * LANES - gains_flat.size))
    small_all = lax.all_gather(
        jnp.concatenate(
            [mod_proj, final_proj, time_proj.reshape(few, -1), gains_flat.reshape(few, LANES)], 1
        ).astype(bf16),
        BOTH,
    )
    qkv_w = gather(attn_proj)

    padded = -(-vocab // 16) * 16
    table_low = jnp.pad(vocab_table.astype(bf16), ((0, padded - vocab), (0, 0)))
    cut = padded // 32 * 16
    upper_rows, lower_rows = table_low[:cut], table_low[cut:]
    first, second = {0: upper_rows}, {0: lower_rows}
    for dq in (1, 2):
        first[dq] = hop(upper_rows, dq=dq)
        second[dq] = hop(lower_rows, dq=dq)

    owner = noise_owner.reshape(-1)
    offset = noise_offset.reshape(-1)
    mixing = jax.nn.softmax(option_scores.reshape(half, cands) / annealed_softness, axis=-1)
    names = (owner * padded + offset).astype(f32).reshape(-1, LANES)
    packed = jnp.concatenate([names, mixing.reshape(-1, LANES)], 0)
    groups_of_line = [[l * PLANE + q for l in range(lines)] for q in range(PLANE)]
    on_line = lax.all_gather(packed, "dp", axis_index_groups=groups_of_line)
    cap = max(2, 2 * half * cands // devices)
    member = (owner[:, None] == jnp.arange(devices, dtype=jnp.int32)[None, :]).astype(jnp.int32)
    slot = jnp.sum((jnp.cumsum(member, 0) - member) * member, 1)
    flat_slot = owner * cap + slot
    late_shards = (
        jnp.concatenate([out_proj, up_proj], 1).astype(bf16),
        down_proj.astype(bf16),
    )
    first, second, flat_slot, late_shards = lax.optimization_barrier(
        (first, second, flat_slot, late_shards)
    )
    first[3] = hop(first[1], dq=2)
    second[3] = hop(second[2], dq=1)
    pieces = []
    for dq in range(PLANE):
        pieces += [first[dq], second[dq]]
        pieces += [hop(first[dq], dr=1), hop(second[dq], dr=1)]
    on_line = from_me(on_line)
    line_owner = on_line[:, : names.shape[0]].astype(jnp.int32)
    line_mix = on_line[:, names.shape[0] :]
    row_owner = line_owner // padded
    slot_of = (((row_owner // reps) % PLANE) ^ chip) * reps + ((row_owner % reps) ^ rep_idx)
    here = (row_owner // (reps * PLANE)) == line
    row_at = jnp.where(here, slot_of * padded + line_owner % padded, 0) * groups
    mix_here = jnp.where(here, line_mix, 0.0)
    row_at = row_at.reshape(lines, 1, half * cands)
    mix_here = mix_here.reshape(lines, 1, half * cands)
    parts = {}

    outer = (1, lines - 1)
    inner = tuple(range(2, lines - 1)) + (0,)
    stacked = [
        (jnp.stack([row_at[d] for d in which]), jnp.stack([mix_here[d] for d in which]))
        for which in (outer, inner)
    ]

    places = jnp.arange(half, dtype=jnp.int32)
    turns = []
    for core in (rep_idx, 1 - rep_idx):
        cosv, sinv = rope_tables(core * half + places, HD)
        turns += [jnp.tile(cosv, (1, 4)), jnp.concatenate([-sinv, sinv] * 2, 1)]
    length = lax.dynamic_slice_in_dim(seq_lengths, dp_idx, 1)
    picks = loss_pick.shape[-1]
    tau = (time_index.astype(f32) + 1.0) / TSTEPS
    starts = (jnp.arange(reps, dtype=jnp.int32) * half)[None, :, None]
    weight_all = jnp.where(
        loss_pick + starts < seq_lengths[:, None, None], (1.0 / (0.1 + tau))[:, None, None], 0.0
    )
    coefficient_aggregate = jnp.sum(weight_all)

    def of_line(values, at_chip, at_core):
        mine = lax.dynamic_slice(
            values.reshape(lines, PLANE, reps, picks), (0, at_chip, at_core, 0), (lines, 1, 1, picks)
        )
        return from_me(mine.reshape(lines, picks))

    def from_start(values):
        return lax.dynamic_slice_in_dim(
            jnp.concatenate([values, values], 0), (lines - line) % lines, lines
        )

    targets = of_line(loss_target, chip, rep_idx).reshape(-1)
    weight = of_line(weight_all, chip, rep_idx).reshape(-1)
    my_pick = lax.dynamic_slice(loss_pick, (dp_idx, rep_idx, 0), (1, 1, picks)).reshape(picks)
    t_owner = targets // vocab
    t_slot = (((t_owner // reps) % PLANE) ^ chip) * reps + ((t_owner % reps) ^ rep_idx)
    t_column = jnp.where(
        t_owner // (reps * PLANE) == line, t_slot * padded + targets % vocab, -1
    )
    among = [(chip ^ dq, rep_idx ^ dr) for dr in range(reps) for dq in range(PLANE)]
    targets_all = jnp.concatenate([of_line(loss_target, q, r).reshape(-1) for q, r in among])
    weight_rows = jnp.concatenate([of_line(weight_all, q, r).reshape(-1) for q, r in among])
    line_facts = (turns, length, weight_all, targets, weight, my_pick, t_column)
    line_facts, targets_all, weight_rows, stacked = lax.optimization_barrier(
        (line_facts, targets_all, weight_rows, stacked)
    )
    turns, length, weight_all, targets, weight, my_pick, t_column = line_facts

    def mix_some(call, keep):
        out = mix_rows(*stacked[call], pieces, cands, keep)
        for k, d in enumerate((outer, inner)[call]):
            parts[d] = out[0][k, : half * groups]
        return out[-1]

    mix_some(0, False)
    parts[1], parts[lines - 1], late_shards = lax.optimization_barrier(
        (parts[1], parts[lines - 1], late_shards)
    )
    out_up = gather(late_shards[0])
    down_w = gather(late_shards[1])
    out_w, up_w = out_up[:, :width], out_up[:, width:]
    far_parts = [hop(parts[d].astype(bf16), dl=d) for d in outer]
    plane_table = mix_some(1, True)
    far_parts += [hop(parts[d].astype(bf16), dl=d) for d in inner[:-1]]
    far_parts[:2], flat_slot, small_all = lax.optimization_barrier(
        (far_parts[:2], flat_slot, small_all)
    )
    small_all = small_all.reshape(devices * few, -1)
    entry = offset * half + jnp.arange(half * cands, dtype=jnp.int32) // cands + 1
    empty = jnp.zeros((devices * cap,), f32)
    lists = [
        empty.at[flat_slot].set(value).reshape(devices, cap)
        for value in (entry.astype(f32), mixing.reshape(-1))
    ]
    asked = jnp.concatenate(lists, 1)
    mod_f = small_all[:, : 6 * width].astype(f32)
    final_f = small_all[:, 6 * width : 8 * width].astype(f32)
    time_f = small_all[:, 8 * width : -LANES].astype(f32).reshape(-1, time_proj.shape[1])
    gain_f = small_all[:, -LANES:].astype(f32).reshape(devices, -1)[:, : norm_gains.size]
    gain_f = gain_f.reshape((devices,) + norm_gains.shape)
    gain_f = gain_f.transpose(1, 0, 2).reshape(norm_gains.shape[0], width)

    feats = time_features(time_index, time_f.shape[0])
    cond, silu_back = jax.vjp(jax.nn.silu, exact(feats, time_f))
    my_cond = lax.dynamic_slice_in_dim(cond, dp_idx, 1)
    mods = exact(my_cond, mod_f)
    fmods = exact(my_cond, final_f)
    far_parts, asked, mods, fmods, gain_f = lax.optimization_barrier(
        (far_parts, asked, mods, fmods, gain_f)
    )
    sh1, sc1, g1, sh2, sc2, g2 = jnp.split(mods, 6, -1)
    fsh, fsc = jnp.split(fmods, 2, -1)
    x0 = (parts[0] + sum(far.astype(f32) for far in far_parts)).reshape(half, width)

    n1, r1 = normalize(x0)
    h1b = (n1 * gain_f[0] * (1.0 + sc1) + sh1).astype(bf16)
    qkv = dense(h1b, qkv_w)
    query, keyed, valued = turn_rows(qkv, turns[0], turns[1])
    attended = (query, keyed, hop(keyed, dr=1), valued, hop(valued, dr=1))
    core = rep_idx.reshape(1)
    mixed_b, lse_att = attend(length, core, *attended)
    mixed_b, h1_far = lax.optimization_barrier((mixed_b, hop(h1b, dr=1)))
    attn = dense(mixed_b, out_w)
    x1 = x0 + g1 * attn
    n2, r2 = normalize(x1)
    h2b = (n2 * gain_f[1] * (1.0 + sc2) + sh2).astype(bf16)
    upper = dense(h2b, up_w)
    act, gelu_back = jax.vjp(lambda u: jax.nn.gelu(u, approximate=True), upper)
    act_b = act.astype(bf16)
    act_b, mixed_far, h2_far = lax.optimization_barrier(
        (act_b, hop(mixed_b, dr=1), hop(h2b, dr=1))
    )
    mlp = dense(act_b, down_w)
    x2 = x1 + g2 * mlp
    nf, rf = normalize(x2)
    final = nf * gain_f[2] * (1.0 + fsc) + fsh

    spread = (jnp.arange(half, dtype=jnp.int32)[:, None] == my_pick[None, :]).astype(f32)
    rows_b = jnp.take(final, my_pick, axis=0).astype(bf16)
    every = jnp.concatenate([rows_b] + [hop(rows_b, dl=-d) for d in range(1, lines)], 0)
    asked = lax.all_to_all(asked, BOTH, split_axis=0, concat_axis=0, tiled=True)
    every, act_far, asked = lax.optimization_barrier((every, hop(act_b, dr=1), asked))
    asked, asked_mix = asked[:, :cap].astype(jnp.int32), asked[:, cap:]
    logits = dense_nt(every, plane_table)
    column = jnp.arange(plane_table.shape[0], dtype=jnp.int32)
    exists = (column % padded) < vocab
    hit = column[None, :] == t_column[:, None]
    logits = jnp.where(exists[None, :], logits, -1e30)
    top = jnp.max(logits, -1)
    sums = jnp.sum(jnp.exp(logits - top[:, None]), -1)
    tgt = jnp.sum(jnp.where(hit, logits, 0.0), -1)
    stats = from_start(
        jnp.stack([value.reshape(lines, picks) for value in (top, sums, tgt)], 1)
    )
    stats_all = jnp.stack([stats] + [hop(stats, dl=-d) for d in range(1, lines)])
    tops = stats_all[:, :, 0]
    best = jnp.max(tops, 0)
    sum_all = jnp.sum(stats_all[:, :, 1] * jnp.exp(tops - best), 0)
    lse_line = best + jnp.log(sum_all)
    tgt_line = jnp.sum(stats_all[:, :, 2], 0)
    loss_here = jnp.sum(from_start(weight.reshape(lines, picks)) * (lse_line - tgt_line))
    loss_here = jnp.where(line == 0, loss_here, 0.0)
    lse = from_me(lse_line).reshape(-1)
    probs = jnp.exp(logits - lse[:, None])
    dlogit = ((weight / coefficient_aggregate)[:, None] * (probs - hit.astype(f32))).astype(bf16)
    drows_part = dense(dlogit, plane_table).reshape(lines, picks, width)
    drows = drows_part[0]
    for d in range(1, lines):
        drows = drows + hop(drows_part[d], dl=d)
    every, lse, drows = lax.optimization_barrier((every, lse, drows))
    pieces_of_lse = []
    for _ in range(3):
        rounded = lax.reduce_precision(lse, 8, 7)
        pieces_of_lse.append(rounded.astype(bf16))
        lse = lse - rounded
    extra = jnp.pad(jnp.stack(pieces_of_lse, 1), ((0, 0), (0, LANES - 3)))
    told = jnp.concatenate([every, extra], 1)
    told_x, told_y = hop(told, dq=1), hop(told, dq=2)
    grad_final = exact(spread, drows)
    dx2, dfsh, dfsc, dgain_f = modulate_back(grad_final, nf, rf, gain_f[2], fsc)
    dg2 = jnp.sum(dx2 * mlp, 0)
    dmlp = (dx2 * g2).astype(bf16)
    g_down = chip_product(act_b, act_far, dmlp)
    dupper = gelu_back(dense_nt(dmlp, down_w))[0].astype(bf16)
    g_up = chip_product(h2b, h2_far, dupper)
    dh2 = dense_nt(dupper, up_w)
    dn2x, dsh2, dsc2, dgain_2 = modulate_back(dh2, n2, r2, gain_f[1], sc2)
    dx1 = dx2 + dn2x
    dg1 = jnp.sum(dx1 * attn, 0)
    dattn = (dx1 * g1).astype(bf16)
    dattn, g_down, g_up, told_x, told_y = lax.optimization_barrier(
        (dattn, g_down, g_up, told_x, told_y)
    )
    down_1 = split_blocks(plane_blocks(g_down), 1, 1)
    up_1 = split_blocks(plane_blocks(g_up), 0, 2)
    g_out = chip_product(mixed_b, mixed_far, dattn)
    dmixed = dense_nt(dattn, out_w).astype(bf16)
    dquery, dkey, dkey_far, dvalue, dvalue_far = attend_back(
        length, core, *attended, lse_att, dmixed, *turns
    )
    told_xy = hop(told_x, dq=2)
    dquery, dkey, dkey_far, dvalue, dvalue_far, down_1, up_1, g_out = lax.optimization_barrier(
        (dquery, dkey, dkey_far, dvalue, dvalue_far, down_1, up_1, g_out)
    )
    down_2 = split_blocks(down_1[0] + down_1[1].astype(f32), 0, 1)
    up_2 = split_blocks(up_1[0] + up_1[1].astype(f32), 1, 1)
    dkey = (dkey + hop(dkey_far, dr=1).astype(f32)).astype(bf16)
    dvalue = (dvalue + hop(dvalue_far, dr=1).astype(f32)).astype(bf16)
    dqkv = jnp.concatenate([dquery, dkey, dvalue], 1)
    dh1 = dense_nt(dqkv, qkv_w)
    dn1x, dsh1, dsc1, dgain_1 = modulate_back(dh1, n1, r1, gain_f[0], sc1)
    dx0 = dx1 + dn1x


    dx0_b = dx0.astype(bf16).reshape(1, half * groups, LANES)
    dqkv_far = hop(pick_half(dqkv, 1 - rep_idx), dr=1)
    told = jnp.stack([told, told_x, told_y, told_xy])
    told = jnp.concatenate([told, hop(told, dr=1)], 0).reshape(-1, width + LANES)
    row_sums = [dsh1, dsc1, dg1, dsh2, dsc2, dg2, dfsh, dfsc, dgain_1, dgain_2, dgain_f]
    dx0_b, down_2, up_2, dqkv_far, told, row_sums = lax.optimization_barrier(
        (dx0_b, down_2, up_2, dqkv_far, told, row_sums)
    )
    sums_here = jnp.concatenate(row_sums)
    g_qkv = chip_product(h1b, h1_far, dqkv, dqkv_far)
    others = lines - 1
    cut = -(-2 * others // 3)
    on_line = jnp.concatenate([hop(dx0_b, dl=-d) for d in range(1, lines)], 0)
    own_x, own_y = hop(dx0_b, dq=1), hop(dx0_b, dq=2)
    g_last = jnp.concatenate([g_qkv, g_out], 1)
    own_x, own_y, g_last, told = lax.optimization_barrier((own_x, own_y, g_last, told))
    own_xy = hop(own_y, dq=1)
    last_1 = split_blocks(plane_blocks(g_last), 1, 1)
    sums_all = lax.all_gather(sums_here.reshape(1, -1, LANES), BOTH, axis=0, tiled=True)
    last_2 = split_blocks(last_1[0] + last_1[1].astype(f32), 0, 1)
    rows_all = told[:, :width]
    lse_all = jnp.sum(told[:, width : width + 3].astype(f32), 1)
    logits_mine = dense_nt(rows_all, table_low)
    own_column = jnp.where(targets_all // vocab == me, targets_all % vocab, -1)
    hit_mine = jnp.arange(padded, dtype=jnp.int32)[None, :] == own_column[:, None]
    dlogit_mine = (
        (weight_rows / coefficient_aggregate)[:, None]
        * (jnp.exp(logits_mine - lse_all[:, None]) - hit_mine.astype(f32))
    ).astype(bf16)
    head_grad = dense_tn(dlogit_mine, rows_all)
    on_line, own_x, own_y, own_xy, last_2, dx0_b, head_grad = lax.optimization_barrier(
        (on_line, own_x, own_y, own_xy, last_2, dx0_b, head_grad)
    )
    line_x, line_y = hop(on_line, dq=1), hop(on_line, dq=2)
    shards = [two[0] + two[1].astype(f32) for two in (down_2, up_2, last_2)]
    both = shards[1].shape[1]
    tall = shards[0].shape[1] // both
    pile = shards[0].reshape(lines, tall, both, -1)
    blocks = jnp.concatenate([pile[:, k] for k in range(tall)] + shards[1:], 2)
    sums = reduce_step(blocks, None, lines - 1)
    early = [(dx0_b, 0, 0), (own_x, 1, 0), (own_y, 2, 0), (own_xy, 3, 0), (on_line, 0, 1)]
    order = []

    def from_cores(gathered):
        sources = []
        for value, dq, first_d in gathered:
            sources.extend(add_source(value, dq, first_d))
        return sources

    def add_source(value, dq, first_d):
        for dr in range(reps):
            for d in range(first_d, first_d + value.shape[0]):
                order.append(
                    (((line + d) % lines) * PLANE + (chip ^ dq)) * reps + (rep_idx ^ dr)
                )
        return [value, hop(value, dr=1)]

    def lists_of(order):
        order = jnp.stack(order)
        entries = jnp.take(asked, order, axis=0)
        count = jnp.sum((entries > 0).astype(jnp.int32), 1)
        entries = jnp.maximum(entries - 1, 0)
        return (
            count,
            entries // half,
            (entries % half) * groups,
            jnp.take(asked_mix, order, axis=0),
        )

    sources = from_cores(early)
    begun = spread_rows(lists_of(order), sources, vocab, width)
    order.clear()
    line_x, line_y, begun, sums, sums_all = lax.optimization_barrier(
        (line_x, line_y, begun, sums, sums_all)
    )
    for d in range(lines - 2, 1, -1):
        sums = reduce_step(blocks, sums, d)
    near = hop(line_x[:cut], dq=2)
    rest = [hop(line_y[cut:], dq=1)] if cut < others else []
    sources = from_cores([(line_x, 1, 1), (line_y, 2, 1)])
    begun = spread_rows(lists_of(order), sources, vocab, width, begun)
    order.clear()
    near, rest, begun, sums = lax.optimization_barrier((near, rest, begun, sums))
    sources = from_cores([(near, 3, 1)] + [(value, 3, 1 + cut) for value in rest])
    sources, sums = lax.optimization_barrier((sources, sums))
    sums = reduce_step(blocks, sums, 1)
    table_grad, table_squares = spread_rows(
        lists_of(order), sources, vocab, width, begun, head_grad
    )
    sums, table_grad, table_squares = lax.optimization_barrier((sums, table_grad, table_squares))
    total = block_at(blocks, 0) + sums[0] + sums[1]
    down_end = tall * pile.shape[3]
    pile = jnp.stack(jnp.split(total[:, :down_end], tall, 1))
    d_down = jnp.concatenate(join_cores(pile.reshape(reps, -1, pile.shape[2])), 1)
    left, right = join_cores(total[:, down_end:].reshape(reps, both // reps, -1))
    joined = []
    at = 0
    for columns in (up_proj.shape[1], attn_proj.shape[1], out_proj.shape[1]):
        part = slice(at, at + columns // 2)
        joined.append(jnp.concatenate([left[:, part], right[:, part]], 1))
        at += columns // 2
    d_up, d_qkv, d_out = joined

    sums_all = sums_all.reshape(n_dp, reps, -1).sum(1)
    dmods = sums_all[:, : 6 * width]
    dfmods = sums_all[:, 6 * width : 8 * width]

    def my_columns(value, count):
        return lax.dynamic_slice_in_dim(value, me * count, count, axis=1)

    d_mod = exact_tn(my_columns(cond, mod_proj.shape[0]), dmods)
    d_final = exact_tn(my_columns(cond, final_proj.shape[0]), dfmods)
    dcond = exact_nt(dmods, mod_f) + exact_nt(dfmods, final_f)
    d_time = exact_tn(my_columns(feats, time_proj.shape[0]), silu_back(dcond)[0])
    d_gains = my_columns(
        jnp.sum(sums_all[:, 8 * width :], 0).reshape(3, width), norm_gains.shape[1]
    )

    reduced = (d_qkv, d_out, d_up, d_down, d_time, d_mod, d_final, d_gains)
    local_sq = jnp.sum(table_squares)
    for g in reduced:
        local_sq = local_sq + jnp.sum(g * g)
    totals = add_up(jnp.stack([local_sq, loss_here]))
    grad_norm = jnp.sqrt(totals[0])
    loss_sum = totals[1]
    clip = jnp.minimum(1.0, 0.01 / (grad_norm + 1e-06))
    masters = (attn_proj, out_proj, up_proj, down_proj, time_proj, mod_proj, final_proj, norm_gains)
    coefficients = (vocab_table,) + masters
    moms = (
        table_mom,
        proj_mom,
        outp_mom,
        up_mom,
        down_mom,
        time_mom,
        mod_mom,
        final_mom,
        gains_mom,
    )
    sqs = (table_sq, proj_sq, outp_sq, up_sq, down_sq, time_sq, mod_sq, final_sq, gains_sq)
    rates = (0.02, 0.02, 0.02, 0.02, 0.02, 0.02, 0.02, 0.02, 0.1)
    grads = (table_grad,) + reduced
    result = [loss_sum, coefficient_aggregate, grad_norm]
    quads = list(zip(coefficients, moms, sqs, grads))
    weight_now, first_m, second_m, grad = quads[0]
    result.extend(adamw(weight_now, first_m, second_m, clip * grad, rates[0]))
    result.extend(adamw_all(clip, quads[1:], rates[1:]))
    return tuple(result)


def solution(mesh):
    shard = P(BOTH, None)
    columns = P(None, BOTH)
    return jax.shard_map(
        local,
        mesh=mesh,
        in_specs=(P("dp", "rep", None),) * 3 + (P(),) * 4 + (shard,) * 24 + (columns,) * 3,
        out_specs=(P(),) * 3 + (shard,) * 24 + (columns,) * 3,
        check_vma=False,
    )
```
